32 devices in a mesh: clip: 8 (over y, x, core), tp: 4 (over z).
Axes of the slice: x: 2, y: 2, z: 4, core: 2. Of those that a mesh axis runs over, the one named last changes fastest.
Arguments:
- patches: bfloat16 [16, 1188, 768], P('clip'), may hold values from -6 to 6
- keep_freq: int32 [16, 12], P('clip'), may hold values from 0 to 1, as said below
- keep_time: int32 [16, 99], P('clip'), may hold values from 0 to 1, as said below
- cotangent: bfloat16 [16, 704, 768], P('clip'), may hold values from -6 to 6
- w_qkv: float32 [768, 3, 768], P(None, None, 'tp'), may hold values from -0.21875 to 0.21875
- w_out: float32 [768, 768], P('tp'), may hold values from -1.5 to 1.5
- w_up: float32 [768, 3072], P(None, 'tp'), may hold values from -0.21875 to 0.21875
- w_down: float32 [3072, 768], P('tp'), may hold values from -0.109375 to 0.109375
- norms: float32 [4, 768], replicated, may hold values from -1 to 1.5
- m_qkv: float32 [768, 3, 768], P('clip', None, 'tp'), may hold values from -256 to 256
- v_qkv: float32 [768, 3, 768], P('clip', None, 'tp'), may hold values from 2008 to 8032
- m_out: float32 [768, 768], P('tp', 'clip'), may hold values from -128 to 128
- v_out: float32 [768, 768], P('tp', 'clip'), may hold values from 385.536 to 1526.08
- m_up: float32 [768, 3072], P('clip', 'tp'), may hold values from -160 to 160
- v_up: float32 [768, 3072], P('clip', 'tp'), may hold values from 722.88 to 2891.52
- m_down: float32 [3072, 768], P('tp', 'clip'), may hold values from -320 to 320
- v_down: float32 [3072, 768], P('tp', 'clip'), may hold values from 3373.44 to 13574.08
- m_norms: float32 [4, 768], P(None, 'clip'), may hold values from -512 to 512
- v_norms: float32 [4, 768], P(None, 'clip'), may hold values from 8032 to 32128
Outputs:
- block_out: bfloat16 [16, 704, 768], P('clip')
- patch_grad: float32 [16, 1188, 768], P('clip')
- norm_grad: float32 [4, 768], P(None, 'clip')
- new_qkv: float32 [768, 3, 768], P(None, None, 'tp')
- new_out: float32 [768, 768], P('tp')
- new_up: float32 [768, 3072], P(None, 'tp')
- new_down: float32 [3072, 768], P('tp')
- new_norms: float32 [4, 768], replicated
- mom1_qkv: float32 [768, 3, 768], P('clip', None, 'tp')
- mom1_out: float32 [768, 768], P('tp', 'clip')
- mom1_up: float32 [768, 3072], P('clip', 'tp')
- mom1_down: float32 [3072, 768], P('tp', 'clip')
- mom1_norms: float32 [4, 768], P(None, 'clip')
- mom2_qkv: float32 [768, 3, 768], P('clip', None, 'tp')
- mom2_out: float32 [768, 768], P('tp', 'clip')
- mom2_up: float32 [768, 3072], P('clip', 'tp')
- mom2_down: float32 [3072, 768], P('tp', 'clip')
- mom2_norms: float32 [4, 768], P(None, 'clip')
- low_qkv: bfloat16 [768, 3, 768], P(None, None, 'tp')
- low_out: bfloat16 [768, 768], P('tp')
- low_up: bfloat16 [768, 3072], P(None, 'tp')
- low_down: bfloat16 [3072, 768], P('tp')
The draws below stay inside these ranges and needn't reach their ends.
Inputs may be any that keep to these rules, and one draw needn't show every extreme that they name: `keep_freq`: each clip keeps between 4 and 12 frequency bins; its kept bins times kept frames lie between 300 and 704, and in every draw some clip keeps exactly 704 patches. `keep_time`: together with keep_freq, each clip keeps between 300 and 704 patches.
All inputs are finite; a program needn't handle non-finite values.
Results may differ from the reference program's by a relative error of at most 0.014.
The reference program's roundings to bfloat16 on the way count: a program that leaves them out, or rounds other values in their place, can miss the bound.
Values sent between devices are 32-bit elements; how exact they have to be, the bound alone decides.
No kernel may reach another device: no remote copies, remote signals or barrier semaphores. Data moves between devices by JAX's collectives and lax.ppermute only.
A program may use at most 128 MiB of HBM per device.

```python
import math
import jax
import jax.numpy as jnp
from jax import lax

D = 768
HEADS = 12
HD = 64
FF = 3072
FREQ = 12
FRAMES = 99
BLOCK = 704
LEAST = 300
STEP = 3
CLIPS = 16


def keep_lists(key):
    base = jax.random.fold_in(key, 7)
    key_freq, key_time, key_full, perm_freq, perm_time = jax.random.split(base, 5)
    least_freq = FREQ // 3
    count_freq = jax.random.randint(key_freq, (CLIPS,), least_freq, FREQ + 1)
    lower_time = (LEAST + count_freq - 1) // count_freq
    upper_time = jnp.minimum(FRAMES, BLOCK // count_freq)
    count_time = jax.random.randint(key_time, (CLIPS,), lower_time, upper_time + 1)
    full_clip = jax.random.randint(key_full, (), 0, CLIPS)
    is_full = jnp.arange(CLIPS) == full_clip
    full_freq = FREQ * 2 // 3
    count_freq = jnp.where(is_full, full_freq, count_freq)
    count_time = jnp.where(is_full, BLOCK // full_freq, count_time)
    order_freq = jax.vmap(lambda sub_key: jax.random.permutation(sub_key, FREQ))(jax.random.split(perm_freq, CLIPS))
    order_time = jax.vmap(lambda sub_key: jax.random.permutation(sub_key, FRAMES))(jax.random.split(perm_time, CLIPS))
    keep_freq = (order_freq < count_freq[:, None]).astype(jnp.int32)
    keep_time = (order_time < count_time[:, None]).astype(jnp.int32)
    return (keep_freq, keep_time)


def draw_keep_freq(key, part):
    return keep_lists(key)[0]


def draw_keep_time(key, part):
    return keep_lists(key)[1]


def draw_norms(key, part):
    key = jax.random.fold_in(key, 11)
    normal_draw = jax.random.normal(key, (4, D), jnp.float32)
    row_index = jnp.arange(4)[:, None]
    gain_rows = jnp.clip(1.0 + 0.1 * normal_draw, 0.5, 1.5)
    shift_rows = jnp.clip(0.2 * normal_draw, -1.0, 1.0)
    return jnp.where(row_index % 2 == 0, gain_rows, shift_rows).astype(jnp.float32)


def level_of(own_key, shape, shards, least, high):
    loudness, own = 1.0, jax.random.fold_in(own_key, 6)
    for position, shards_of in shards:
        heights = jnp.exp(jax.random.uniform(jax.random.fold_in(own, position), (shards_of,), jnp.float32, least / len(shards), high / len(shards)))
        loudness = loudness * jnp.repeat(heights, shape[position] // shards_of).reshape([-1 if axis == position else 1 for axis in range(len(shape))])
    return loudness


def normal_values(stream_key, dims, scale, reach, cuts=(), kind=jnp.bfloat16):
    factor_of = level_of(stream_key, dims, cuts, -0.22, 0.18) if cuts else 1.0
    values = jax.random.normal(stream_key, dims, jnp.float32) * scale * factor_of
    return jnp.minimum(jnp.maximum(values, -reach), reach).astype(kind)


def setup_inputs(seed: int = 0) -> dict:
    arg_keys = jax.random.split(jax.random.key(seed), 20)
    return {
        "patches": normal_values(arg_keys[0], (CLIPS, FREQ * FRAMES, D), 1.0, 6.0, ((0, 8),)),
        "keep_freq": draw_keep_freq(jax.random.fold_in(arg_keys[19], 71), 0),
        "keep_time": draw_keep_time(jax.random.fold_in(arg_keys[19], 71), 0),
        "cotangent": normal_values(arg_keys[3], (CLIPS, BLOCK, D), 1.0, 6.0, ((0, 8),)),
        "w_qkv": normal_values(arg_keys[4], (D, 3, D), D ** -0.5, 0.21875, ((2, 4),), jnp.float32),
        "w_out": normal_values(arg_keys[5], (D, D), (max(16 * D // BLOCK, 1)) ** -0.5, 1.5, ((0, 4),), jnp.float32),
        "w_up": normal_values(arg_keys[6], (D, FF), D ** -0.5, 0.21875, ((1, 4),), jnp.float32),
        "w_down": normal_values(arg_keys[7], (FF, D), FF ** -0.5, 0.109375, ((0, 4),), jnp.float32),
        "norms": draw_norms(jax.random.fold_in(arg_keys[19], 71), 0),
        "m_qkv": normal_values(arg_keys[9], (D, 3, D), (0.5 * ((LEAST + BLOCK) // 2 * CLIPS) ** 0.5), 256.0, ((0, 8), (2, 4)), jnp.float32),
        "v_qkv": jnp.clip(jnp.exp(math.log(8032.0) - 1.3862944 * jax.random.uniform(arg_keys[10], (D, 3, D), jnp.float32) ** level_of(arg_keys[10], (D, 3, D), ((0, 8), (2, 4)), -0.2, 0.2)), 2008.0, 8032.0),
        "m_out": normal_values(arg_keys[11], (D, D), (0.22 * ((LEAST + BLOCK) // 2 * CLIPS) ** 0.5), 128.0, ((0, 4), (1, 8)), jnp.float32),
        "v_out": jnp.clip(jnp.exp(math.log(1526.08) - 1.375823 * jax.random.uniform(arg_keys[12], (D, D), jnp.float32) ** level_of(arg_keys[12], (D, D), ((0, 4), (1, 8)), -0.2, 0.2)), 385.536, 1526.08),
        "m_up": normal_values(arg_keys[13], (D, FF), (0.3 * ((LEAST + BLOCK) // 2 * CLIPS) ** 0.5), 160.0, ((0, 8), (1, 4)), jnp.float32),
        "v_up": jnp.clip(jnp.exp(math.log(2891.52) - 1.3862944 * jax.random.uniform(arg_keys[14], (D, FF), jnp.float32) ** level_of(arg_keys[14], (D, FF), ((0, 8), (1, 4)), -0.2, 0.2)), 722.88, 2891.52),
        "m_down": normal_values(arg_keys[15], (FF, D), (0.65 * ((LEAST + BLOCK) // 2 * CLIPS) ** 0.5), 320.0, ((0, 4), (1, 8)), jnp.float32),
        "v_down": jnp.clip(jnp.exp(math.log(13574.08) - 1.3922291 * jax.random.uniform(arg_keys[16], (FF, D), jnp.float32) ** level_of(arg_keys[16], (FF, D), ((0, 4), (1, 8)), -0.2, 0.2)), 3373.44, 13574.08),
        "m_norms": normal_values(arg_keys[17], (4, D), (1.0 * ((LEAST + BLOCK) // 2 * CLIPS) ** 0.5), 512.0, ((1, 8),), jnp.float32),
        "v_norms": jnp.clip(jnp.exp(math.log(32128.0) - 1.3862944 * jax.random.uniform(arg_keys[18], (4, D), jnp.float32) ** level_of(arg_keys[18], (4, D), ((1, 8),), -0.2, 0.2)), 8032.0, 32128.0),
    }


HIGH = lax.Precision.HIGHEST
EPSILON = 1e-06

@jax.custom_vjp
def low(v):
    return lax.optimization_barrier(v.astype(jnp.bfloat16)).astype(jnp.float32)

@jax.custom_vjp
def low_back(v):
    return v

def low_keep(v):
    return (low(v), None)

def low_pass(kept, grad):
    return (grad,)

def back_keep(v):
    return (v, None)

def back_low(kept, grad):
    return (low(grad),)
low.defvjp(low_keep, low_pass)
low_back.defvjp(back_keep, back_low)

def positions(keep_freq, keep_time):
    freq_int = keep_freq.astype(jnp.int32)
    time_int = keep_time.astype(jnp.int32)
    rank_freq = jnp.cumsum(freq_int, axis=-1) - freq_int
    rank_time = jnp.cumsum(time_int, axis=-1) - time_int
    time_count = lax.optimization_barrier(jnp.sum(time_int, axis=-1))
    placed = rank_freq[:, :, None] * time_count[:, None, None] + rank_time[:, None, :]
    present = freq_int[:, :, None] * time_int[:, None, :] > 0
    placed = jnp.where(present, placed, -1).reshape(placed.shape[0], -1)
    kept_count = lax.optimization_barrier(jnp.sum(freq_int, axis=-1)) * time_count
    return (placed.astype(jnp.int32), kept_count.astype(jnp.int32))

def layer_norm(values, norm_gain, norm_shift):
    centre = values - lax.optimization_barrier(jnp.mean(values, axis=-1, keepdims=True))
    spread = lax.optimization_barrier(jnp.mean(centre * centre, axis=-1, keepdims=True))
    return centre * lax.rsqrt(spread + EPSILON) * norm_gain + norm_shift

def attend(members):
    queries, key_rows, value_rows, key_live = members
    scores = jnp.einsum('jhe,khe->hjk', queries, key_rows, precision=HIGH) * HD ** (-0.5)
    scores = low_back(jnp.where(key_live[None, None, :], scores, -1000000000.0))
    soft_weights = low(jax.nn.softmax(scores, axis=-1))
    mixed = jnp.einsum('hjk,khe->jhe', soft_weights, value_rows, precision=HIGH)
    return low_back(low(mixed))

def forward(patch_vals, w_qkv, w_out, w_up, w_down, norms, select, key_live, row_live):
    clip_count = select.shape[0]
    block_len = select.shape[1]
    inputs = low_back(jnp.einsum('cjp,cpd->cjd', select, patch_vals, precision=HIGH))
    first = low(layer_norm(inputs, norms[0], norms[1]))
    packed = low_back(low(jnp.einsum('cjd,dke->cjke', first, low(w_qkv), precision=HIGH)))
    queries = packed[:, :, 0].reshape(clip_count, block_len, HEADS, HD)
    key_rows = packed[:, :, 1].reshape(clip_count, block_len, HEADS, HD)
    value_rows = packed[:, :, 2].reshape(clip_count, block_len, HEADS, HD)
    mixed = lax.map(jax.checkpoint(attend), (queries, key_rows, value_rows, key_live))
    mixed = mixed.reshape(clip_count, block_len, D)
    attn = low_back(jnp.einsum('cjf,fd->cjd', mixed, low(w_out), precision=HIGH))
    middle = inputs + attn
    second = low(layer_norm(middle, norms[2], norms[3]))
    hidden = low_back(jnp.einsum('cjd,df->cjf', second, low(w_up), precision=HIGH))
    active = low(jax.nn.gelu(hidden, approximate=False))
    branch = low_back(jnp.einsum('cjf,fd->cjd', active, low(w_down), precision=HIGH))
    return (middle + branch) * row_live[:, :, None]

def adam_step(weight, gradient, first_mom, second_mom, rate):
    first_new = 0.5 * first_mom + 0.5 * gradient
    second_new = 0.5 * second_mom + 0.5 * gradient * gradient
    fix = 1.0 - 0.5 ** STEP
    direction = first_new / fix / (jnp.sqrt(second_new / fix) + 1e-08)
    return (weight - rate * (direction + 0.01 * weight), first_new, second_new)

def reference(patches, keep_freq, keep_time, cotangent, w_qkv, w_out, w_up, w_down, norms, m_qkv, v_qkv, m_out, v_out, m_up, v_up, m_down, v_down, m_norms, v_norms):
    placed, kept_count = positions(keep_freq, keep_time)
    slot_ids = jnp.arange(BLOCK, dtype=jnp.int32)
    select = (placed[:, None, :] == slot_ids[None, :, None]).astype(jnp.float32)
    key_live = slot_ids[None, :] < kept_count[:, None]
    row_live = key_live.astype(jnp.float32)

    def tied(patch_vals, weight_qkv, weight_out, weight_up, weight_down, norm_vals):
        return forward(patch_vals, weight_qkv, weight_out, weight_up, weight_down, norm_vals, select, key_live, row_live)
    result, pull = jax.vjp(tied, patches.astype(jnp.float32), w_qkv, w_out, w_up, w_down, norms)
    grad_patch, grad_qkv, grad_out, grad_up, grad_down, grad_norms = pull(cotangent.astype(jnp.float32))
    rate_model = D ** (-0.5)
    qkv_new = adam_step(w_qkv, grad_qkv, m_qkv, v_qkv, rate_model)
    out_new = adam_step(w_out, grad_out, m_out, v_out, max(16 * D // BLOCK, 1) ** (-0.5))
    up_new = adam_step(w_up, grad_up, m_up, v_up, rate_model)
    down_new = adam_step(w_down, grad_down, m_down, v_down, FF ** (-0.5))
    norms_new = adam_step(norms, grad_norms, m_norms, v_norms, 0.3)
    return (result.astype(jnp.bfloat16), grad_patch, grad_norms, qkv_new[0], out_new[0], up_new[0], down_new[0], norms_new[0], qkv_new[1], out_new[1], up_new[1], down_new[1], norms_new[1], qkv_new[2], out_new[2], up_new[2], down_new[2], norms_new[2], qkv_new[0].astype(jnp.bfloat16), out_new[0].astype(jnp.bfloat16), up_new[0].astype(jnp.bfloat16), down_new[0].astype(jnp.bfloat16))
```

```python
import functools

import jax
import jax.numpy as jnp
from jax import lax
from jax.experimental import pallas as pl
from jax.experimental.pallas import tpu as pltpu
from jax.sharding import PartitionSpec as P

D = 768
HD = 64
FF = 3072
BLOCK = 704
STEP = 3
EPSILON = 1e-06
SCALE = HD ** (-0.5)
GROUP = 8
F32 = jnp.float32
BF16 = jnp.bfloat16
VMEM_LIMIT = 56 * 2**20


def dot(left, right, left_dim, right_dim):
    return lax.dot_general(
        left, right, (((left_dim,), (right_dim,)), ((), ())), preferred_element_type=F32
    )


def positions(keep_freq, keep_time):
    rank_freq = jnp.cumsum(keep_freq, axis=-1) - keep_freq
    rank_time = jnp.cumsum(keep_time, axis=-1) - keep_time
    time_count = jnp.sum(keep_time, axis=-1)
    placed = rank_freq[:, :, None] * time_count[:, None, None] + rank_time[:, None, :]
    present = keep_freq[:, :, None] * keep_time[:, None, :] > 0
    placed = jnp.where(present, placed, -1).reshape(placed.shape[0], -1)
    kept_count = jnp.sum(keep_freq, axis=-1) * time_count
    return (placed, kept_count)


def norm_parts(values):
    centre = values - jnp.mean(values, axis=-1, keepdims=True)
    spread = jnp.mean(centre * centre, axis=-1, keepdims=True)
    inverse = lax.rsqrt(spread + EPSILON)
    return centre * inverse, inverse


def norm_back(values, gain, grad):
    unit, inverse = norm_parts(values)
    grad_unit = grad * gain
    mean_grad = jnp.mean(grad_unit, axis=-1, keepdims=True)
    mean_both = jnp.mean(grad_unit * unit, axis=-1, keepdims=True)
    back = inverse * (grad_unit - mean_grad - unit * mean_both)
    gain_grad = jnp.sum(grad * unit, axis=0, keepdims=True)
    shift_grad = jnp.sum(grad, axis=0, keepdims=True)
    return back, gain_grad, shift_grad


def live_column(kept, length):
    return lax.broadcasted_iota(jnp.int32, (length, 1), 0) < kept


def tree_sum(parts, odd):
    if len(parts) != 4:
        total = parts[0]
        for part in parts[1:]:
            total = total + part
        return total
    own, after, across, before = parts
    near = jnp.where(odd, before, after)
    far = jnp.where(odd, after, before)
    return (own + near) + (across + far)


def call(body, grid, in_specs, out_specs, out_shape, scratch=(), scalars=2, aliases=None, cost=None):
    return pl.pallas_call(
        body,
        grid_spec=pltpu.PrefetchScalarGridSpec(
            num_scalar_prefetch=scalars,
            grid=grid,
            in_specs=in_specs,
            out_specs=out_specs,
            scratch_shapes=list(scratch),
        ),
        out_shape=out_shape,
        input_output_aliases=aliases or {},
        compiler_params=pltpu.CompilerParams(
            dimension_semantics=("arbitrary",) * len(grid), vmem_limit_bytes=VMEM_LIMIT
        ),
        cost_estimate=pl.CostEstimate(flops=cost[0], bytes_accessed=cost[1], transcendentals=0)
        if cost
        else None,
    )


def clip_block(*dims):
    return pl.BlockSpec((1, *dims), lambda c, *_: (c,) + (0,) * len(dims))


def whole_block(*dims):
    return pl.BlockSpec(dims, lambda *_: (0,) * len(dims))


ANY = pl.BlockSpec(memory_space=pl.ANY)


def front_kernel(kept, order, placed, patches, cot, norms, inputs, first, grad):
    clip = pl.program_id(0)
    length, patch_count = first.shape[1], placed.shape[2]
    slots = lax.broadcasted_iota(jnp.int32, (length, patch_count), 0)
    select = jnp.where(placed[0] == slots, 1.0, 0.0).astype(BF16)
    picked = dot(select, patches[0], 1, 0)
    inputs[0] = picked
    unit, _ = norm_parts(picked)
    first[0] = (unit * norms[0:1] + norms[1:2]).astype(BF16)
    live = live_column(kept[clip], length)
    grad[0] = jnp.where(live, cot[0].astype(F32), 0.0).astype(BF16)


def piece_copies(order, sources, start, rows, target, sems):
    near, far = sources
    copies = []
    for slot in range(GROUP):
        source = (near if slot < GROUP // 2 else far).at[slot % (GROUP // 2), pl.ds(start, rows)]
        place = pl.multiple_of(order[slot] * rows, 8)
        copies.append(
            pltpu.make_async_copy(source, target.at[pl.ds(place, rows)], sems.at[slot])
        )
    return copies


def augment(rows, extra_row, length):
    index = lax.broadcasted_iota(jnp.int32, (16, length), 0)
    extra = jnp.where(index == 0, extra_row, 0.0).astype(BF16)
    return jnp.concatenate([rows, extra], axis=0)


def key_bias(kept, length):
    slot = lax.broadcasted_iota(jnp.int32, (1, length), 1)
    return jnp.where(slot < kept, 0.0, -1000000000.0)


def attend_kernel(own, heads, kept, order, first, *refs):
    clip = pl.program_id(0)
    if own:
        source, packed, mixed, total, low = refs

        @pl.when(clip == 0)
        def _():
            low[...] = source[...].astype(BF16)
    else:
        near, far, packed, mixed, total, low, staged, sems = refs

        @pl.when(clip == 0)
        def _():
            copies = piece_copies(order, (near, far), 0, low.shape[0] // GROUP, staged, sems)
            for copy in copies:
                copy.start()
            for copy in copies:
                copy.wait()
            low[...] = staged[...].astype(BF16)

    length = first.shape[1]
    width = heads * HD
    rows = dot(low[...], first[0], 1, 1).astype(BF16)
    packed[0] = rows
    bias = key_bias(kept[clip], length)
    ones = jnp.ones((1, length), F32)
    for head in range(heads):
        at = head * HD
        query = augment((rows[at : at + HD] * SCALE).astype(BF16), ones, length)
        key = augment(rows[width + at : width + at + HD], bias, length)
        value = rows[2 * width + at : 2 * width + at + HD]
        scores = dot(key, query, 0, 0)
        largest = jnp.max(scores, axis=0, keepdims=True)
        exponent = jnp.exp(scores - largest)
        summed = jnp.sum(exponent, axis=0, keepdims=True)
        mix = dot(value, exponent.astype(BF16), 1, 0) / summed
        mixed[0, at : at + HD] = mix.astype(BF16)
        total[0, head : head + 1] = largest + jnp.log(summed)


def project_kernel(shards, kept, order, *refs):
    clip = pl.program_id(0)
    inputs, norms, source = refs[:3]
    pieces = refs[3 : 3 + 2 * (shards - 1)]
    mixes = refs[3 + 2 * (shards - 1) : 3 + 2 * (shards - 1) + shards]
    middle, second, low, staged, sems = refs[3 + 2 * (shards - 1) + shards :]

    @pl.when(clip == 0)
    def _():
        copies = []
        for shard in range(shards - 1):
            copies += piece_copies(
                order,
                pieces[2 * shard : 2 * shard + 2],
                0,
                low.shape[1] // GROUP,
                staged.at[shard],
                sems.at[shard],
            )
        for copy in copies:
            copy.start()
        low[0] = source[...].astype(BF16)
        for copy in copies:
            copy.wait()
        for shard in range(shards - 1):
            low[shard + 1] = staged[shard].astype(BF16)

    odd = order[GROUP] > 0
    parts = [dot(mixes[shard][0], low[shard], 0, 0) for shard in range(shards)]
    values = inputs[0] + tree_sum(parts, odd)
    middle[0] = values
    unit, _ = norm_parts(values)
    second[0] = (unit * norms[2:3] + norms[3:4]).astype(BF16)


HALF_ROOT = 0.7071067811865476
DENSITY = 0.3989422804014327


def mlp_kernel(own, chunk, kept, order, second, grad, *refs):
    clip = pl.program_id(0)
    if own:
        up_source, down_source, branch, back, up_grad, down_grad, up_low, down_low = refs

        @pl.when(clip == 0)
        def _():
            up_low[...] = up_source[...].astype(BF16)
            down_low[...] = down_source[...].astype(BF16)
            up_grad[...] = jnp.zeros_like(up_grad)
            down_grad[...] = jnp.zeros_like(down_grad)
    else:
        near, far, branch, back, up_low, down_low, staged, sems = refs

        @pl.when(clip == 0)
        def _():
            rows = up_low.shape[0] // GROUP
            skip = near.shape[1] - 2 * rows
            copies = []
            for index in range(2):
                copies += piece_copies(
                    order, (near, far), skip + index * rows, rows, staged.at[index], sems.at[index]
                )
            for copy in copies:
                copy.start()
            for copy in copies:
                copy.wait()
            up_low[...] = staged[0].astype(BF16)
            down_low[...] = staged[1].astype(BF16)

    rows = second[0]
    upstream = grad[0]
    branch_sum = None
    for start in range(0, up_low.shape[1], chunk):
        up = up_low[:, start : start + chunk]
        down = down_low[start : start + chunk]
        hidden = dot(rows, up, 1, 0)
        grad_active = dot(upstream, down, 1, 1)
        cumulative = 0.5 * (lax.erf(hidden * HALF_ROOT) + 1.0)
        active = (hidden * cumulative).astype(BF16)
        slope = cumulative + hidden * (DENSITY * jnp.exp(-0.5 * hidden * hidden))
        grad_hidden = (slope * grad_active).astype(BF16)
        branch_part = dot(active, down, 1, 0)
        back_part = dot(grad_hidden, up, 1, 1)
        branch_sum = branch_part if branch_sum is None else branch_sum + branch_part
        back_sum = back_part if start == 0 else back_sum + back_part
        if own:
            up_grad[:, start : start + chunk] += dot(rows, grad_hidden, 0, 0)
            down_grad[:, start : start + chunk] += dot(upstream, active, 0, 0)
    branch[0] = branch_sum
    back[0] = back_sum


def close_kernel(shards, kept, order, *refs):
    clip = pl.program_id(0)
    middle, grad, norms = refs[:3]
    branches = refs[3 : 3 + shards]
    backs = refs[3 + shards : 3 + 2 * shards]
    result, grad_middle, low, norm_grad = refs[3 + 2 * shards :]
    odd = order[GROUP] > 0
    live = live_column(kept[clip], middle.shape[1])
    values = middle[0]
    total = values + tree_sum([ref[0] for ref in branches], odd)
    result[0] = jnp.where(live, total, 0.0).astype(BF16)
    back, gain_grad, shift_grad = norm_back(
        values, norms[2:3], tree_sum([ref[0] for ref in backs], odd)
    )
    both = grad[0].astype(F32) + back
    grad_middle[0] = both
    low[0] = both.astype(BF16)

    @pl.when(clip == 0)
    def _():
        norm_grad[...] = jnp.zeros_like(norm_grad)

    norm_grad[0:1] += gain_grad
    norm_grad[1:2] += shift_grad


def attend_back_kernel(own, heads, kept, order, packed, mixed, total, grad, out_low, *refs):
    clip = pl.program_id(0)
    if own:
        first, grad_packed, qkv_grad, out_grad = refs
    else:
        (grad_packed,) = refs
    length = grad.shape[1]
    width = heads * HD
    grad_mixed = dot(out_low[0], grad[0], 1, 1).astype(BF16)
    bias = key_bias(kept[clip], length)
    ones = jnp.ones((1, length), F32)
    for head in range(heads):
        at = head * HD
        query_low = (packed[0, at : at + HD] * SCALE).astype(BF16)
        key_low = packed[0, width + at : width + at + HD]
        value = packed[0, 2 * width + at : 2 * width + at + HD]
        query = augment(query_low, ones, length)
        key = augment(key_low, bias, length)
        upstream = grad_mixed[at : at + HD]
        offset = jnp.sum(
            upstream.astype(F32) * mixed[0, at : at + HD].astype(F32), axis=0, keepdims=True
        )
        probs = jnp.exp(dot(key, query, 0, 0) - total[0, head : head + 1])
        grad_probs = dot(value, upstream, 0, 0)
        scores_low = (probs * (grad_probs - offset)).astype(BF16)
        probs_low = probs.astype(BF16)
        grad_packed[0, at : at + HD] = (dot(key_low, scores_low, 1, 0) * SCALE).astype(BF16)
        grad_packed[0, width + at : width + at + HD] = dot(query_low, scores_low, 1, 1).astype(BF16)
        grad_packed[0, 2 * width + at : 2 * width + at + HD] = dot(
            upstream, probs_low, 1, 1
        ).astype(BF16)
    if own:

        @pl.when(clip == 0)
        def _():
            qkv_grad[...] = jnp.zeros_like(qkv_grad)
            out_grad[...] = jnp.zeros_like(out_grad)

        qkv_grad[...] += dot(first[0], grad_packed[0], 0, 1)
        out_grad[...] += dot(grad[0], mixed[0], 0, 1)


def final_kernel(shards, kept, order, *refs):
    clip = pl.program_id(0)
    placed, inputs, grad_middle, norms = refs[:4]
    packs = refs[4 : 4 + shards]
    lows = refs[4 + shards : 4 + 2 * shards]
    patch_grad, norm_grad = refs[4 + 2 * shards :]
    odd = order[GROUP] > 0
    parts = [dot(packs[shard][0], lows[shard][...], 0, 0) for shard in range(shards)]
    back, gain_grad, shift_grad = norm_back(inputs[0], norms[0:1], tree_sum(parts, odd))
    low = (grad_middle[0] + back).astype(BF16)
    length, patch_count = low.shape[0], placed.shape[2]
    slots = lax.broadcasted_iota(jnp.int32, (length, patch_count), 0)
    select = jnp.where(placed[0] == slots, 1.0, 0.0).astype(BF16)
    patch_grad[0] = dot(select, low, 0, 0)

    @pl.when(clip == 0)
    def _():
        norm_grad[...] = jnp.zeros_like(norm_grad)

    norm_grad[0:1] += gain_grad
    norm_grad[1:2] += shift_grad


def bits_of(count):
    return count.bit_length() - 1


def swap_pairs(index, bits):
    out = index & 1
    bit = 1
    while bit < bits:
        if bit + 1 < bits:
            out = out | ((index >> bit & 1) << (bit + 1)) | ((index >> (bit + 1) & 1) << bit)
            bit += 2
        else:
            out = out | (index >> bit & 1) << bit
            bit += 1
    return out


def partner(clip, mask, bits):
    return clip ^ (swap_pairs(mask, bits) if clip & 1 else mask)


def exchange(array, mask, bits, clips, shards):
    pairs = [
        (clip * shards + shard, partner(clip, mask, bits) * shards + shard)
        for clip in range(clips)
        for shard in range(shards)
    ]
    return lax.ppermute(array, ("clip", "tp"), pairs)


def shift(array, step, clips, shards):
    pairs = [
        (clip * shards + (shard + step) % shards, clip * shards + shard)
        for clip in range(clips)
        for shard in range(shards)
    ]
    return lax.ppermute(array, ("clip", "tp"), pairs)


def gather_shard(piece, clips, shards):
    bits = bits_of(GROUP)
    pair = jnp.stack([piece, exchange(piece, 2, bits, clips, shards)])
    near = jnp.concatenate([pair, exchange(pair, 4, bits, clips, shards)])
    return near, exchange(near, 1, bits, clips, shards)


def gather_order(clip_index):
    bits = bits_of(GROUP)
    me = clip_index % GROUP
    odd = me & 1

    def place(base, parity, code):
        return base ^ jnp.where(parity == 1, swap_pairs(code, bits), code)

    codes = (0, 2, 4, 6)
    near = [place(me, odd, code) for code in codes]
    far = [place(me ^ 1, 1 - odd, code) for code in codes]
    return near + far


def scatter_sum(stack, clips, shards):
    bits = bits_of(clips)
    if clips == 1:
        return stack[0]
    got = exchange(stack[1::2], 1, bits, clips, shards)
    keep = stack[0::2]
    turned = [swap_pairs(2 * j, bits) // 2 for j in range(clips // 2)]
    stack = jnp.stack([keep[j] + got[turned[j]] for j in range(clips // 2)])
    for bit in reversed(range(1, bits)):
        half = stack.shape[0] // 2
        got = exchange(stack[half:], 1 << bit, bits, clips, shards)
        stack = stack[:half] + got
    return stack[0]


def spread(piece, clips, shards):
    bits = bits_of(clips)
    stack = piece[None]
    for bit in range(1, bits):
        stack = jnp.concatenate([stack, exchange(stack, 1 << bit, bits, clips, shards)])
    if clips == 1:
        return [stack[0]]
    got = exchange(stack, 1, bits, clips, shards)
    out = []
    for q in range(clips):
        if q & 1:
            out.append(got[swap_pairs(q ^ 1, bits) // 2])
        else:
            out.append(stack[q // 2])
    return out


def clip_order(clip_index, clips):
    bits = bits_of(clips)
    return [
        clip_index ^ jnp.where(clip_index & 1 == 1, swap_pairs(q, bits), q) for q in range(clips)
    ]


def sum_all(array, clips, shards):
    for bit in range(bits_of(clips)):
        pairs = [
            (clip * shards + shard, (clip ^ 1 << bit) * shards + shard)
            for clip in range(clips)
            for shard in range(shards)
        ]
        array = array + lax.ppermute(array, ("clip", "tp"), pairs)
    return array


def own_part(array, axis_dim, clip_index, parts):
    part_width = array.shape[axis_dim] // parts
    return lax.dynamic_slice_in_dim(array, clip_index * part_width, part_width, axis_dim)


def adam_step(weight, gradient, first_mom, second_mom, rate):
    first_new = 0.5 * first_mom + 0.5 * gradient
    second_new = 0.5 * second_mom + 0.5 * gradient * gradient
    fix = 1.0 - 0.5**STEP
    direction = first_new / fix / (jnp.sqrt(second_new / fix) + 1e-08)
    return (weight - rate * (direction + 0.01 * weight), first_new, second_new)


def on_device(
    patches,
    keep_freq,
    keep_time,
    cotangent,
    w_qkv,
    w_out,
    w_up,
    w_down,
    norms,
    m_qkv,
    v_qkv,
    m_out,
    v_out,
    m_up,
    v_up,
    m_down,
    v_down,
    m_norms,
    v_norms,
):
    clip_count, length, width = cotangent.shape
    patch_count = patches.shape[1]
    clips, shards = lax.axis_size("clip"), lax.axis_size("tp")
    clip_index, shard_index = lax.axis_index("clip"), lax.axis_index("tp")
    local = w_qkv.shape[2]
    heads = local // HD
    hidden = w_up.shape[1]
    packed_width = 3 * local
    member = clip_index % GROUP

    qkv_rows = jnp.transpose(w_qkv, (1, 2, 0)).reshape(packed_width, width)

    def piece_of(rows):
        return own_part(rows, 0, member, GROUP)

    qkv_piece = piece_of(qkv_rows)
    rest_piece = jnp.concatenate([piece_of(w_out), piece_of(w_up), piece_of(w_down)])
    qkv_pieces = [
        gather_shard(shift(qkv_piece, step, clips, shards), clips, shards)
        for step in range(1, shards)
    ]
    rest_pieces = [
        gather_shard(shift(rest_piece, step, clips, shards), clips, shards)
        for step in range(1, shards)
    ]
    order = jnp.stack([*gather_order(clip_index), shard_index & 1]).astype(jnp.int32)

    placed, kept = positions(keep_freq, keep_time)
    placed = placed[:, None, :].astype(jnp.int32)
    kept = kept.astype(jnp.int32)

    row = functools.partial(clip_block, length)
    shape = jax.ShapeDtypeStruct
    rows_f32 = shape((clip_count, length, width), F32)
    rows_low = shape((clip_count, length, width), BF16)
    grid = (clip_count,)

    inputs, first, grad = call(
        front_kernel,
        grid,
        [clip_block(1, patch_count), clip_block(patch_count, width), row(width), whole_block(4, width)],
        [row(width)] * 3,
        [rows_f32, rows_low, rows_low],
        cost=(2 * clip_count * length * patch_count * width, 20_000_000),
    )(kept, order, placed, patches, cotangent, norms)

    packs, mixes, totals, qkv_lows = [], [], [], []
    for shard in range(shards):
        own = shard == 0
        packed, mixed, total, low = call(
            functools.partial(attend_kernel, own, heads),
            grid,
            [row(width)] + ([whole_block(packed_width, width)] if own else [ANY, ANY]),
            [
                clip_block(packed_width, length),
                clip_block(local, length),
                clip_block(heads, length),
                whole_block(packed_width, width),
            ],
            [
                shape((clip_count, packed_width, length), BF16),
                shape((clip_count, local, length), BF16),
                shape((clip_count, heads, length), F32),
                shape((packed_width, width), BF16),
            ],
            scratch=()
            if own
            else (pltpu.VMEM((packed_width, width), F32), pltpu.SemaphoreType.DMA((GROUP,))),
            cost=(6_000_000_000, 10_000_000),
        )(kept, order, first, *((qkv_rows,) if own else qkv_pieces[shard - 1]))
        packs.append(packed)
        mixes.append(mixed)
        totals.append(total)
        qkv_lows.append(low)

    middle, second, out_lows = call(
        functools.partial(project_kernel, shards),
        grid,
        [row(width), whole_block(4, width), whole_block(local, width)]
        + [ANY] * (2 * (shards - 1))
        + [clip_block(local, length)] * shards,
        [row(width), row(width), whole_block(shards, local, width)],
        [rows_f32, rows_low, shape((shards, local, width), BF16)],
        scratch=(
            pltpu.VMEM((shards - 1, local, width), F32),
            pltpu.SemaphoreType.DMA((shards - 1, GROUP)),
        ),
        cost=(2_000_000_000, 15_000_000),
    )(
        kept,
        order,
        inputs,
        norms,
        w_out,
        *[piece for pair in rest_pieces for piece in pair],
        *mixes,
    )

    branches, backs = [], []
    for shard in range(shards):
        own = shard == 0
        weights = shape((width, hidden), F32)
        results = call(
            functools.partial(mlp_kernel, own, 256),
            grid,
            [row(width), row(width)]
            + ([whole_block(width, hidden), whole_block(hidden, width)] if own else [ANY, ANY]),
            [row(width), row(width)] + ([whole_block(width, hidden)] * 2 if own else []),
            [rows_f32, rows_f32] + ([weights, weights] if own else []),
            scratch=(pltpu.VMEM((width, hidden), BF16), pltpu.VMEM((hidden, width), BF16))
            + (
                ()
                if own
                else (
                    pltpu.VMEM((2, width, hidden), F32),
                    pltpu.SemaphoreType.DMA((2, GROUP)),
                )
            ),
            cost=(8_000_000_000, 18_000_000),
        )(kept, order, second, grad, *((w_up, w_down) if own else rest_pieces[shard - 1]))
        branches.append(results[0])
        backs.append(results[1])
        if own:
            grad_up, grad_down = results[2:]

    block_out, grad_middle, middle_low, norm_grad2 = call(
        functools.partial(close_kernel, shards),
        grid,
        [row(width), row(width), whole_block(4, width)] + [row(width)] * (2 * shards),
        [row(width), row(width), row(width), whole_block(2, width)],
        [rows_low, rows_f32, rows_low, shape((2, width), F32)],
        cost=(100_000_000, 50_000_000),
    )(kept, order, middle, grad, norms, *branches, *backs)

    grad_packs = []
    for shard in range(shards):
        own = shard == 0
        results = call(
            functools.partial(attend_back_kernel, own, heads),
            grid,
            [
                clip_block(packed_width, length),
                clip_block(local, length),
                clip_block(heads, length),
                row(width),
                pl.BlockSpec((1, local, width), functools.partial(lambda s, *_: (s, 0, 0), shard)),
            ]
            + ([row(width)] if own else []),
            [clip_block(packed_width, length)]
            + ([whole_block(width, packed_width), whole_block(width, local)] if own else []),
            [shape((clip_count, packed_width, length), BF16)]
            + (
                [shape((width, packed_width), F32), shape((width, local), F32)] if own else []
            ),
            cost=(10_000_000_000, 10_000_000),
        )(
            kept,
            order,
            packs[shard],
            mixes[shard],
            totals[shard],
            middle_low,
            out_lows,
            *((first,) if own else ()),
        )
        grad_packs.append(results[0])
        if own:
            grad_qkv, grad_out = results[1:]

    patch_grad, norm_grad1 = call(
        functools.partial(final_kernel, shards),
        grid,
        [clip_block(1, patch_count), row(width), row(width), whole_block(4, width)]
        + [clip_block(packed_width, length)] * shards
        + [whole_block(packed_width, width)] * shards,
        [clip_block(patch_count, width), whole_block(2, width)],
        [shape((clip_count, patch_count, width), F32), shape((2, width), F32)],
        cost=(8_000_000_000, 30_000_000),
    )(kept, order, placed, inputs, grad_middle, norms, *grad_packs, *qkv_lows)

    places = clip_order(clip_index, clips)
    part = width // clips

    def to_stack(array):
        blocks = array.reshape(clips, part, array.shape[1])
        return jnp.concatenate([lax.dynamic_slice_in_dim(blocks, at, 1, 0) for at in places])

    def from_list(pieces):
        stack = jnp.stack(pieces)
        bits = bits_of(clips)
        order_back = []
        for piece in range(clips):
            code = piece ^ clip_index
            order_back.append(jnp.where(clip_index & 1 == 1, swap_pairs(code, bits), code))
        return jnp.concatenate(
            [lax.dynamic_slice_in_dim(stack, at, 1, 0) for at in order_back]
        ).reshape(clips * part, -1)

    rate_model = D ** (-0.5)
    rest_sum = scatter_sum(
        to_stack(jnp.concatenate([grad_out, grad_up, grad_down], axis=1)), clips, shards
    )
    qkv_sum = scatter_sum(to_stack(grad_qkv), clips, shards)
    out_new = adam_step(
        own_part(w_out, 1, clip_index, clips),
        rest_sum[:, :local].T,
        m_out,
        v_out,
        max(16 * D // BLOCK, 1) ** (-0.5),
    )
    up_new = adam_step(
        own_part(w_up, 0, clip_index, clips), rest_sum[:, local : local + hidden], m_up, v_up, rate_model
    )
    down_new = adam_step(
        own_part(w_down, 1, clip_index, clips),
        rest_sum[:, local + hidden :].T,
        m_down,
        v_down,
        FF ** (-0.5),
    )
    qkv_new = adam_step(
        own_part(w_qkv, 0, clip_index, clips),
        qkv_sum.reshape(part, 3, local),
        m_qkv,
        v_qkv,
        rate_model,
    )
    rest_full = from_list(
        spread(jnp.concatenate([out_new[0].T, up_new[0], down_new[0].T], axis=1), clips, shards)
    )
    qkv_full = from_list(spread(qkv_new[0].reshape(part, packed_width), clips, shards))
    full_out = rest_full[:, :local].T
    full_up = rest_full[:, local : local + hidden]
    full_down = rest_full[:, local + hidden :].T
    full_qkv = qkv_full.reshape(width, 3, local)

    norm_sum = sum_all(jnp.concatenate([norm_grad1, norm_grad2]), clips, shards)
    piece_norms = own_part(norm_sum, 1, clip_index, clips)
    norms_new = adam_step(own_part(norms, 1, clip_index, clips), piece_norms, m_norms, v_norms, 0.3)
    full_norms = lax.all_gather(norms_new[0], "clip", axis=1, tiled=True)

    return (
        block_out,
        patch_grad,
        piece_norms,
        full_qkv,
        full_out,
        full_up,
        full_down,
        full_norms,
        qkv_new[1],
        out_new[1],
        up_new[1],
        down_new[1],
        norms_new[1],
        qkv_new[2],
        out_new[2],
        up_new[2],
        down_new[2],
        norms_new[2],
        full_qkv.astype(BF16),
        full_out.astype(BF16),
        full_up.astype(BF16),
        full_down.astype(BF16),
    )


def solution(mesh):
    return jax.shard_map(
        on_device,
        mesh=mesh,
        in_specs=(
            P("clip", None, None),
            P("clip", None),
            P("clip", None),
            P("clip", None, None),
            P(None, None, "tp"),
            P("tp", None),
            P(None, "tp"),
            P("tp", None),
            P(),
            P("clip", None, "tp"),
            P("clip", None, "tp"),
            P("tp", "clip"),
            P("tp", "clip"),
            P("clip", "tp"),
            P("clip", "tp"),
            P("tp", "clip"),
            P("tp", "clip"),
            P(None, "clip"),
            P(None, "clip"),
        ),
        out_specs=(
            P("clip", None, None),
            P("clip", None, None),
            P(None, "clip"),
            P(None, None, "tp"),
            P("tp", None),
            P(None, "tp"),
            P("tp", None),
            P(),
            P("clip", None, "tp"),
            P("tp", "clip"),
            P("clip", "tp"),
            P("tp", "clip"),
            P(None, "clip"),
            P("clip", None, "tp"),
            P("tp", "clip"),
            P("clip", "tp"),
            P("tp", "clip"),
            P(None, "clip"),
            P(None, None, "tp"),
            P("tp", None),
            P(None, "tp"),
            P("tp", None),
        ),
        check_vma=False,
    )
```

```python
import functools

import jax
import jax.numpy as jnp
from jax import lax
from jax.experimental import pallas as pl
from jax.experimental.pallas import tpu as pltpu
from jax.sharding import PartitionSpec as P

D = 768
HD = 64
FF = 3072
BLOCK = 704
STEP = 3
EPSILON = 1e-06
SCALE = HD ** (-0.5)
GROUP = 8
SOURCES = GROUP // 2
F32 = jnp.float32
BF16 = jnp.bfloat16
VMEM_LIMIT = 56 * 2**20
COST_PART = 10


def dot(left, right, left_dim, right_dim):
    return lax.dot_general(
        left, right, (((left_dim,), (right_dim,)), ((), ())), preferred_element_type=F32
    )


def positions(keep_freq, keep_time):
    bins, frames = keep_freq.shape[1], keep_time.shape[1]
    count = bins * frames
    patch = lax.broadcasted_iota(jnp.int32, (1, count), 1)
    patch_bin = jnp.zeros((1, count), jnp.int32)
    for index in range(1, bins):
        patch_bin += (patch >= index * frames).astype(jnp.int32)
    patch_frame = patch - patch_bin * frames

    def spread(index, size):
        return jnp.where(
            lax.broadcasted_iota(jnp.int32, (size, count), 0) == index, 1.0, 0.0
        ).astype(BF16)

    def before(size):
        row = lax.broadcasted_iota(jnp.int32, (size, size), 0)
        column = lax.broadcasted_iota(jnp.int32, (size, size), 1)
        return jnp.where(row < column, 1.0, 0.0).astype(BF16)

    freq, time = keep_freq.astype(F32).astype(BF16), keep_time.astype(F32).astype(BF16)
    rank_freq = dot(freq, before(bins), 1, 0).astype(BF16)
    rank_time = dot(time, before(frames), 1, 0).astype(BF16)
    by_bin, by_frame = spread(patch_bin, bins), spread(patch_frame, frames)
    time_count = jnp.sum(keep_time.astype(F32), axis=1, keepdims=True)
    placed = dot(rank_freq, by_bin, 1, 0) * time_count + dot(rank_time, by_frame, 1, 0)
    present = dot(freq, by_bin, 1, 0) * dot(time, by_frame, 1, 0)
    return jnp.where(present > 0.5, placed, -1.0).astype(jnp.int32)


def norm_parts(values):
    centre = values - jnp.mean(values, axis=-1, keepdims=True)
    spread = jnp.mean(centre * centre, axis=-1, keepdims=True)
    inverse = lax.rsqrt(spread + EPSILON)
    return centre * inverse, inverse


def norm_back(values, gain, grad):
    unit, inverse = norm_parts(values)
    grad_unit = grad * gain
    mean_grad = jnp.mean(grad_unit, axis=-1, keepdims=True)
    mean_both = jnp.mean(grad_unit * unit, axis=-1, keepdims=True)
    back = inverse * (grad_unit - mean_grad - unit * mean_both)
    gain_grad = jnp.sum(grad * unit, axis=0, keepdims=True)
    shift_grad = jnp.sum(grad, axis=0, keepdims=True)
    return back, gain_grad, shift_grad


def live_column(kept, length):
    return lax.broadcasted_iota(jnp.int32, (length, 1), 0) < kept


def tree_sum(parts, odd):
    if len(parts) != 4:
        total = parts[0]
        for part in parts[1:]:
            total = total + part
        return total
    own, after, across, before = parts
    near = jnp.where(odd, before, after)
    far = jnp.where(odd, after, before)
    return (own + near) + (across + far)


def call(body, grid, in_specs, out_specs, out_shape, scratch=(), scalars=2, aliases=None, cost=None):
    return pl.pallas_call(
        body,
        grid_spec=pltpu.PrefetchScalarGridSpec(
            num_scalar_prefetch=scalars,
            grid=grid,
            in_specs=in_specs,
            out_specs=out_specs,
            scratch_shapes=list(scratch),
        ),
        out_shape=out_shape,
        input_output_aliases=aliases or {},
        compiler_params=pltpu.CompilerParams(
            dimension_semantics=("arbitrary",) * len(grid), vmem_limit_bytes=VMEM_LIMIT
        ),
        cost_estimate=pl.CostEstimate(flops=cost[0] * COST_PART, bytes_accessed=cost[1] * COST_PART, transcendentals=0)
        if cost
        else None,
    )


def clip_block(*dims):
    return pl.BlockSpec((1, *dims), lambda c, *_: (c,) + (0,) * len(dims))


def whole_block(*dims):
    return pl.BlockSpec(dims, lambda *_: (0,) * len(dims))


ANY = pl.BlockSpec(memory_space=pl.ANY)


def front_kernel(kept, order, freq, time, patches, cot, norms, inputs, first, grad, placed):
    clip = pl.program_id(0)
    placed[0] = positions(freq[0], time[0])
    length, patch_count = first.shape[1], placed.shape[2]
    slots = lax.broadcasted_iota(jnp.int32, (length, patch_count), 0)
    select = jnp.where(placed[0] == slots, 1.0, 0.0).astype(BF16)
    picked = dot(select, patches[0], 1, 0)
    inputs[0] = picked
    unit, _ = norm_parts(picked)
    first[0] = (unit * norms[0:1] + norms[1:2]).astype(BF16)
    live = live_column(kept[clip], length)
    grad[0] = jnp.where(live, cot[0].astype(F32), 0.0).astype(BF16)


def pieces_kernel(kept, order, *refs):
    *sources, early, late, sems = refs
    copies = []
    for target, pair in ((early, sources[:2]), (late, sources[2:])):
        start = 0
        for source in pair:
            rows = source.shape[0] // GROUP
            place = pl.multiple_of(order[2 * GROUP] * rows, 8)
            copies.append(
                pltpu.make_async_copy(
                    source.at[pl.ds(place, rows)],
                    target.at[pl.ds(start, rows)],
                    sems.at[len(copies)],
                )
            )
            start += rows
    for copy in copies:
        copy.start()
    for copy in copies:
        copy.wait()


def piece_copies(order, sources, start, rows, target, sems):
    copies = []
    for slot in range(GROUP):
        source = sources[slot // 2].at[slot % 2, pl.ds(start, rows)]
        place = pl.multiple_of(order[slot] * rows, 8)
        copies.append(
            pltpu.make_async_copy(source, target.at[pl.ds(place, rows)], sems.at[slot])
        )
    return copies


def augment(rows, extra_row, length):
    index = lax.broadcasted_iota(jnp.int32, (16, length), 0)
    extra = jnp.where(index == 0, extra_row, 0.0).astype(BF16)
    return jnp.concatenate([rows, extra], axis=0)


def key_bias(kept, length):
    slot = lax.broadcasted_iota(jnp.int32, (1, length), 1)
    return jnp.where(slot < kept, 0.0, -1000000000.0)


def attend_kernel(mode, fixed, heads, kept, order, first, before, *refs):
    clip = pl.program_id(0) if fixed is None else fixed
    if mode == "own":
        source, out_source, packed, mixed, total, after, low, out_low = refs
        low[...] = source[...].astype(BF16)
        out_low[...] = out_source[...].astype(BF16)
    elif mode == "gathered":
        sources, (packed, mixed, total, after, low, out_low) = refs[:SOURCES], refs[SOURCES:-3]
        staged, out_staged, sems = refs[-3:]

        @pl.when(clip == 0)
        def _():
            rows, out_rows = low.shape[0] // GROUP, out_low.shape[0] // GROUP
            copies = piece_copies(order, sources, 0, rows, staged, sems.at[0])
            copies += piece_copies(order, sources, rows, out_rows, out_staged, sems.at[1])
            for copy in copies:
                copy.start()
            for copy in copies:
                copy.wait()
            low[...] = staged[...].astype(BF16)
            out_low[...] = out_staged[...].astype(BF16)
    else:
        low, out_low, _, _, _, _, packed, mixed, total, after = refs

    length = first.shape[1]
    width = heads * HD
    rows = dot(low[...], first[0], 1, 1).astype(BF16)
    packed[0] = rows
    bias = key_bias(kept[clip], length)
    ones = jnp.ones((1, length), F32)
    for head in range(heads):
        at = head * HD
        query = augment((rows[at : at + HD] * SCALE).astype(BF16), ones, length)
        key = augment(rows[width + at : width + at + HD], bias, length)
        value = rows[2 * width + at : 2 * width + at + HD]
        scores = dot(key, query, 0, 0)
        largest = jnp.max(scores, axis=0, keepdims=True)
        exponent = jnp.exp(scores - largest)
        summed = jnp.sum(exponent, axis=0, keepdims=True)
        mix = dot(value, exponent.astype(BF16), 1, 0) / summed
        mixed[0, at : at + HD] = mix.astype(BF16)
        total[0, head : head + 1] = largest + jnp.log(summed)
    after[0] = before[0] + dot(mixed[0], out_low[...], 0, 0)


HALF_ROOT = 0.7071067811865476
DENSITY = 0.3989422804014327


def load_mlp(order, sources, up_low, down_low, staged, sems):
    rows = up_low.shape[0] // GROUP
    copies = []
    for index in range(2):
        copies += piece_copies(
            order, sources, index * rows, rows, staged.at[index], sems.at[index]
        )
    for copy in copies:
        copy.start()
    for copy in copies:
        copy.wait()
    up_low[...] = staged[0].astype(BF16)
    down_low[...] = staged[1].astype(BF16)


def mlp_rows(rows, upstream, up_low, down_low, chunk, grads=None):
    branch_sum = back_sum = None
    for start in range(0, up_low.shape[1], chunk):
        up = up_low[:, start : start + chunk]
        down = down_low[start : start + chunk]
        hidden = dot(rows, up, 1, 0)
        grad_active = dot(upstream, down, 1, 1)
        cumulative = 0.5 * (lax.erf(hidden * HALF_ROOT) + 1.0)
        active = (hidden * cumulative).astype(BF16)
        slope = cumulative + hidden * (DENSITY * jnp.exp(-0.5 * hidden * hidden))
        grad_hidden = (slope * grad_active).astype(BF16)
        branch_part = dot(active, down, 1, 0)
        back_part = dot(grad_hidden, up, 1, 1)
        branch_sum = branch_part if branch_sum is None else branch_sum + branch_part
        back_sum = back_part if back_sum is None else back_sum + back_part
        if grads is not None:
            width = up_low.shape[1]
            grads[:, start : start + chunk] += dot(rows, grad_hidden, 0, 0)
            grads[:, width + start : width + start + chunk] += dot(upstream, active, 0, 0)
    return branch_sum, back_sum


def part_copies(order, source, keep, send, sems):
    rows = keep.shape[1]
    copies = []
    for slot in range(GROUP):
        target = (keep if slot < GROUP // 2 else send).at[slot % (GROUP // 2)]
        place = pl.multiple_of(order[GROUP + slot] * rows, 8)
        copies.append(pltpu.make_async_copy(source.at[pl.ds(place, rows)], target, sems.at[slot]))
    return copies


def mlp_own_kernel(chunk, kept, order, middle, grad, norms, up_source, down_source, *refs):
    second, branch, back, keep, send, up_low, down_low, grads, sems = refs
    clip = pl.program_id(0)

    @pl.when(clip == 0)
    def _():
        up_low[...] = up_source[...].astype(BF16)
        down_low[...] = down_source[...].astype(BF16)
        grads[...] = jnp.zeros_like(grads)

    values = middle[0]
    unit, _ = norm_parts(values)
    second[0] = (unit * norms[2:3] + norms[3:4]).astype(BF16)
    branch_part, back_part = mlp_rows(second[0], grad[0], up_low, down_low, chunk, grads)
    branch[0] = values + branch_part
    back[0] = back_part

    @pl.when(clip == pl.num_programs(0) - 1)
    def _():
        copies = part_copies(order, grads, keep, send, sems)
        for copy in copies:
            copy.start()
        for copy in copies:
            copy.wait()


def mlp_kernel(chunk, kept, order, second, grad, branch_in, back_in, *refs):
    sources = refs[:SOURCES]
    branch, back, up_low, down_low, staged, sems = refs[SOURCES:]
    clip = pl.program_id(0)

    @pl.when(clip == 0)
    def _():
        load_mlp(order, sources, up_low, down_low, staged, sems)

    branch_part, back_part = mlp_rows(second[0], grad[0], up_low, down_low, chunk)
    branch[0] = branch_in[0] + branch_part
    back[0] = back_in[0] + back_part


def mlp_last_kernel(chunk, kept, order, second, grad, branch_in, back_in, *refs):
    sources = refs[:SOURCES]
    middle, norms, result, grad_middle, low, norm_grad = refs[SOURCES : SOURCES + 6]
    up_low, down_low, staged, sems = refs[SOURCES + 6 :]
    clip = pl.program_id(0)

    @pl.when(clip == 0)
    def _():
        load_mlp(order, sources, up_low, down_low, staged, sems)
        norm_grad[...] = jnp.zeros_like(norm_grad)

    branch_part, back_part = mlp_rows(second[0], grad[0], up_low, down_low, chunk)
    live = live_column(kept[clip], middle.shape[1])
    result[0] = jnp.where(live, branch_in[0] + branch_part, 0.0).astype(BF16)
    back, gain_grad, shift_grad = norm_back(middle[0], norms[2:3], back_in[0] + back_part)
    both = grad[0].astype(F32) + back
    grad_middle[0] = both
    low[0] = both.astype(BF16)
    norm_grad[0:1] += gain_grad
    norm_grad[1:2] += shift_grad


def attend_back_kernel(own, heads, kept, order, packed, mixed, total, grad, low, out_low, *refs):
    clip = pl.program_id(0)
    if own:
        first, grad_packed, after, keep, send, grads, sems = refs
    else:
        before, after, grad_packed = refs
    length = grad.shape[1]
    width = heads * HD
    grad_mixed = dot(out_low[...], grad[0], 1, 1).astype(BF16)
    bias = key_bias(kept[clip], length)
    ones = jnp.ones((1, length), F32)
    for head in range(heads):
        at = head * HD
        query_low = (packed[0, at : at + HD] * SCALE).astype(BF16)
        key_low = packed[0, width + at : width + at + HD]
        value = packed[0, 2 * width + at : 2 * width + at + HD]
        query = augment(query_low, ones, length)
        key = augment(key_low, bias, length)
        upstream = grad_mixed[at : at + HD]
        offset = jnp.sum(
            upstream.astype(F32) * mixed[0, at : at + HD].astype(F32), axis=0, keepdims=True
        )
        probs = jnp.exp(dot(key, query, 0, 0) - total[0, head : head + 1])
        grad_probs = dot(value, upstream, 0, 0)
        scores_low = (probs * (grad_probs - offset)).astype(BF16)
        probs_low = probs.astype(BF16)
        grad_packed[0, at : at + HD] = (dot(key_low, scores_low, 1, 0) * SCALE).astype(BF16)
        grad_packed[0, width + at : width + at + HD] = dot(query_low, scores_low, 1, 1).astype(BF16)
        grad_packed[0, 2 * width + at : 2 * width + at + HD] = dot(
            upstream, probs_low, 1, 1
        ).astype(BF16)
    back = dot(grad_packed[0], low[...], 0, 0)
    if own:
        after[0] = back

        @pl.when(clip == 0)
        def _():
            grads[...] = jnp.zeros_like(grads)

        grads[:, : 3 * width] += dot(first[0], grad_packed[0], 0, 1)
        grads[:, 3 * width :] += dot(grad[0], mixed[0], 0, 1)

        @pl.when(clip == pl.num_programs(0) - 1)
        def _():
            copies = part_copies(order, grads, keep, send, sems)
            for copy in copies:
                copy.start()
            for copy in copies:
                copy.wait()
    else:
        after[0] = before[0] + back


def final_kernel(kept, order, inputs, grad_middle, norms, grad_first, low, norm_grad):
    clip = pl.program_id(0)
    back, gain_grad, shift_grad = norm_back(inputs[0], norms[0:1], grad_first[0])
    low[0] = (grad_middle[0] + back).astype(BF16)

    @pl.when(clip == 0)
    def _():
        norm_grad[...] = jnp.zeros_like(norm_grad)

    norm_grad[0:1] += gain_grad
    norm_grad[1:2] += shift_grad


def unselect_kernel(kept, order, placed, low, patch_grad):
    clip_count, length, width = low.shape
    patch_count = placed.shape[2]
    lanes = 128
    tiles = width // lanes
    slots = lax.broadcasted_iota(jnp.int32, (length, patch_count), 0)
    for clip in range(clip_count):
        select = jnp.where(placed[clip] == slots, 1.0, 0.0).astype(BF16)
        back = dot(select, low[clip], 0, 0)
        for tile in range(tiles):
            rows = pl.ds(tile * clip_count + clip, patch_count, stride=tiles * clip_count)
            patch_grad[rows, :] = back[:, tile * lanes : (tile + 1) * lanes]


def adam_direction(gradient, first_mom, second_mom):
    first_new = 0.5 * first_mom + 0.5 * gradient
    second_new = 0.5 * second_mom + 0.5 * gradient * gradient
    fix = 1.0 - 0.5**STEP
    direction = first_new / fix / (jnp.sqrt(second_new / fix) + 1e-08)
    return direction, first_new, second_new


def moments_kernel(layout, kept, order, gradient, *refs):
    count = len(layout)
    firsts, seconds = refs[:count], refs[count : 2 * count]
    direction, first_outs, second_outs = (
        refs[2 * count],
        refs[2 * count + 1 : 3 * count + 1],
        refs[3 * count + 1 :],
    )
    start = 0
    for index, (wide, form) in enumerate(layout):
        parts = 3 if form == "stack" else 1
        for part in range(parts):
            columns = slice(start, start + wide)
            grad = gradient[:, columns]
            if form == "turned":
                first, second = firsts[index][...].T, seconds[index][...].T
            elif form == "stack":
                first, second = firsts[index][part], seconds[index][part]
            else:
                first, second = firsts[index][...], seconds[index][...]
            step, first, second = adam_direction(grad, first, second)
            direction[:, columns] = step
            if form == "turned":
                first_outs[index][...], second_outs[index][...] = first.T, second.T
            elif form == "stack":
                first_outs[index][part], second_outs[index][part] = first, second
            else:
                first_outs[index][...], second_outs[index][...] = first, second
            start += wide


def assemble_kernel(layout, kept, order, *refs):
    count = len(layout)
    sources, refs = refs[:SOURCES], refs[SOURCES:]
    weights, outs = refs[:count], refs[count : 3 * count]
    staged, sems = refs[3 * count :]
    copies = piece_copies(order, sources, 0, sources[0].shape[1], staged, sems)
    for copy in copies:
        copy.start()
    for copy in copies:
        copy.wait()
    start = 0
    for index, (wide, turned, rate) in enumerate(layout):
        step = staged[:, start : start + wide]
        if turned:
            step = step.T
        weight = weights[index][...]
        values = weight - rate * (step + 0.01 * weight)
        outs[2 * index][...] = values
        outs[2 * index + 1][...] = values.astype(BF16)
        start += wide


def swap_bits(code):
    return code & 1 | (code >> 2 & 1) << 1 | (code >> 1 & 1) << 2


def members(clips):
    return clips // GROUP


def exchange(array, code, clips, shards):
    step = members(clips)
    pairs = []
    for clip in range(clips):
        member, rest = divmod(clip, step)
        other = member ^ (swap_bits(code) if member & 1 else code)
        for shard in range(shards):
            pairs.append((clip * shards + shard, (other * step + rest) * shards + shard))
    return lax.ppermute(array, ("clip", "tp"), pairs)


def swap_rest(array, mask, clips, shards):
    pairs = [
        (clip * shards + shard, (clip ^ mask) * shards + shard)
        for clip in range(clips)
        for shard in range(shards)
    ]
    return lax.ppermute(array, ("clip", "tp"), pairs)


def shift(array, step, clips, shards):
    pairs = [
        (clip * shards + (shard + step) % shards, clip * shards + shard)
        for clip in range(clips)
        for shard in range(shards)
    ]
    return lax.ppermute(array, ("clip", "tp"), pairs)


def tie(array, *others):
    return lax.optimization_barrier((array, *others))[0]


def piece_order(member):
    odd = member & 1

    def place(base, parity, code):
        return base ^ jnp.where(parity == 1, swap_bits(code), code)

    near = [place(member, odd, code) for code in (0, 2, 4, 6)]
    far = [place(member ^ 1, 1 - odd, code) for code in (0, 2, 4, 6)]
    return near + far


def grad_order(member):
    odd = member & 1

    def place(code):
        return member ^ jnp.where(odd == 1, swap_bits(code), code)

    return [place(code) for code in (0, 2, 4, 6)] + [place(code) for code in (1, 5, 3, 7)]


def sum_rest(part, clips, shards, clip_index):
    step = members(clips)
    rest = clip_index % step
    half = step // 2
    while half:
        low, high = jnp.split(part, 2)
        upper = (rest & half) > 0
        got = swap_rest(jnp.where(upper, low, high), half, clips, shards)
        part = jnp.where(upper, high, low) + got
        half //= 2
    return part


def gather_rest(part, clips, shards, clip_index):
    step = members(clips)
    rest = clip_index % step
    half = 1
    while half < step:
        got = swap_rest(part, half, clips, shards)
        upper = (rest & half) > 0
        part = jnp.concatenate([jnp.where(upper, got, part), jnp.where(upper, part, got)])
        half *= 2
    return part


def sum_all(array, clips, shards):
    mask = 1
    while mask < clips:
        array = array + swap_rest(array, mask, clips, shards)
        mask *= 2
    return array


def own_part(array, axis_dim, clip_index, parts):
    part_width = array.shape[axis_dim] // parts
    return lax.dynamic_slice_in_dim(array, clip_index * part_width, part_width, axis_dim)


def on_device(
    patches,
    keep_freq,
    keep_time,
    cotangent,
    w_qkv,
    w_out,
    w_up,
    w_down,
    norms,
    m_qkv,
    v_qkv,
    m_out,
    v_out,
    m_up,
    v_up,
    m_down,
    v_down,
    m_norms,
    v_norms,
):
    clip_count, length, width = cotangent.shape
    patch_count = patches.shape[1]
    clips, shards = lax.axis_size("clip"), lax.axis_size("tp")
    clip_index, shard_index = lax.axis_index("clip"), lax.axis_index("tp")
    local = w_qkv.shape[2]
    heads = local // HD
    hidden = w_up.shape[1]
    packed_width = 3 * local
    member = clip_index % GROUP

    group = members(clips)
    member = clip_index // group
    waiting, started, slow = [], [], []

    def ex(array, code):
        started.append(exchange(array, code, clips, shards))
        return started[-1]

    def move(array, step, two_kernels=False):
        kind = slow if two_kernels else started
        kind.append(shift(array, step, clips, shards))
        return kind[-1]

    def swap(array, mask):
        started.append(swap_rest(array, mask, clips, shards))
        return started[-1]

    def gate(array):
        array = tie(array, *waiting)
        waiting[:] = started
        started[:] = slow
        slow.clear()
        return array

    shape = jax.ShapeDtypeStruct

    qkv_rows = jnp.transpose(w_qkv, (1, 2, 0)).reshape(packed_width, width)

    order = jnp.stack([*piece_order(member), *grad_order(member), member]).astype(jnp.int32)
    kept = (jnp.sum(keep_freq, axis=-1) * jnp.sum(keep_time, axis=-1)).astype(jnp.int32)
    early_piece, late_piece = call(
        pieces_kernel,
        (1,),
        [ANY] * 4,
        [
            whole_block((packed_width + local) // GROUP, width),
            whole_block((width + hidden) // GROUP, width),
        ],
        [
            shape(((packed_width + local) // GROUP, width), F32),
            shape(((width + hidden) // GROUP, width), F32),
        ],
        scratch=(pltpu.SemaphoreType.DMA((4,)),),
        cost=(1_000_000, 4_000_000),
    )(kept, order, qkv_rows, w_out, w_up, w_down)
    steps = (1, 3, 2) if shards == 4 else tuple(range(1, shards))
    early = {step: [move(early_piece, step)] for step in steps[:2]}
    late = {}

    def hop(pieces, done):
        if len(pieces) == 1:
            return [*pieces, ex(tie(pieces[0], done), 2)]
        if pieces[0].ndim == 2:
            pair = jnp.stack([tie(piece, done) for piece in pieces])
            return [pair, ex(pair, 4)]
        return [*pieces, *[ex(tie(piece, done), 1) for piece in pieces]]

    row = functools.partial(clip_block, length)
    rows_f32 = shape((clip_count, length, width), F32)
    rows_low = shape((clip_count, length, width), BF16)
    grid = (clip_count,)

    def fixed_block(clip, *dims):
        return pl.BlockSpec((1, *dims), lambda *_: (clip,) + (0,) * len(dims))

    s1, s2, s3 = steps
    freq = gate(tie(keep_freq[:, None, :], early[s1][0], early[s2][0]))
    waiting.clear()
    early[s1] = hop(early[s1], freq)
    early[s2] = hop(early[s2], freq)
    early[s3] = [move(tie(early_piece, freq), s3)]
    inputs, first, grad, placed = call(
        front_kernel,
        grid,
        [
            clip_block(1, keep_freq.shape[1]),
            clip_block(1, keep_time.shape[1]),
            clip_block(patch_count, width),
            row(width),
            whole_block(4, width),
        ],
        [row(width)] * 3 + [clip_block(1, patch_count)],
        [rows_f32, rows_low, rows_low, shape((clip_count, 1, patch_count), jnp.int32)],
        cost=(2 * clip_count * length * patch_count * width, 20_000_000),
    )(kept, order, gate(freq), keep_time[:, None, :], patches, cotangent, norms)

    packs, mixes, totals, lows, out_lows = [], [], [], [], []

    attend_outs = [
        shape((clip_count, packed_width, length), BF16),
        shape((clip_count, local, length), BF16),
        shape((clip_count, heads, length), F32),
        rows_f32,
    ]
    low_outs = [shape((packed_width, width), BF16), shape((local, width), BF16)]
    low_specs = [whole_block(packed_width, width), whole_block(local, width)]
    attend_cost = (18_000_000_000, 25_000_000)

    def attend_own():
        def specs(clip):
            return [
                fixed_block(clip, packed_width, length),
                fixed_block(clip, local, length),
                fixed_block(clip, heads, length),
                fixed_block(clip, length, width),
            ]

        results = call(
            functools.partial(attend_kernel, "own", 0, heads),
            (1,),
            [fixed_block(0, length, width)] * 2 + low_specs,
            specs(0) + low_specs,
            attend_outs + low_outs,
            cost=attend_cost,
        )(kept, order, gate(first), inputs, qkv_rows, w_out)
        yield results
        for clip in range(1, clip_count):
            *arrays, low, out_low = results
            arrays = call(
                functools.partial(attend_kernel, "rest", clip, heads),
                (1,),
                [fixed_block(clip, length, width)] * 2 + low_specs + [ANY] * 4,
                specs(clip),
                attend_outs,
                aliases={6 + index: index for index in range(4)},
                cost=attend_cost,
            )(kept, order, gate(first), inputs, low, out_low, *arrays)
            results = [*arrays, low, out_low]
            yield results

    def attend(before, pieces):
        return call(
            functools.partial(attend_kernel, "gathered", None, heads),
            grid,
            [row(width), row(width)] + [ANY] * SOURCES,
            [
                clip_block(packed_width, length),
                clip_block(local, length),
                clip_block(heads, length),
                row(width),
            ]
            + low_specs,
            attend_outs + low_outs,
            scratch=(
                pltpu.VMEM((packed_width, width), F32),
                pltpu.VMEM((local, width), F32),
                pltpu.SemaphoreType.DMA((2, GROUP)),
            ),
            aliases={3: 3},
            cost=attend_cost,
        )(kept, order, gate(first), before, *pieces)

    def keep(results):
        packed, mixed, total, after, low, out_low = results
        packs.append(packed)
        mixes.append(mixed)
        totals.append(total)
        lows.append(low)
        out_lows.append(out_low)
        return after

    early[s1] = hop(early[s1], first)
    late[s1] = [move(tie(late_piece, first), s1, True)]
    halves = attend_own()
    results = next(halves)
    early[s1] = hop(early[s1], results[0])
    early[s2] = hop(early[s2], results[0])
    early[s3] = hop(early[s3], results[0])
    late[s2] = [move(tie(late_piece, results[0]), s2, True)]
    for results in halves:
        pass
    middle = keep(results)
    early[s2] = hop(early[s2], middle)
    early[s3] = hop(early[s3], middle)
    late[s1] = hop(late[s1], middle)
    middle = keep(attend(middle, early[s1]))
    early[s3] = hop(early[s3], middle)
    late[s1] = hop(late[s1], middle)
    half_rows = late_piece.shape[0] // 2
    late_up = move(tie(late_piece[:half_rows], middle), s3)
    middle = keep(attend(middle, early[s2]))
    late[s1] = hop(late[s1], middle)
    late[s2] = hop(late[s2], middle)
    late_down = move(tie(late_piece[half_rows:], middle), s3)
    middle = keep(attend(middle, early[s3]))
    late[s2] = hop(late[s2], middle)
    late[s3] = hop([jnp.concatenate([tie(late_up, middle), late_down])], middle)

    mlp_scratch = (pltpu.VMEM((width, hidden), BF16), pltpu.VMEM((hidden, width), BF16))
    stage_scratch = (
        pltpu.VMEM((2, width, hidden), F32),
        pltpu.SemaphoreType.DMA((2, GROUP)),
    )
    chunk = 256
    half_parts = shape((GROUP // 2, width // GROUP, 2 * hidden), F32)
    second, branch, back, mlp_keep, mlp_send = call(
        functools.partial(mlp_own_kernel, chunk),
        grid,
        [row(width), row(width), whole_block(4, width)]
        + [whole_block(width, hidden), whole_block(hidden, width)],
        [row(width)] * 3 + [ANY, ANY],
        [rows_low, rows_f32, rows_f32, half_parts, half_parts],
        scratch=mlp_scratch
        + (pltpu.VMEM((width, 2 * hidden), F32), pltpu.SemaphoreType.DMA((GROUP,))),
        cost=(12_000_000_000, 30_000_000),
    )(kept, order, gate(middle), grad, norms, w_up, w_down)

    late[s2] = hop(late[s2], second)
    late[s3] = hop(late[s3], second)
    mlp_got = ex(mlp_send, 1)

    def mlp(branch, back, pieces):
        return call(
            functools.partial(mlp_kernel, chunk),
            grid,
            [row(width)] * 4 + [ANY] * SOURCES,
            [row(width), row(width)],
            [rows_f32, rows_f32],
            scratch=mlp_scratch + stage_scratch,
            aliases={4: 0, 5: 1},
            cost=(9_000_000_000, 25_000_000),
        )(kept, order, gate(second), grad, branch, back, *pieces)

    branch, back = mlp(branch, back, late[s1])
    late[s3] = hop(late[s3], branch)
    mlp_sum = mlp_keep + mlp_got
    mlp_got = ex(tie(mlp_sum[2:], branch), 4)
    branch, back = mlp(branch, back, late[s2])
    mlp_sum = mlp_sum[:2] + mlp_got
    mlp_got = ex(tie(mlp_sum[1], branch), 2)
    block_out, grad_middle, middle_low, norm_grad2 = call(
        functools.partial(mlp_last_kernel, chunk),
        grid,
        [row(width)] * 4 + [ANY] * SOURCES + [row(width), whole_block(4, width)],
        [row(width)] * 3 + [whole_block(2, width)],
        [rows_low, rows_f32, rows_low, shape((2, width), F32)],
        scratch=mlp_scratch + stage_scratch,
        cost=(9_000_000_000, 25_000_000),
    )(kept, order, gate(second), grad, branch, back, *late[s3], middle, norms)
    mlp_sum = sum_rest(mlp_sum[0] + tie(mlp_got, middle_low), clips, shards, clip_index)

    half_parts = shape((GROUP // 2, width // GROUP, packed_width + local), F32)

    def attend_back(index, before):
        own = index == 0
        return call(
            functools.partial(attend_back_kernel, own, heads),
            grid,
            [
                clip_block(packed_width, length),
                clip_block(local, length),
                clip_block(heads, length),
                row(width),
                whole_block(packed_width, width),
                whole_block(local, width),
                row(width),
            ],
            [clip_block(packed_width, length), row(width), ANY, ANY] if own else row(width),
            [shape((clip_count, packed_width, length), BF16), rows_f32, half_parts, half_parts]
            if own
            else rows_f32,
            scratch=(
                pltpu.VMEM((width, packed_width + local), F32),
                pltpu.SemaphoreType.DMA((GROUP,)),
            )
            if own
            else (pltpu.VMEM((1, packed_width, length), BF16),),
            aliases={} if own else {8: 0},
            cost=(14_000_000_000, 14_000_000),
        )(
            kept,
            order,
            packs[index],
            mixes[index],
            totals[index],
            gate(middle_low),
            lows[index],
            out_lows[index],
            first if own else before,
        )

    own_rows = width // clips

    def moments(gradient, layout, firsts, seconds):
        count = len(layout)
        specs = [whole_block(*array.shape) for array in (*firsts, *seconds)]
        results = call(
            functools.partial(moments_kernel, layout),
            (1,),
            [whole_block(*gradient.shape)] + specs,
            [whole_block(*gradient.shape)] + specs,
            [shape(array.shape, F32) for array in (gradient, *firsts, *seconds)],
            cost=(1_000_000, 5_000_000),
        )(kept, order, gradient, *firsts, *seconds)
        return results[0], results[1 : count + 1], results[count + 1 :]

    def assemble(pieces, weights, layout, done):
        total = sum(entry[0] for entry in layout)
        return call(
            functools.partial(assemble_kernel, layout),
            (1,),
            [ANY] * SOURCES + [whole_block(*weight.shape) for weight in weights],
            [whole_block(*weight.shape) for weight in weights for _ in range(2)],
            [shape(weight.shape, kind) for weight in weights for kind in (F32, BF16)],
            scratch=(pltpu.VMEM((width, total), F32), pltpu.SemaphoreType.DMA((GROUP,))),
            cost=(1_000_000, 15_000_000),
        )(kept, order, gate(tie(pieces[0], done)), *pieces[1:], *weights)

    norm_moments = jnp.zeros((8, width), F32)
    norm_moments = lax.dynamic_update_slice(
        norm_moments, jnp.concatenate([m_norms, v_norms]), (0, clip_index * own_rows)
    )

    rate_model = D ** (-0.5)
    mlp_dir, (mom1_up, mom1_down), (mom2_up, mom2_down) = moments(
        mlp_sum,
        ((hidden, "plain"), (hidden, "plain")),
        (m_up, m_down.T),
        (v_up, v_down.T),
    )
    mlp_part = gather_rest(mlp_dir, clips, shards, clip_index)
    mlp_other = ex(mlp_part, 2)
    _, grad_first, att_keep, att_send = attend_back(0, None)
    att_got = ex(att_send, 1)
    mlp_pair = jnp.stack([mlp_part, mlp_other])
    mlp_other = ex(tie(mlp_pair, grad_first), 4)
    norm_moments = norm_moments + swap(tie(norm_moments, grad_first), 1)
    grad_first = attend_back(1, grad_first)
    att_sum = att_keep + att_got
    att_got = ex(tie(att_sum[2:], grad_first), 4)
    mlp_pieces = hop([mlp_pair, mlp_other], grad_first)
    norm_moments = norm_moments + swap(tie(norm_moments, grad_first), 2)
    grad_first = attend_back(2, grad_first)
    mask = 4
    while mask < clips:
        norm_moments = norm_moments + swap(tie(norm_moments, grad_first), mask)
        mask *= 2
    att_sum = att_sum[:2] + att_got
    att_got = ex(tie(att_sum[1], grad_first), 2)
    grad_first = attend_back(3, grad_first)
    att_sum = sum_rest(att_sum[0] + tie(att_got, grad_first), clips, shards, clip_index)
    att_dir, (mom1_qkv, mom1_out), (mom2_qkv, mom2_out) = moments(
        att_sum,
        ((local, "stack"), (local, "turned")),
        (jnp.transpose(m_qkv, (1, 0, 2)), m_out),
        (jnp.transpose(v_qkv, (1, 0, 2)), v_out),
    )
    att_part = gather_rest(att_dir, clips, shards, clip_index)
    att_other = ex(att_part, 2)
    inputs_low, norm_grad1 = call(
        final_kernel,
        grid,
        [row(width), row(width), whole_block(4, width), row(width)],
        [row(width), whole_block(2, width)],
        [rows_low, shape((2, width), F32)],
        cost=(10_000_000, 20_000_000),
    )(kept, order, gate(tie(inputs, att_part)), grad_middle, norms, grad_first)

    att_pair = jnp.stack([att_part, att_other])
    att_other = ex(tie(att_pair, norm_grad1), 4)
    norm_sum = jnp.concatenate([norm_grad1, norm_grad2])
    norm_got = swap(norm_sum, 1)

    flat_rows = patch_count * (width // 128) * clip_count
    patch_flat = call(
        unselect_kernel,
        (1,),
        [whole_block(clip_count, 1, patch_count), whole_block(clip_count, length, width)],
        whole_block(flat_rows, 128),
        shape((flat_rows, 128), F32),
        cost=(5_000_000_000, 20_000_000),
    )(kept, order, placed, gate(inputs_low))
    patch_grad = (
        patch_flat.reshape(patch_count, width // 128, clip_count, 128)
        .transpose(0, 2, 1, 3)
        .reshape(patch_count, clip_count, width)
        .transpose(1, 0, 2)
    )
    att_pieces = hop([att_pair, att_other], patch_flat)
    norm_sum = norm_sum + tie(norm_got, patch_flat)
    norm_got = swap(norm_sum, 2)
    full_up, low_up, full_down, low_down = assemble(
        mlp_pieces,
        (w_up, w_down),
        ((hidden, False, rate_model), (hidden, True, FF ** (-0.5))),
        norm_sum,
    )
    norm_sum = norm_sum + tie(norm_got, full_up)
    mask = 4
    while mask < clips:
        norm_got = swap(norm_sum, mask)
        if mask == 4:
            qkv_full, qkv_low, full_out, low_out = assemble(
                att_pieces,
                (qkv_rows, w_out),
                (
                    (packed_width, True, rate_model),
                    (local, True, max(16 * D // BLOCK, 1) ** (-0.5)),
                ),
                norm_sum,
            )
            norm_got = tie(norm_got, qkv_full)
        norm_sum = norm_sum + norm_got
        mask *= 2

    def unrow(array):
        return jnp.transpose(array.reshape(3, local, width), (2, 0, 1))

    def norm_piece(array):
        return own_part(array, 1, clip_index, clips)

    norm_dir, mom1_norms, mom2_norms = adam_direction(norm_sum, norm_moments[:4], norm_moments[4:])
    full_norms = norms - 0.3 * (norm_dir + 0.01 * norms)

    return (
        block_out,
        patch_grad,
        norm_piece(norm_sum),
        unrow(qkv_full),
        full_out,
        full_up,
        full_down,
        full_norms,
        jnp.transpose(mom1_qkv, (1, 0, 2)),
        mom1_out,
        mom1_up,
        mom1_down.T,
        norm_piece(mom1_norms),
        jnp.transpose(mom2_qkv, (1, 0, 2)),
        mom2_out,
        mom2_up,
        mom2_down.T,
        norm_piece(mom2_norms),
        unrow(qkv_low),
        low_out,
        low_up,
        low_down,
    )


def solution(mesh):
    return jax.shard_map(
        on_device,
        mesh=mesh,
        in_specs=(
            P("clip", None, None),
            P("clip", None),
            P("clip", None),
            P("clip", None, None),
            P(None, None, "tp"),
            P("tp", None),
            P(None, "tp"),
            P("tp", None),
            P(),
            P("clip", None, "tp"),
            P("clip", None, "tp"),
            P("tp", "clip"),
            P("tp", "clip"),
            P("clip", "tp"),
            P("clip", "tp"),
            P("tp", "clip"),
            P("tp", "clip"),
            P(None, "clip"),
            P(None, "clip"),
        ),
        out_specs=(
            P("clip", None, None),
            P("clip", None, None),
            P(None, "clip"),
            P(None, None, "tp"),
            P("tp", None),
            P(None, "tp"),
            P("tp", None),
            P(),
            P("clip", None, "tp"),
            P("tp", "clip"),
            P("clip", "tp"),
            P("tp", "clip"),
            P(None, "clip"),
            P("clip", None, "tp"),
            P("tp", "clip"),
            P("clip", "tp"),
            P("tp", "clip"),
            P(None, "clip"),
            P(None, None, "tp"),
            P("tp", None),
            P(None, "tp"),
            P("tp", None),
        ),
        check_vma=False,
    )
```

```python
import functools

import jax
import jax.numpy as jnp
from jax import lax
from jax.experimental import pallas as pl
from jax.experimental.pallas import tpu as pltpu
from jax.sharding import PartitionSpec as P

D = 768
HD = 64
FF = 3072
BLOCK = 704
STEP = 3
EPSILON = 1e-06
SCALE = HD ** (-0.5)
GROUP = 8
SOURCES = GROUP // 2
F32 = jnp.float32
BF16 = jnp.bfloat16
VMEM_LIMIT = 18 * 2**20
COST_PART = 10


def dot(left, right, left_dim, right_dim):
    return lax.dot_general(
        left, right, (((left_dim,), (right_dim,)), ((), ())), preferred_element_type=F32
    )


def positions(keep_freq, keep_time):
    bins, frames = keep_freq.shape[1], keep_time.shape[1]
    count = bins * frames
    patch = lax.broadcasted_iota(jnp.int32, (1, count), 1)
    patch_bin = jnp.zeros((1, count), jnp.int32)
    for index in range(1, bins):
        patch_bin += (patch >= index * frames).astype(jnp.int32)
    patch_frame = patch - patch_bin * frames

    def spread(index, size):
        return jnp.where(
            lax.broadcasted_iota(jnp.int32, (size, count), 0) == index, 1.0, 0.0
        ).astype(BF16)

    def before(size):
        row = lax.broadcasted_iota(jnp.int32, (size, size), 0)
        column = lax.broadcasted_iota(jnp.int32, (size, size), 1)
        return jnp.where(row < column, 1.0, 0.0).astype(BF16)

    freq, time = keep_freq.astype(F32).astype(BF16), keep_time.astype(F32).astype(BF16)
    rank_freq = dot(freq, before(bins), 1, 0).astype(BF16)
    rank_time = dot(time, before(frames), 1, 0).astype(BF16)
    by_bin, by_frame = spread(patch_bin, bins), spread(patch_frame, frames)
    time_count = jnp.sum(keep_time.astype(F32), axis=1, keepdims=True)
    placed = dot(rank_freq, by_bin, 1, 0) * time_count + dot(rank_time, by_frame, 1, 0)
    present = dot(freq, by_bin, 1, 0) * dot(time, by_frame, 1, 0)
    return jnp.where(present > 0.5, placed, -1.0).astype(jnp.int32)


def norm_parts(values):
    centre = values - jnp.mean(values, axis=-1, keepdims=True)
    spread = jnp.mean(centre * centre, axis=-1, keepdims=True)
    inverse = lax.rsqrt(spread + EPSILON)
    return centre * inverse, inverse


def norm_back(values, gain, grad):
    unit, inverse = norm_parts(values)
    grad_unit = grad * gain
    mean_grad = jnp.mean(grad_unit, axis=-1, keepdims=True)
    mean_both = jnp.mean(grad_unit * unit, axis=-1, keepdims=True)
    back = inverse * (grad_unit - mean_grad - unit * mean_both)
    gain_grad = jnp.sum(grad * unit, axis=0, keepdims=True)
    shift_grad = jnp.sum(grad, axis=0, keepdims=True)
    return back, gain_grad, shift_grad


def live_column(kept, length):
    return lax.broadcasted_iota(jnp.int32, (length, 1), 0) < kept


def tree_sum(parts, odd):
    if len(parts) != 4:
        total = parts[0]
        for part in parts[1:]:
            total = total + part
        return total
    own, after, across, before = parts
    near = jnp.where(odd, before, after)
    far = jnp.where(odd, after, before)
    return (own + near) + (across + far)


def plain_call(body, grid, in_specs, out_specs, out_shape, scratch=(), aliases=None, cost=None, limit=None):
    at = 2 + len(in_specs)

    def with_token(*refs):
        refs[at][...] = jnp.zeros_like(refs[at])
        body(*refs[:at], *refs[at + 1 :])

    return pl.pallas_call(
        with_token,
        grid_spec=pltpu.PrefetchScalarGridSpec(
            num_scalar_prefetch=2,
            grid=grid,
            in_specs=in_specs,
            out_specs=[whole_block(8, 128), *out_specs],
            scratch_shapes=list(scratch),
        ),
        out_shape=[jax.ShapeDtypeStruct((8, 128), F32), *out_shape],
        input_output_aliases={key: value + 1 for key, value in (aliases or {}).items()},
        compiler_params=pltpu.CompilerParams(
            dimension_semantics=("arbitrary",) * len(grid), vmem_limit_bytes=limit or VMEM_LIMIT
        ),
        cost_estimate=pl.CostEstimate(
            flops=cost[0] * COST_PART, bytes_accessed=cost[1] * COST_PART, transcendentals=0
        ),
    )


def clip_block(*dims):
    return pl.BlockSpec((1, *dims), lambda c, *_: (c,) + (0,) * len(dims))


def whole_block(*dims):
    return pl.BlockSpec(dims, lambda *_: (0,) * len(dims))


ANY = pl.BlockSpec(memory_space=pl.ANY)


def front_kernel(kept, order, freq, time, patches, cot, norms, inputs, first, grad, placed):
    clip = pl.program_id(0)
    placed[0] = positions(freq[0], time[0])
    length, patch_count = first.shape[1], placed.shape[2]
    slots = lax.broadcasted_iota(jnp.int32, (length, patch_count), 0)
    select = jnp.where(placed[0] == slots, 1.0, 0.0).astype(BF16)
    picked = dot(select, patches[0], 1, 0)
    inputs[0] = picked
    unit, _ = norm_parts(picked)
    first[0] = (unit * norms[0:1] + norms[1:2]).astype(BF16)
    live = live_column(kept[clip], length)
    grad[0] = jnp.where(live, cot[0].astype(F32), 0.0).astype(BF16)


def pieces_kernel(kept, order, *refs):
    *sources, early, late, sems = refs
    copies = []
    for target, pair in ((early, sources[:2]), (late, sources[2:])):
        start = 0
        for source in pair:
            rows = source.shape[0] // GROUP
            place = pl.multiple_of(order[2 * GROUP] * rows, 8)
            copies.append(
                pltpu.make_async_copy(
                    source.at[pl.ds(place, rows)],
                    target.at[pl.ds(start, rows)],
                    sems.at[len(copies)],
                )
            )
            start += rows
    for copy in copies:
        copy.start()
    for copy in copies:
        copy.wait()


def piece_copies(order, sources, start, rows, target, sems):
    copies = []
    for slot in range(GROUP):
        source = sources[slot // 2].at[slot % 2, pl.ds(start, rows)]
        place = pl.multiple_of(order[slot] * rows, 8)
        copies.append(
            pltpu.make_async_copy(source, target.at[pl.ds(place, rows)], sems.at[slot])
        )
    return copies


def augment(rows, extra_row, length):
    index = lax.broadcasted_iota(jnp.int32, (16, length), 0)
    extra = jnp.where(index == 0, extra_row, 0.0).astype(BF16)
    return jnp.concatenate([rows, extra], axis=0)


def key_bias(kept, length):
    slot = lax.broadcasted_iota(jnp.int32, (1, length), 1)
    return jnp.where(slot < kept, 0.0, -1000000000.0)


def attend_kernel(mode, fixed, heads, kept, order, first, before, *refs):
    clip = pl.program_id(0) if fixed is None else fixed
    if mode == "own":
        source, out_source, packed, mixed, total, after, low, out_low = refs
        low[...] = source[...].astype(BF16)
        out_low[...] = out_source[...].astype(BF16)
    elif mode == "gathered":
        sources, (packed, mixed, total, after, low, out_low) = refs[:SOURCES], refs[SOURCES:-3]
        staged, out_staged, sems = refs[-3:]

        @pl.when(clip == 0)
        def _():
            rows, out_rows = low.shape[0] // GROUP, out_low.shape[0] // GROUP
            copies = piece_copies(order, sources, 0, rows, staged, sems.at[0])
            copies += piece_copies(order, sources, rows, out_rows, out_staged, sems.at[1])
            for copy in copies:
                copy.start()
            for copy in copies:
                copy.wait()
            low[...] = staged[...].astype(BF16)
            out_low[...] = out_staged[...].astype(BF16)
    else:
        low, out_low, _, _, _, _, packed, mixed, total, after = refs

    length = first.shape[1]
    width = heads * HD
    rows = dot(low[...], first[0], 1, 1).astype(BF16)
    packed[0] = rows
    bias = key_bias(kept[clip], length)
    ones = jnp.ones((1, length), F32)
    for head in range(heads):
        at = head * HD
        query = augment((rows[at : at + HD] * SCALE).astype(BF16), ones, length)
        key = augment(rows[width + at : width + at + HD], bias, length)
        value = rows[2 * width + at : 2 * width + at + HD]
        scores = dot(key, query, 0, 0)
        largest = jnp.max(scores, axis=0, keepdims=True)
        exponent = jnp.exp(scores - largest)
        summed = jnp.sum(exponent, axis=0, keepdims=True)
        mix = dot(value, exponent.astype(BF16), 1, 0) / summed
        mixed[0, at : at + HD] = mix.astype(BF16)
        total[0, head : head + 1] = largest + jnp.log(summed)
    after[0] = before[0] + dot(mixed[0], out_low[...], 0, 0)


HALF_ROOT = 0.7071067811865476
DENSITY = 0.3989422804014327


def load_mlp(order, sources, up_low, down_low, staged, sems):
    rows = up_low.shape[0] // GROUP
    copies = []
    for index in range(2):
        copies += piece_copies(
            order, sources, index * rows, rows, staged.at[index], sems.at[index]
        )
    for copy in copies:
        copy.start()
    for copy in copies:
        copy.wait()
    up_low[...] = staged[0].astype(BF16)
    down_low[...] = staged[1].astype(BF16)


def mlp_rows(rows, upstream, up_low, down_low, chunk, grads=None):
    branch_sum = back_sum = None
    for start in range(0, up_low.shape[1], chunk):
        up = up_low[:, start : start + chunk]
        down = down_low[start : start + chunk]
        hidden = dot(rows, up, 1, 0)
        grad_active = dot(upstream, down, 1, 1)
        cumulative = 0.5 * (lax.erf(hidden * HALF_ROOT) + 1.0)
        active = (hidden * cumulative).astype(BF16)
        slope = cumulative + hidden * (DENSITY * jnp.exp(-0.5 * hidden * hidden))
        grad_hidden = (slope * grad_active).astype(BF16)
        branch_part = dot(active, down, 1, 0)
        back_part = dot(grad_hidden, up, 1, 1)
        branch_sum = branch_part if branch_sum is None else branch_sum + branch_part
        back_sum = back_part if back_sum is None else back_sum + back_part
        if grads is not None:
            width = up_low.shape[1]
            grads[:, start : start + chunk] += dot(rows, grad_hidden, 0, 0)
            grads[:, width + start : width + start + chunk] += dot(upstream, active, 0, 0)
    return branch_sum, back_sum


def part_copies(order, source, keep, send, sems):
    rows = keep.shape[1]
    copies = []
    for slot in range(GROUP):
        target = (keep if slot < GROUP // 2 else send).at[slot % (GROUP // 2)]
        place = pl.multiple_of(order[GROUP + slot] * rows, 8)
        copies.append(pltpu.make_async_copy(source.at[pl.ds(place, rows)], target, sems.at[slot]))
    return copies


def mlp_own_kernel(chunk, kept, order, middle, grad, norms, up_source, down_source, *refs):
    second, branch, back, keep, send, up_low, down_low, grads, sems = refs
    clip = pl.program_id(0)

    @pl.when(clip == 0)
    def _():
        up_low[...] = up_source[...].astype(BF16)
        down_low[...] = down_source[...].astype(BF16)
        grads[...] = jnp.zeros_like(grads)

    values = middle[0]
    unit, _ = norm_parts(values)
    second[0] = (unit * norms[2:3] + norms[3:4]).astype(BF16)
    branch_part, back_part = mlp_rows(second[0], grad[0], up_low, down_low, chunk, grads)
    branch[0] = values + branch_part
    back[0] = back_part

    @pl.when(clip == pl.num_programs(0) - 1)
    def _():
        copies = part_copies(order, grads, keep, send, sems)
        for copy in copies:
            copy.start()
        for copy in copies:
            copy.wait()


def mlp_kernel(chunk, kept, order, second, grad, branch_in, back_in, *refs):
    sources = refs[:SOURCES]
    branch, back, up_low, down_low, staged, sems = refs[SOURCES:]
    clip = pl.program_id(0)

    @pl.when(clip == 0)
    def _():
        load_mlp(order, sources, up_low, down_low, staged, sems)

    branch_part, back_part = mlp_rows(second[0], grad[0], up_low, down_low, chunk)
    branch[0] = branch_in[0] + branch_part
    back[0] = back_in[0] + back_part


def mlp_last_kernel(chunk, kept, order, second, grad, branch_in, back_in, *refs):
    sources = refs[:SOURCES]
    middle, norms, result, grad_middle, low, norm_grad = refs[SOURCES : SOURCES + 6]
    up_low, down_low, staged, sems = refs[SOURCES + 6 :]
    clip = pl.program_id(0)

    @pl.when(clip == 0)
    def _():
        load_mlp(order, sources, up_low, down_low, staged, sems)
        norm_grad[...] = jnp.zeros_like(norm_grad)

    branch_part, back_part = mlp_rows(second[0], grad[0], up_low, down_low, chunk)
    live = live_column(kept[clip], middle.shape[1])
    result[0] = jnp.where(live, branch_in[0] + branch_part, 0.0).astype(BF16)
    back, gain_grad, shift_grad = norm_back(middle[0], norms[2:3], back_in[0] + back_part)
    both = grad[0].astype(F32) + back
    grad_middle[0] = both
    low[0] = both.astype(BF16)
    norm_grad[0:1] += gain_grad
    norm_grad[1:2] += shift_grad


def attend_back_kernel(own, heads, kept, order, packed, mixed, total, grad, low, out_low, *refs):
    clip = pl.program_id(0)
    if own:
        first, grad_packed, after, keep, send, grads, sems = refs
    else:
        before, after, grad_packed = refs
    length = grad.shape[1]
    width = heads * HD
    grad_mixed = dot(out_low[...], grad[0], 1, 1).astype(BF16)
    bias = key_bias(kept[clip], length)
    ones = jnp.ones((1, length), F32)
    for head in range(heads):
        at = head * HD
        query_low = (packed[0, at : at + HD] * SCALE).astype(BF16)
        key_low = packed[0, width + at : width + at + HD]
        value = packed[0, 2 * width + at : 2 * width + at + HD]
        query = augment(query_low, ones, length)
        key = augment(key_low, bias, length)
        upstream = grad_mixed[at : at + HD]
        offset = jnp.sum(
            upstream.astype(F32) * mixed[0, at : at + HD].astype(F32), axis=0, keepdims=True
        )
        probs = jnp.exp(dot(key, query, 0, 0) - total[0, head : head + 1])
        grad_probs = dot(value, upstream, 0, 0)
        scores_low = (probs * (grad_probs - offset)).astype(BF16)
        probs_low = probs.astype(BF16)
        grad_packed[0, at : at + HD] = (dot(key_low, scores_low, 1, 0) * SCALE).astype(BF16)
        grad_packed[0, width + at : width + at + HD] = dot(query_low, scores_low, 1, 1).astype(BF16)
        grad_packed[0, 2 * width + at : 2 * width + at + HD] = dot(
            upstream, probs_low, 1, 1
        ).astype(BF16)
    back = dot(grad_packed[0], low[...], 0, 0)
    if own:
        after[0] = back

        @pl.when(clip == 0)
        def _():
            grads[...] = jnp.zeros_like(grads)

        grads[:, : 3 * width] += dot(first[0], grad_packed[0], 0, 1)
        grads[:, 3 * width :] += dot(grad[0], mixed[0], 0, 1)

        @pl.when(clip == pl.num_programs(0) - 1)
        def _():
            copies = part_copies(order, grads, keep, send, sems)
            for copy in copies:
                copy.start()
            for copy in copies:
                copy.wait()
    else:
        after[0] = before[0] + back


def final_kernel(kept, order, inputs, grad_middle, norms, grad_first, low, norm_grad):
    clip = pl.program_id(0)
    back, gain_grad, shift_grad = norm_back(inputs[0], norms[0:1], grad_first[0])
    low[0] = (grad_middle[0] + back).astype(BF16)

    @pl.when(clip == 0)
    def _():
        norm_grad[...] = jnp.zeros_like(norm_grad)

    norm_grad[0:1] += gain_grad
    norm_grad[1:2] += shift_grad


def unselect_kernel(kept, order, placed, low, patch_grad):
    clip_count, length, width = low.shape
    patch_count = placed.shape[2]
    lanes = 128
    tiles = width // lanes
    slots = lax.broadcasted_iota(jnp.int32, (length, patch_count), 0)
    for clip in range(clip_count):
        select = jnp.where(placed[clip] == slots, 1.0, 0.0).astype(BF16)
        back = dot(select, low[clip], 0, 0)
        for tile in range(tiles):
            rows = pl.ds(tile * clip_count + clip, patch_count, stride=tiles * clip_count)
            patch_grad[rows, :] = back[:, tile * lanes : (tile + 1) * lanes]


def adam_direction(gradient, first_mom, second_mom):
    first_new = 0.5 * first_mom + 0.5 * gradient
    second_new = 0.5 * second_mom + 0.5 * gradient * gradient
    fix = 1.0 - 0.5**STEP
    direction = first_new / fix / (jnp.sqrt(second_new / fix) + 1e-08)
    return direction, first_new, second_new


def moments_kernel(layout, kept, order, gradient, *refs):
    count = len(layout)
    firsts, seconds = refs[:count], refs[count : 2 * count]
    direction, first_outs, second_outs = (
        refs[2 * count],
        refs[2 * count + 1 : 3 * count + 1],
        refs[3 * count + 1 :],
    )
    start = 0
    for index, (wide, form) in enumerate(layout):
        parts = 3 if form == "stack" else 1
        for part in range(parts):
            columns = slice(start, start + wide)
            grad = gradient[:, columns]
            if form == "turned":
                first, second = firsts[index][...].T, seconds[index][...].T
            elif form == "stack":
                first, second = firsts[index][part], seconds[index][part]
            else:
                first, second = firsts[index][...], seconds[index][...]
            step, first, second = adam_direction(grad, first, second)
            direction[:, columns] = step
            if form == "turned":
                first_outs[index][...], second_outs[index][...] = first.T, second.T
            elif form == "stack":
                first_outs[index][part], second_outs[index][part] = first, second
            else:
                first_outs[index][...], second_outs[index][...] = first, second
            start += wide


def assemble_kernel(layout, kept, order, *refs):
    count = len(layout)
    sources, refs = refs[:SOURCES], refs[SOURCES:]
    weights, outs = refs[:count], refs[count : 3 * count]
    staged, sems = refs[3 * count :]
    copies = piece_copies(order, sources, 0, sources[0].shape[1], staged, sems)
    for copy in copies:
        copy.start()
    for copy in copies:
        copy.wait()
    start = 0
    for index, (wide, turned, rate) in enumerate(layout):
        step = staged[:, start : start + wide]
        if turned:
            step = step.T
        weight = weights[index][...]
        values = weight - rate * (step + 0.01 * weight)
        outs[2 * index][...] = values
        outs[2 * index + 1][...] = values.astype(BF16)
        start += wide


def swap_bits(code):
    return code & 1 | (code >> 2 & 1) << 1 | (code >> 1 & 1) << 2


def members(clips):
    return clips // GROUP


def exchange(array, code, clips, shards):
    step = members(clips)
    pairs = []
    for clip in range(clips):
        member, rest = divmod(clip, step)
        other = member ^ (swap_bits(code) if member & 1 else code)
        for shard in range(shards):
            pairs.append((clip * shards + shard, (other * step + rest) * shards + shard))
    return lax.ppermute(array, ("clip", "tp"), pairs)


def swap_rest(array, mask, clips, shards):
    pairs = [
        (clip * shards + shard, (clip ^ mask) * shards + shard)
        for clip in range(clips)
        for shard in range(shards)
    ]
    return lax.ppermute(array, ("clip", "tp"), pairs)


def shift(array, step, clips, shards):
    pairs = [
        (clip * shards + (shard + step) % shards, clip * shards + shard)
        for clip in range(clips)
        for shard in range(shards)
    ]
    return lax.ppermute(array, ("clip", "tp"), pairs)


def tie(array, *others):
    return lax.optimization_barrier((array, *others))[0]


def piece_order(member):
    odd = member & 1

    def place(base, parity, code):
        return base ^ jnp.where(parity == 1, swap_bits(code), code)

    near = [place(member, odd, code) for code in (0, 2, 4, 6)]
    far = [place(member ^ 1, 1 - odd, code) for code in (0, 2, 4, 6)]
    return near + far


def grad_order(member):
    odd = member & 1

    def place(code):
        return member ^ jnp.where(odd == 1, swap_bits(code), code)

    return [place(code) for code in (0, 2, 4, 6)] + [place(code) for code in (1, 5, 3, 7)]


def sum_rest(part, clips, shards, clip_index):
    step = members(clips)
    rest = clip_index % step
    half = step // 2
    while half:
        low, high = jnp.split(part, 2)
        upper = (rest & half) > 0
        got = swap_rest(jnp.where(upper, low, high), half, clips, shards)
        part = jnp.where(upper, high, low) + got
        half //= 2
    return part


def gather_rest(part, clips, shards, clip_index):
    step = members(clips)
    rest = clip_index % step
    half = 1
    while half < step:
        got = swap_rest(part, half, clips, shards)
        upper = (rest & half) > 0
        part = jnp.concatenate([jnp.where(upper, got, part), jnp.where(upper, part, got)])
        half *= 2
    return part


def sum_all(array, clips, shards):
    mask = 1
    while mask < clips:
        array = array + swap_rest(array, mask, clips, shards)
        mask *= 2
    return array


def own_part(array, axis_dim, clip_index, parts):
    part_width = array.shape[axis_dim] // parts
    return lax.dynamic_slice_in_dim(array, clip_index * part_width, part_width, axis_dim)


def on_device(
    patches,
    keep_freq,
    keep_time,
    cotangent,
    w_qkv,
    w_out,
    w_up,
    w_down,
    norms,
    m_qkv,
    v_qkv,
    m_out,
    v_out,
    m_up,
    v_up,
    m_down,
    v_down,
    m_norms,
    v_norms,
):
    clip_count, length, width = cotangent.shape
    patch_count = patches.shape[1]
    clips, shards = lax.axis_size("clip"), lax.axis_size("tp")
    clip_index, shard_index = lax.axis_index("clip"), lax.axis_index("tp")
    local = w_qkv.shape[2]
    heads = local // HD
    hidden = w_up.shape[1]
    packed_width = 3 * local
    member = clip_index % GROUP

    group = members(clips)
    member = clip_index // group
    waiting, started, slow, tokens = [], [], [], []

    def call(*args, **kwargs):
        run = plain_call(*args, **kwargs)

        def keep_token(*operands):
            results = run(*operands)
            tokens.append(results[0])
            return results

        return keep_token


    def ex(array, code):
        started.append(exchange(array, code, clips, shards))
        return started[-1]

    def move(array, step, two_kernels=False):
        kind = slow if two_kernels else started
        kind.append(shift(array, step, clips, shards))
        return kind[-1]

    def swap(array, mask):
        started.append(swap_rest(array, mask, clips, shards))
        return started[-1]

    def gate(array):
        array = tie(array, *waiting)
        waiting[:] = started
        started[:] = slow
        slow.clear()
        return array

    shape = jax.ShapeDtypeStruct

    qkv_rows = jnp.transpose(w_qkv, (1, 2, 0)).reshape(packed_width, width)

    order = jnp.stack([*piece_order(member), *grad_order(member), member]).astype(jnp.int32)
    kept = (jnp.sum(keep_freq, axis=-1) * jnp.sum(keep_time, axis=-1)).astype(jnp.int32)
    _, early_piece, late_piece = call(
        pieces_kernel,
        (1,),
        [ANY] * 4,
        [
            whole_block((packed_width + local) // GROUP, width),
            whole_block((width + hidden) // GROUP, width),
        ],
        [
            shape(((packed_width + local) // GROUP, width), F32),
            shape(((width + hidden) // GROUP, width), F32),
        ],
        scratch=(pltpu.SemaphoreType.DMA((4,)),),
        cost=(1_000_000, 4_000_000),
        limit=56 * 2**20,
    )(kept, order, qkv_rows, w_out, w_up, w_down)
    steps = (1, 3, 2) if shards == 4 else tuple(range(1, shards))
    early = {step: [move(early_piece, step)] for step in steps[:2]}
    late = {}

    def hop(pieces, done):
        if len(pieces) == 1:
            return [*pieces, ex(tie(pieces[0], done), 2)]
        if pieces[0].ndim == 2:
            pair = jnp.stack([tie(piece, done) for piece in pieces])
            return [pair, ex(pair, 4)]
        return [*pieces, *[ex(tie(piece, done), 1) for piece in pieces]]

    row = functools.partial(clip_block, length)
    rows_f32 = shape((clip_count, length, width), F32)
    rows_low = shape((clip_count, length, width), BF16)
    grid = (clip_count,)

    def fixed_block(clip, *dims):
        return pl.BlockSpec((1, *dims), lambda *_: (clip,) + (0,) * len(dims))

    s1, s2, s3 = steps
    freq = gate(tie(keep_freq[:, None, :], early[s1][0], early[s2][0]))
    waiting.clear()
    early[s1] = hop(early[s1], freq)
    early[s2] = hop(early[s2], freq)
    early[s3] = [move(tie(early_piece, freq), s3)]
    front_done, inputs, first, grad, placed = call(
        front_kernel,
        grid,
        [
            clip_block(1, keep_freq.shape[1]),
            clip_block(1, keep_time.shape[1]),
            clip_block(patch_count, width),
            row(width),
            whole_block(4, width),
        ],
        [row(width)] * 3 + [clip_block(1, patch_count)],
        [rows_f32, rows_low, rows_low, shape((clip_count, 1, patch_count), jnp.int32)],
        cost=(2 * clip_count * length * patch_count * width, 20_000_000),
    )(kept, order, gate(freq), keep_time[:, None, :], patches, cotangent, norms)

    packs, mixes, totals, lows, out_lows = [], [], [], [], []

    attend_outs = [
        shape((clip_count, packed_width, length), BF16),
        shape((clip_count, local, length), BF16),
        shape((clip_count, heads, length), F32),
        rows_f32,
    ]
    low_outs = [shape((packed_width, width), BF16), shape((local, width), BF16)]
    low_specs = [whole_block(packed_width, width), whole_block(local, width)]
    attend_cost = (18_000_000_000, 25_000_000)

    def attend_own():
        def specs(clip):
            return [
                fixed_block(clip, packed_width, length),
                fixed_block(clip, local, length),
                fixed_block(clip, heads, length),
                fixed_block(clip, length, width),
            ]

        results = call(
            functools.partial(attend_kernel, "own", 0, heads),
            (1,),
            [fixed_block(0, length, width)] * 2 + low_specs,
            specs(0) + low_specs,
            attend_outs + low_outs,
            cost=attend_cost,
        )(kept, order, gate(first), inputs, qkv_rows, w_out)
        yield results
        for clip in range(1, clip_count):
            _, *arrays, low, out_low = results
            arrays = call(
                functools.partial(attend_kernel, "rest", clip, heads),
                (1,),
                [fixed_block(clip, length, width)] * 2 + low_specs + [ANY] * 4,
                specs(clip),
                attend_outs,
                aliases={6 + index: index for index in range(4)},
                cost=attend_cost,
            )(kept, order, gate(first), inputs, low, out_low, *arrays)
            results = [*arrays, low, out_low]
            yield results

    def attend(before, pieces):
        return call(
            functools.partial(attend_kernel, "gathered", None, heads),
            grid,
            [row(width), row(width)] + [ANY] * SOURCES,
            [
                clip_block(packed_width, length),
                clip_block(local, length),
                clip_block(heads, length),
                row(width),
            ]
            + low_specs,
            attend_outs + low_outs,
            scratch=(
                pltpu.VMEM((packed_width, width), F32),
                pltpu.VMEM((local, width), F32),
                pltpu.SemaphoreType.DMA((2, GROUP)),
            ),
            aliases={3: 3},
            cost=attend_cost,
        )(kept, order, gate(first), before, *pieces)

    def keep(results):
        done, packed, mixed, total, after, low, out_low = results
        packs.append(packed)
        mixes.append(mixed)
        totals.append(total)
        lows.append(low)
        out_lows.append(out_low)
        return after, done

    early[s1] = hop(early[s1], front_done)
    late[s1] = [move(tie(late_piece, front_done), s1, True)]
    halves = attend_own()
    results = next(halves)
    early[s1] = hop(early[s1], results[0])
    early[s2] = hop(early[s2], results[0])
    early[s3] = hop(early[s3], results[0])
    late[s2] = [move(tie(late_piece, results[0]), s2, True)]
    for results in halves:
        pass
    middle, done = keep(results)
    early[s2] = hop(early[s2], done)
    early[s3] = hop(early[s3], done)
    late[s1] = hop(late[s1], done)
    middle, done = keep(attend(middle, early[s1]))
    early[s3] = hop(early[s3], done)
    late[s1] = hop(late[s1], done)
    half_rows = late_piece.shape[0] // 2
    late_up = move(tie(late_piece[:half_rows], done), s3)
    middle, done = keep(attend(middle, early[s2]))
    late[s1] = hop(late[s1], done)
    late[s2] = hop(late[s2], done)
    late_down = move(tie(late_piece[half_rows:], done), s3)
    middle, done = keep(attend(middle, early[s3]))
    late[s2] = hop(late[s2], done)
    late[s3] = hop([jnp.concatenate([tie(late_up, done), late_down])], done)

    mlp_scratch = (pltpu.VMEM((width, hidden), BF16), pltpu.VMEM((hidden, width), BF16))
    stage_scratch = (
        pltpu.VMEM((2, width, hidden), F32),
        pltpu.SemaphoreType.DMA((2, GROUP)),
    )
    chunk = 256
    half_parts = shape((GROUP // 2, width // GROUP, 2 * hidden), F32)
    done, second, branch, back, mlp_keep, mlp_send = call(
        functools.partial(mlp_own_kernel, chunk),
        grid,
        [row(width), row(width), whole_block(4, width)]
        + [whole_block(width, hidden), whole_block(hidden, width)],
        [row(width)] * 3 + [ANY, ANY],
        [rows_low, rows_f32, rows_f32, half_parts, half_parts],
        scratch=mlp_scratch
        + (pltpu.VMEM((width, 2 * hidden), F32), pltpu.SemaphoreType.DMA((GROUP,))),
        cost=(12_000_000_000, 30_000_000),
    )(kept, order, gate(middle), grad, norms, w_up, w_down)

    late[s2] = hop(late[s2], done)
    late[s3] = hop(late[s3], done)
    mlp_got = ex(mlp_send, 1)

    def mlp(branch, back, pieces):
        return call(
            functools.partial(mlp_kernel, chunk),
            grid,
            [row(width)] * 4 + [ANY] * SOURCES,
            [row(width), row(width)],
            [rows_f32, rows_f32],
            scratch=mlp_scratch + stage_scratch,
            aliases={4: 0, 5: 1},
            cost=(9_000_000_000, 25_000_000),
        )(kept, order, gate(second), grad, branch, back, *pieces)

    done, branch, back = mlp(branch, back, late[s1])
    late[s3] = hop(late[s3], done)
    mlp_sum = mlp_keep + mlp_got
    mlp_got = ex(tie(mlp_sum[2:], done), 4)
    done, branch, back = mlp(branch, back, late[s2])
    mlp_sum = mlp_sum[:2] + mlp_got
    mlp_got = ex(tie(mlp_sum[1], done), 2)
    done, block_out, grad_middle, middle_low, norm_grad2 = call(
        functools.partial(mlp_last_kernel, chunk),
        grid,
        [row(width)] * 4 + [ANY] * SOURCES + [row(width), whole_block(4, width)],
        [row(width)] * 3 + [whole_block(2, width)],
        [rows_low, rows_f32, rows_low, shape((2, width), F32)],
        scratch=mlp_scratch + stage_scratch,
        cost=(9_000_000_000, 25_000_000),
    )(kept, order, gate(second), grad, branch, back, *late[s3], middle, norms)
    mlp_sum = sum_rest(mlp_sum[0] + tie(mlp_got, done), clips, shards, clip_index)

    half_parts = shape((GROUP // 2, width // GROUP, packed_width + local), F32)

    def attend_back(index, before):
        own = index == 0
        return call(
            functools.partial(attend_back_kernel, own, heads),
            grid,
            [
                clip_block(packed_width, length),
                clip_block(local, length),
                clip_block(heads, length),
                row(width),
                whole_block(packed_width, width),
                whole_block(local, width),
                row(width),
            ],
            [clip_block(packed_width, length), row(width), ANY, ANY] if own else [row(width)],
            [shape((clip_count, packed_width, length), BF16), rows_f32, half_parts, half_parts]
            if own
            else [rows_f32],
            scratch=(
                pltpu.VMEM((width, packed_width + local), F32),
                pltpu.SemaphoreType.DMA((GROUP,)),
            )
            if own
            else (pltpu.VMEM((1, packed_width, length), BF16),),
            aliases={} if own else {8: 0},
            cost=(14_000_000_000, 14_000_000),
        )(
            kept,
            order,
            packs[index],
            mixes[index],
            totals[index],
            gate(middle_low),
            lows[index],
            out_lows[index],
            first if own else before,
        )

    own_rows = width // clips

    def moments(gradient, layout, firsts, seconds):
        count = len(layout)
        specs = [whole_block(*array.shape) for array in (*firsts, *seconds)]
        results = call(
            functools.partial(moments_kernel, layout),
            (1,),
            [whole_block(*gradient.shape)] + specs,
            [whole_block(*gradient.shape)] + specs,
            [shape(array.shape, F32) for array in (gradient, *firsts, *seconds)],
            cost=(1_000_000, 5_000_000),
        )(kept, order, gradient, *firsts, *seconds)
        return results[1], results[2 : count + 2], results[count + 2 :]

    def assemble(pieces, weights, layout, done):
        total = sum(entry[0] for entry in layout)
        return call(
            functools.partial(assemble_kernel, layout),
            (1,),
            [ANY] * SOURCES + [whole_block(*weight.shape) for weight in weights],
            [whole_block(*weight.shape) for weight in weights for _ in range(2)],
            [shape(weight.shape, kind) for weight in weights for kind in (F32, BF16)],
            scratch=(pltpu.VMEM((width, total), F32), pltpu.SemaphoreType.DMA((GROUP,))),
            cost=(1_000_000, 15_000_000),
        )(kept, order, gate(tie(pieces[0], done)), *pieces[1:], *weights)

    norm_moments = jnp.zeros((8, width), F32)
    norm_moments = lax.dynamic_update_slice(
        norm_moments, jnp.concatenate([m_norms, v_norms]), (0, clip_index * own_rows)
    )

    rate_model = D ** (-0.5)
    mlp_dir, (mom1_up, mom1_down), (mom2_up, mom2_down) = moments(
        mlp_sum,
        ((hidden, "plain"), (hidden, "plain")),
        (m_up, m_down.T),
        (v_up, v_down.T),
    )
    mlp_part = gather_rest(mlp_dir, clips, shards, clip_index)
    mlp_other = ex(mlp_part, 2)
    done, _, grad_first, att_keep, att_send = attend_back(0, None)
    att_got = ex(att_send, 1)
    mlp_pair = jnp.stack([mlp_part, mlp_other])
    mlp_other = ex(tie(mlp_pair, done), 4)
    norm_moments = norm_moments + swap(tie(norm_moments, done), 1)
    done, grad_first = attend_back(1, grad_first)
    att_sum = att_keep + att_got
    att_got = ex(tie(att_sum[2:], done), 4)
    mlp_pieces = hop([mlp_pair, mlp_other], done)
    norm_moments = norm_moments + swap(tie(norm_moments, done), 2)
    done, grad_first = attend_back(2, grad_first)
    mask = 4
    while mask < clips:
        norm_moments = norm_moments + swap(tie(norm_moments, done), mask)
        mask *= 2
    att_sum = att_sum[:2] + att_got
    att_got = ex(tie(att_sum[1], done), 2)
    done, grad_first = attend_back(3, grad_first)
    att_sum = sum_rest(att_sum[0] + tie(att_got, done), clips, shards, clip_index)
    att_dir, (mom1_qkv, mom1_out), (mom2_qkv, mom2_out) = moments(
        att_sum,
        ((local, "stack"), (local, "turned")),
        (jnp.transpose(m_qkv, (1, 0, 2)), m_out),
        (jnp.transpose(v_qkv, (1, 0, 2)), v_out),
    )
    att_part = gather_rest(att_dir, clips, shards, clip_index)
    att_other = ex(att_part, 2)
    done, inputs_low, norm_grad1 = call(
        final_kernel,
        grid,
        [row(width), row(width), whole_block(4, width), row(width)],
        [row(width), whole_block(2, width)],
        [rows_low, shape((2, width), F32)],
        cost=(10_000_000, 20_000_000),
    )(kept, order, gate(tie(inputs, att_part)), grad_middle, norms, grad_first)

    att_pair = jnp.stack([att_part, att_other])
    att_other = ex(tie(att_pair, done), 4)
    norm_sum = jnp.concatenate([norm_grad1, norm_grad2])
    norm_got = swap(norm_sum, 1)

    flat_rows = patch_count * (width // 128) * clip_count
    done, patch_flat = call(
        unselect_kernel,
        (1,),
        [whole_block(clip_count, 1, patch_count), whole_block(clip_count, length, width)],
        [whole_block(flat_rows, 128)],
        [shape((flat_rows, 128), F32)],
        cost=(5_000_000_000, 20_000_000),
    )(kept, order, placed, gate(inputs_low))
    patch_grad = (
        patch_flat.reshape(patch_count, width // 128, clip_count, 128)
        .transpose(0, 2, 1, 3)
        .reshape(patch_count, clip_count, width)
        .transpose(1, 0, 2)
    )
    att_pieces = hop([att_pair, att_other], done)
    norm_sum = norm_sum + tie(norm_got, done)
    norm_got = swap(norm_sum, 2)
    done, full_up, low_up, full_down, low_down = assemble(
        mlp_pieces,
        (w_up, w_down),
        ((hidden, False, rate_model), (hidden, True, FF ** (-0.5))),
        norm_sum,
    )
    norm_sum = norm_sum + tie(norm_got, done)
    mask = 4
    while mask < clips:
        norm_got = swap(norm_sum, mask)
        if mask == 4:
            done, qkv_full, qkv_low, full_out, low_out = assemble(
                att_pieces,
                (qkv_rows, w_out),
                (
                    (packed_width, True, rate_model),
                    (local, True, max(16 * D // BLOCK, 1) ** (-0.5)),
                ),
                norm_sum,
            )
            norm_got = tie(norm_got, done)
        norm_sum = norm_sum + norm_got
        mask *= 2

    def unrow(array):
        return jnp.transpose(array.reshape(3, local, width), (2, 0, 1))

    def norm_piece(array):
        return own_part(array, 1, clip_index, clips)

    norm_dir, mom1_norms, mom2_norms = adam_direction(norm_sum, norm_moments[:4], norm_moments[4:])
    norm_sum = tie(norm_sum, *tokens)
    full_norms = norms - 0.3 * (norm_dir + 0.01 * norms)

    return (
        block_out,
        patch_grad,
        norm_piece(norm_sum),
        unrow(qkv_full),
        full_out,
        full_up,
        full_down,
        full_norms,
        jnp.transpose(mom1_qkv, (1, 0, 2)),
        mom1_out,
        mom1_up,
        mom1_down.T,
        norm_piece(mom1_norms),
        jnp.transpose(mom2_qkv, (1, 0, 2)),
        mom2_out,
        mom2_up,
        mom2_down.T,
        norm_piece(mom2_norms),
        unrow(qkv_low),
        low_out,
        low_up,
        low_down,
    )


def solution(mesh):
    return jax.shard_map(
        on_device,
        mesh=mesh,
        in_specs=(
            P("clip", None, None),
            P("clip", None),
            P("clip", None),
            P("clip", None, None),
            P(None, None, "tp"),
            P("tp", None),
            P(None, "tp"),
            P("tp", None),
            P(),
            P("clip", None, "tp"),
            P("clip", None, "tp"),
            P("tp", "clip"),
            P("tp", "clip"),
            P("clip", "tp"),
            P("clip", "tp"),
            P("tp", "clip"),
            P("tp", "clip"),
            P(None, "clip"),
            P(None, "clip"),
        ),
        out_specs=(
            P("clip", None, None),
            P("clip", None, None),
            P(None, "clip"),
            P(None, None, "tp"),
            P("tp", None),
            P(None, "tp"),
            P("tp", None),
            P(),
            P("clip", None, "tp"),
            P("tp", "clip"),
            P("clip", "tp"),
            P("tp", "clip"),
            P(None, "clip"),
            P("clip", None, "tp"),
            P("tp", "clip"),
            P("clip", "tp"),
            P("tp", "clip"),
            P(None, "clip"),
            P(None, None, "tp"),
            P("tp", None),
            P(None, "tp"),
            P("tp", None),
        ),
        check_vma=False,
    )
```

```python
import functools

import jax
import jax.numpy as jnp
from jax import lax
from jax.experimental import pallas as pl
from jax.experimental.pallas import tpu as pltpu
from jax.sharding import PartitionSpec as P

D = 768
HD = 64
FF = 3072
BLOCK = 704
STEP = 3
EPSILON = 1e-06
SCALE = HD ** (-0.5)
GROUP = 8
SOURCES = GROUP // 2
F32 = jnp.float32
BF16 = jnp.bfloat16
VMEM_LIMIT = 18 * 2**20
MLP_LIMIT = 16 * 2**20
COST_PART = 10


def dot(left, right, left_dim, right_dim):
    return lax.dot_general(
        left, right, (((left_dim,), (right_dim,)), ((), ())), preferred_element_type=F32
    )


def positions(keep_freq, keep_time):
    bins, frames = keep_freq.shape[1], keep_time.shape[1]
    count = bins * frames
    patch = lax.broadcasted_iota(jnp.int32, (1, count), 1)
    patch_bin = jnp.zeros((1, count), jnp.int32)
    for index in range(1, bins):
        patch_bin += (patch >= index * frames).astype(jnp.int32)
    patch_frame = patch - patch_bin * frames

    def spread(index, size):
        return jnp.where(
            lax.broadcasted_iota(jnp.int32, (size, count), 0) == index, 1.0, 0.0
        ).astype(BF16)

    def before(size):
        row = lax.broadcasted_iota(jnp.int32, (size, size), 0)
        column = lax.broadcasted_iota(jnp.int32, (size, size), 1)
        return jnp.where(row < column, 1.0, 0.0).astype(BF16)

    freq, time = keep_freq.astype(F32).astype(BF16), keep_time.astype(F32).astype(BF16)
    rank_freq = dot(freq, before(bins), 1, 0).astype(BF16)
    rank_time = dot(time, before(frames), 1, 0).astype(BF16)
    by_bin, by_frame = spread(patch_bin, bins), spread(patch_frame, frames)
    time_count = jnp.sum(keep_time.astype(F32), axis=1, keepdims=True)
    placed = dot(rank_freq, by_bin, 1, 0) * time_count + dot(rank_time, by_frame, 1, 0)
    present = dot(freq, by_bin, 1, 0) * dot(time, by_frame, 1, 0)
    return jnp.where(present > 0.5, placed, -1.0).astype(jnp.int32)


def norm_parts(values):
    centre = values - jnp.mean(values, axis=-1, keepdims=True)
    spread = jnp.mean(centre * centre, axis=-1, keepdims=True)
    inverse = lax.rsqrt(spread + EPSILON)
    return centre * inverse, inverse


def norm_back(values, gain, grad):
    unit, inverse = norm_parts(values)
    grad_unit = grad * gain
    mean_grad = jnp.mean(grad_unit, axis=-1, keepdims=True)
    mean_both = jnp.mean(grad_unit * unit, axis=-1, keepdims=True)
    back = inverse * (grad_unit - mean_grad - unit * mean_both)
    gain_grad = jnp.sum(grad * unit, axis=0, keepdims=True)
    shift_grad = jnp.sum(grad, axis=0, keepdims=True)
    return back, gain_grad, shift_grad


def live_column(kept, length):
    return lax.broadcasted_iota(jnp.int32, (length, 1), 0) < kept


def tree_sum(parts, odd):
    if len(parts) != 4:
        total = parts[0]
        for part in parts[1:]:
            total = total + part
        return total
    own, after, across, before = parts
    near = jnp.where(odd, before, after)
    far = jnp.where(odd, after, before)
    return (own + near) + (across + far)


def plain_call(body, grid, in_specs, out_specs, out_shape, scratch=(), aliases=None, cost=None, limit=None, far=(), far_outs=()):
    at = 2 + len(in_specs)
    out_shape = [
        pltpu.HBM(array.shape, array.dtype) if index in far_outs else array
        for index, array in enumerate(out_shape)
    ]

    def with_token(*refs):
        refs[at][...] = jnp.zeros_like(refs[at])
        body(*refs[:at], *refs[at + 1 :])

    run = pl.pallas_call(
        with_token,
        grid_spec=pltpu.PrefetchScalarGridSpec(
            num_scalar_prefetch=2,
            grid=grid,
            in_specs=in_specs,
            out_specs=[whole_block(8, 128), *out_specs],
            scratch_shapes=list(scratch),
        ),
        out_shape=[jax.ShapeDtypeStruct((8, 128), F32), *out_shape],
        input_output_aliases={key: value + 1 for key, value in (aliases or {}).items()},
        compiler_params=pltpu.CompilerParams(
            dimension_semantics=("arbitrary",) * len(grid), vmem_limit_bytes=limit or VMEM_LIMIT
        ),
        cost_estimate=pl.CostEstimate(
            flops=cost[0] * COST_PART, bytes_accessed=cost[1] * COST_PART, transcendentals=0
        ),
    )

    def placed_run(*operands):
        return run(
            *[
                pltpu.with_memory_space_constraint(array, pltpu.HBM) if index - 2 in far else array
                for index, array in enumerate(operands)
            ]
        )

    return placed_run


def clip_block(*dims):
    return pl.BlockSpec((1, *dims), lambda c, *_: (c,) + (0,) * len(dims))


def whole_block(*dims):
    return pl.BlockSpec(dims, lambda *_: (0,) * len(dims))


ANY = pl.BlockSpec(memory_space=pl.ANY)


def front_kernel(kept, order, freq, time, patches, cot, norms, inputs, first, grad, placed):
    clip = pl.program_id(0)
    placed[0] = positions(freq[0], time[0])
    length, patch_count = first.shape[1], placed.shape[2]
    slots = lax.broadcasted_iota(jnp.int32, (length, patch_count), 0)
    select = jnp.where(placed[0] == slots, 1.0, 0.0).astype(BF16)
    picked = dot(select, patches[0], 1, 0)
    inputs[0] = picked
    unit, _ = norm_parts(picked)
    first[0] = (unit * norms[0:1] + norms[1:2]).astype(BF16)
    live = live_column(kept[clip], length)
    grad[0] = jnp.where(live, cot[0].astype(F32), 0.0).astype(BF16)


def pieces_kernel(kept, order, *refs):
    *sources, early, late, up, down, sems = refs
    copies = []
    for target, pair in ((early, sources[:2]), (late, sources[2:]), (up, sources[2:3]), (down, sources[3:])):
        start = 0
        for source in pair:
            rows = source.shape[0] // GROUP
            place = pl.multiple_of(order[2 * GROUP] * rows, 8)
            copies.append(
                pltpu.make_async_copy(
                    source.at[pl.ds(place, rows)],
                    target.at[pl.ds(start, rows)],
                    sems.at[len(copies)],
                )
            )
            start += rows
    for copy in copies:
        copy.start()
    for copy in copies:
        copy.wait()


def piece_copies(order, sources, start, rows, target, sems):
    copies = []
    for slot in range(GROUP):
        source = sources[slot // 2].at[slot % 2, pl.ds(start, rows)]
        place = pl.multiple_of(order[slot] * rows, 8)
        copies.append(
            pltpu.make_async_copy(source, target.at[pl.ds(place, rows)], sems.at[slot])
        )
    return copies


def augment(rows, extra_row, length):
    index = lax.broadcasted_iota(jnp.int32, (16, length), 0)
    extra = jnp.where(index == 0, extra_row, 0.0).astype(BF16)
    return jnp.concatenate([rows, extra], axis=0)


def key_bias(kept, length):
    slot = lax.broadcasted_iota(jnp.int32, (1, length), 1)
    return jnp.where(slot < kept, 0.0, -1000000000.0)


def attend_kernel(mode, fixed, heads, kept, order, first, *refs):
    clip = pl.program_id(0) if fixed is None else fixed
    if mode == "own":
        source, out_source, packed, mixed, total, low, out_low = refs
        low[...] = source[...].astype(BF16)
        out_low[...] = out_source[...].astype(BF16)
    elif mode == "gathered":
        sources, (packed, mixed, total, low, out_low) = refs[:SOURCES], refs[SOURCES:-3]
        staged, out_staged, sems = refs[-3:]

        @pl.when(clip == 0)
        def _():
            rows, out_rows = low.shape[0] // GROUP, out_low.shape[0] // GROUP
            copies = piece_copies(order, sources, 0, rows, staged, sems.at[0])
            copies += piece_copies(order, sources, rows, out_rows, out_staged, sems.at[1])
            for copy in copies:
                copy.start()
            for copy in copies:
                copy.wait()
            low[...] = staged[...].astype(BF16)
            out_low[...] = out_staged[...].astype(BF16)
    else:
        low, _, _, _, packed, mixed, total = refs

    length = first.shape[1]
    width = heads * HD
    rows = dot(low[...], first[0], 1, 1).astype(BF16)
    packed[0] = rows
    bias = key_bias(kept[clip], length)
    ones = jnp.ones((1, length), F32)
    for head in range(heads):
        at = head * HD
        query = augment((rows[at : at + HD] * SCALE).astype(BF16), ones, length)
        key = augment(rows[width + at : width + at + HD], bias, length)
        value = rows[2 * width + at : 2 * width + at + HD]
        scores = dot(key, query, 0, 0)
        largest = jnp.max(scores, axis=0, keepdims=True)
        exponent = jnp.exp(scores - largest)
        summed = jnp.sum(exponent, axis=0, keepdims=True)
        mix = dot(value, exponent.astype(BF16), 1, 0) / summed
        mixed[0, at : at + HD] = mix.astype(BF16)
        total[0, head : head + 1] = largest + jnp.log(summed)

HALF_ROOT = 0.7071067811865476
DENSITY = 0.3989422804014327


def load_mlp(order, sources, up_low, down_low, staged, sems):
    rows = up_low.shape[0] // GROUP
    lows = (up_low, down_low)
    copies = [
        piece_copies(order, sources, index * rows, rows, staged.at[index], sems.at[index])
        for index in range(2)
    ]
    for copy in copies[0] + copies[1]:
        copy.start()
    for index in range(2):
        for slot, copy in enumerate(copies[index]):
            copy.wait()
            place = pl.ds(pl.multiple_of(order[slot] * rows, 16), rows)
            lows[index][place] = staged[index, place].astype(BF16)


def mlp_rows(rows, upstream, up_low, down_low, chunk, grads=None):
    branch_sum = back_sum = None
    for start in range(0, up_low.shape[1], chunk):
        up = up_low[:, start : start + chunk]
        down = down_low[start : start + chunk]
        hidden = dot(rows, up, 1, 0)
        grad_active = dot(upstream, down, 1, 1)
        cumulative = 0.5 * (lax.erf(hidden * HALF_ROOT) + 1.0)
        active = (hidden * cumulative).astype(BF16)
        slope = cumulative + hidden * (DENSITY * jnp.exp(-0.5 * hidden * hidden))
        grad_hidden = (slope * grad_active).astype(BF16)
        branch_part = dot(active, down, 1, 0)
        back_part = dot(grad_hidden, up, 1, 1)
        branch_sum = branch_part if branch_sum is None else branch_sum + branch_part
        back_sum = back_part if back_sum is None else back_sum + back_part
        if grads is not None:
            width = up_low.shape[1]
            grads[:, start : start + chunk] += dot(rows, grad_hidden, 0, 0)
            grads[:, width + start : width + start + chunk] += dot(upstream, active, 0, 0)
    return branch_sum, back_sum


def part_copies(order, source, keep, send, sems):
    rows = keep.shape[1]
    copies = []
    for slot in range(GROUP):
        target = (keep if slot < GROUP // 2 else send).at[slot % (GROUP // 2)]
        place = pl.multiple_of(order[GROUP + slot] * rows, 8)
        copies.append(pltpu.make_async_copy(source.at[pl.ds(place, rows)], target, sems.at[slot]))
    return copies


def mlp_own_kernel(chunk, shards, kept, order, inputs, grad, norms, up_source, down_source, *refs):
    mixes, out_lows, refs = refs[:shards], refs[shards : 2 * shards], refs[2 * shards :]
    middle, second, branch, back, keep, send, up_low, down_low, staged, grads, sems = refs
    clip = pl.program_id(0)
    loads = [
        pltpu.make_async_copy(source, staged.at[index], sems.at[index])
        for index, source in enumerate((up_source, down_source))
    ]

    @pl.when(clip == 0)
    def _():
        for copy in loads:
            copy.start()
        grads[...] = jnp.zeros_like(grads)

    values = inputs[0]
    for mixed, out_low in zip(mixes, out_lows):
        values = values + dot(mixed[0], out_low[...], 0, 0)
    middle[0] = values
    unit, _ = norm_parts(values)
    second[0] = (unit * norms[2:3] + norms[3:4]).astype(BF16)

    @pl.when(clip == 0)
    def _():
        for copy, low, index in zip(loads, (up_low, down_low), range(2)):
            copy.wait()
            low[...] = staged[index].astype(BF16)

    branch_part, back_part = mlp_rows(second[0], grad[0], up_low, down_low, chunk, grads)
    branch[0] = values + branch_part
    back[0] = back_part

    @pl.when(clip == pl.num_programs(0) - 1)
    def _():
        copies = part_copies(order, grads, keep, send, sems)
        for copy in copies:
            copy.start()
        for copy in copies:
            copy.wait()


def mlp_kernel(chunk, kept, order, second, grad, branch_in, back_in, *refs):
    sources = refs[:SOURCES]
    branch, back, up_low, down_low, staged, sems = refs[SOURCES:]
    clip = pl.program_id(0)

    @pl.when(clip == 0)
    def _():
        load_mlp(order, sources, up_low, down_low, staged, sems)

    branch_part, back_part = mlp_rows(second[0], grad[0], up_low, down_low, chunk)
    branch[0] = branch_in[0] + branch_part
    back[0] = back_in[0] + back_part


def mlp_last_kernel(chunk, kept, order, second, grad, branch_in, back_in, *refs):
    sources = refs[:SOURCES]
    middle, norms, result, grad_middle, low, norm_grad = refs[SOURCES : SOURCES + 6]
    up_low, down_low, staged, sems = refs[SOURCES + 6 :]
    clip = pl.program_id(0)

    @pl.when(clip == 0)
    def _():
        load_mlp(order, sources, up_low, down_low, staged, sems)
        norm_grad[...] = jnp.zeros_like(norm_grad)

    branch_part, back_part = mlp_rows(second[0], grad[0], up_low, down_low, chunk)
    live = live_column(kept[clip], middle.shape[1])
    result[0] = jnp.where(live, branch_in[0] + branch_part, 0.0).astype(BF16)
    back, gain_grad, shift_grad = norm_back(middle[0], norms[2:3], back_in[0] + back_part)
    both = grad[0].astype(F32) + back
    grad_middle[0] = both
    low[0] = both.astype(BF16)
    norm_grad[0:1] += gain_grad
    norm_grad[1:2] += shift_grad


def attend_back_kernel(own, heads, kept, order, packed, mixed, total, grad, out_low, *refs):
    clip = pl.program_id(0)
    if own:
        first, grad_packed, keep, send, grads, sems = refs
    else:
        (grad_packed,) = refs
    length = grad.shape[1]
    width = heads * HD
    grad_mixed = dot(out_low[...], grad[0], 1, 1).astype(BF16)
    bias = key_bias(kept[clip], length)
    ones = jnp.ones((1, length), F32)
    for head in range(heads):
        at = head * HD
        query_low = (packed[0, at : at + HD] * SCALE).astype(BF16)
        key_low = packed[0, width + at : width + at + HD]
        value = packed[0, 2 * width + at : 2 * width + at + HD]
        query = augment(query_low, ones, length)
        key = augment(key_low, bias, length)
        upstream = grad_mixed[at : at + HD]
        offset = jnp.sum(
            upstream.astype(F32) * mixed[0, at : at + HD].astype(F32), axis=0, keepdims=True
        )
        probs = jnp.exp(dot(key, query, 0, 0) - total[0, head : head + 1])
        grad_probs = dot(value, upstream, 0, 0)
        scores_low = (probs * (grad_probs - offset)).astype(BF16)
        probs_low = probs.astype(BF16)
        grad_packed[0, at : at + HD] = (dot(key_low, scores_low, 1, 0) * SCALE).astype(BF16)
        grad_packed[0, width + at : width + at + HD] = dot(query_low, scores_low, 1, 1).astype(BF16)
        grad_packed[0, 2 * width + at : 2 * width + at + HD] = dot(
            upstream, probs_low, 1, 1
        ).astype(BF16)
    if own:

        @pl.when(clip == 0)
        def _():
            grads[...] = jnp.zeros_like(grads)

        grads[:, : 3 * width] += dot(first[0], grad_packed[0], 0, 1)
        grads[:, 3 * width :] += dot(grad[0], mixed[0], 0, 1)

        @pl.when(clip == pl.num_programs(0) - 1)
        def _():
            copies = part_copies(order, grads, keep, send, sems)
            for copy in copies:
                copy.start()
            for copy in copies:
                copy.wait()


def final_kernel(shards, kept, order, inputs, grad_middle, norms, *refs):
    packs, lows, (low, norm_grad) = refs[:shards], refs[shards : 2 * shards], refs[2 * shards :]
    clip = pl.program_id(0)
    grad_first = None
    for packed, weight in zip(packs, lows):
        part = dot(packed[0], weight[...], 0, 0)
        grad_first = part if grad_first is None else grad_first + part
    back, gain_grad, shift_grad = norm_back(inputs[0], norms[0:1], grad_first)
    low[0] = (grad_middle[0] + back).astype(BF16)

    @pl.when(clip == 0)
    def _():
        norm_grad[...] = jnp.zeros_like(norm_grad)

    norm_grad[0:1] += gain_grad
    norm_grad[1:2] += shift_grad


def unselect_kernel(kept, order, placed, low, patch_grad):
    clip_count, length, width = low.shape
    patch_count = placed.shape[2]
    lanes = 128
    tiles = width // lanes
    slots = lax.broadcasted_iota(jnp.int32, (length, patch_count), 0)
    for clip in range(clip_count):
        select = jnp.where(placed[clip] == slots, 1.0, 0.0).astype(BF16)
        back = dot(select, low[clip], 0, 0)
        for tile in range(tiles):
            rows = pl.ds(tile * clip_count + clip, patch_count, stride=tiles * clip_count)
            patch_grad[rows, :] = back[:, tile * lanes : (tile + 1) * lanes]


def adam_direction(gradient, first_mom, second_mom):
    first_new = 0.5 * first_mom + 0.5 * gradient
    second_new = 0.5 * second_mom + 0.5 * gradient * gradient
    fix = 1.0 - 0.5**STEP
    direction = first_new / fix / (jnp.sqrt(second_new / fix) + 1e-08)
    return direction, first_new, second_new


def moments_kernel(layout, kept, order, gradient, *refs):
    count = len(layout)
    firsts, seconds = refs[:count], refs[count : 2 * count]
    direction, first_outs, second_outs = (
        refs[2 * count],
        refs[2 * count + 1 : 3 * count + 1],
        refs[3 * count + 1 :],
    )
    start = 0
    for index, (wide, form) in enumerate(layout):
        parts = 3 if form == "stack" else 1
        for part in range(parts):
            columns = slice(start, start + wide)
            grad = gradient[:, columns]
            if form == "turned":
                first, second = firsts[index][...].T, seconds[index][...].T
            elif form == "stack":
                first, second = firsts[index][part], seconds[index][part]
            else:
                first, second = firsts[index][...], seconds[index][...]
            step, first, second = adam_direction(grad, first, second)
            direction[:, columns] = step
            if form == "turned":
                first_outs[index][...], second_outs[index][...] = first.T, second.T
            elif form == "stack":
                first_outs[index][part], second_outs[index][part] = first, second
            else:
                first_outs[index][...], second_outs[index][...] = first, second
            start += wide


def assemble_kernel(layout, kept, order, *refs):
    count = len(layout)
    sources, refs = refs[:SOURCES], refs[SOURCES:]
    weights, outs = refs[:count], refs[count : 3 * count]
    staged, sems = refs[3 * count :]
    copies = piece_copies(order, sources, 0, sources[0].shape[1], staged, sems)
    for copy in copies:
        copy.start()
    for copy in copies:
        copy.wait()
    start = 0
    for index, (wide, turned, rate) in enumerate(layout):
        step = staged[:, start : start + wide]
        if turned:
            step = step.T
        weight = weights[index][...]
        values = weight - rate * (step + 0.01 * weight)
        outs[2 * index][...] = values
        outs[2 * index + 1][...] = values.astype(BF16)
        start += wide


def swap_bits(code):
    return code & 1 | (code >> 2 & 1) << 1 | (code >> 1 & 1) << 2


def members(clips):
    return clips // GROUP


def exchange(array, code, clips, shards):
    step = members(clips)
    pairs = []
    for clip in range(clips):
        member, rest = divmod(clip, step)
        other = member ^ (swap_bits(code) if member & 1 else code)
        for shard in range(shards):
            pairs.append((clip * shards + shard, (other * step + rest) * shards + shard))
    return lax.ppermute(array, ("clip", "tp"), pairs)


def swap_rest(array, mask, clips, shards):
    pairs = [
        (clip * shards + shard, (clip ^ mask) * shards + shard)
        for clip in range(clips)
        for shard in range(shards)
    ]
    return lax.ppermute(array, ("clip", "tp"), pairs)


def shift(array, step, clips, shards):
    pairs = [
        (clip * shards + (shard + step) % shards, clip * shards + shard)
        for clip in range(clips)
        for shard in range(shards)
    ]
    return lax.ppermute(array, ("clip", "tp"), pairs)


def tie(array, *others):
    return lax.optimization_barrier((array, *others))[0]


def piece_order(member):
    odd = member & 1

    def place(base, parity, code):
        return base ^ jnp.where(parity == 1, swap_bits(code), code)

    near = [place(member, odd, code) for code in (0, 2, 4, 6)]
    far = [place(member ^ 1, 1 - odd, code) for code in (0, 2, 4, 6)]
    return near + far


def grad_order(member):
    odd = member & 1

    def place(code):
        return member ^ jnp.where(odd == 1, swap_bits(code), code)

    return [place(code) for code in (0, 2, 4, 6)] + [place(code) for code in (1, 5, 3, 7)]


def sum_rest(part, clips, shards, clip_index):
    step = members(clips)
    rest = clip_index % step
    half = step // 2
    while half:
        low, high = jnp.split(part, 2)
        upper = (rest & half) > 0
        got = swap_rest(jnp.where(upper, low, high), half, clips, shards)
        part = jnp.where(upper, high, low) + got
        half //= 2
    return part


def gather_rest(part, clips, shards, clip_index):
    step = members(clips)
    rest = clip_index % step
    half = 1
    while half < step:
        got = swap_rest(part, half, clips, shards)
        upper = (rest & half) > 0
        part = jnp.concatenate([jnp.where(upper, got, part), jnp.where(upper, part, got)])
        half *= 2
    return part


def sum_all(array, clips, shards):
    mask = 1
    while mask < clips:
        array = array + swap_rest(array, mask, clips, shards)
        mask *= 2
    return array


def own_part(array, axis_dim, clip_index, parts):
    part_width = array.shape[axis_dim] // parts
    return lax.dynamic_slice_in_dim(array, clip_index * part_width, part_width, axis_dim)


def on_device(
    patches,
    keep_freq,
    keep_time,
    cotangent,
    w_qkv,
    w_out,
    w_up,
    w_down,
    norms,
    m_qkv,
    v_qkv,
    m_out,
    v_out,
    m_up,
    v_up,
    m_down,
    v_down,
    m_norms,
    v_norms,
):
    clip_count, length, width = cotangent.shape
    patch_count = patches.shape[1]
    clips, shards = lax.axis_size("clip"), lax.axis_size("tp")
    clip_index, shard_index = lax.axis_index("clip"), lax.axis_index("tp")
    local = w_qkv.shape[2]
    heads = local // HD
    hidden = w_up.shape[1]
    packed_width = 3 * local
    member = clip_index % GROUP

    group = members(clips)
    member = clip_index // group
    waiting, started, slow, tokens = [], [], [], []

    def call(*args, **kwargs):
        run = plain_call(*args, **kwargs)

        def keep_token(*operands):
            results = run(*operands)
            tokens.append(results[0])
            return results

        return keep_token


    def ex(array, code):
        started.append(exchange(array, code, clips, shards))
        return started[-1]

    def move(array, step, two_kernels=False):
        kind = slow if two_kernels else started
        kind.append(shift(array, step, clips, shards))
        return kind[-1]

    def swap(array, mask):
        started.append(swap_rest(array, mask, clips, shards))
        return started[-1]

    def gate(array):
        array = tie(array, *waiting, *tokens[-1:])
        waiting[:] = started
        started[:] = slow
        slow.clear()
        return array

    shape = jax.ShapeDtypeStruct

    qkv_rows = jnp.transpose(w_qkv, (1, 2, 0)).reshape(packed_width, width)

    order = jnp.stack([*piece_order(member), *grad_order(member), member]).astype(jnp.int32)
    kept = (jnp.sum(keep_freq, axis=-1) * jnp.sum(keep_time, axis=-1)).astype(jnp.int32)
    _, early_piece, late_piece, up_piece, down_piece = call(
        pieces_kernel,
        (1,),
        [ANY] * 4,
        [
            whole_block((packed_width + local) // GROUP, width),
            whole_block((width + hidden) // GROUP, width),
            whole_block(width // GROUP, hidden),
            whole_block(hidden // GROUP, width),
        ],
        [
            shape(((packed_width + local) // GROUP, width), F32),
            shape(((width + hidden) // GROUP, width), F32),
            shape((width // GROUP, hidden), F32),
            shape((hidden // GROUP, width), F32),
        ],
        scratch=(pltpu.SemaphoreType.DMA((6,)),),
        cost=(1_000_000, 4_000_000),
        limit=56 * 2**20,
    )(kept, order, qkv_rows, w_out, w_up, w_down)
    steps = (1, 3, 2) if shards == 4 else tuple(range(1, shards))
    early = {step: [move(early_piece, step)] for step in steps[:2]}
    late = {}

    def hop(pieces, done):
        if len(pieces) == 1:
            return [*pieces, ex(tie(pieces[0], done), 2)]
        if pieces[0].ndim == 2:
            pair = jnp.stack([tie(piece, done) for piece in pieces])
            return [pair, ex(pair, 4)]
        return [*pieces, *[ex(tie(piece, done), 1) for piece in pieces]]

    row = functools.partial(clip_block, length)
    rows_f32 = shape((clip_count, length, width), F32)
    rows_low = shape((clip_count, length, width), BF16)
    grid = (clip_count,)

    def fixed_block(clip, *dims):
        return pl.BlockSpec((1, *dims), lambda *_: (clip,) + (0,) * len(dims))

    s1, s2, s3 = steps
    freq = gate(keep_freq[:, None, :])
    front_done, inputs, first, grad, placed = call(
        front_kernel,
        grid,
        [
            clip_block(1, keep_freq.shape[1]),
            clip_block(1, keep_time.shape[1]),
            clip_block(patch_count, width),
            row(width),
            whole_block(4, width),
        ],
        [row(width)] * 3 + [clip_block(1, patch_count)],
        [rows_f32, rows_low, rows_low, shape((clip_count, 1, patch_count), jnp.int32)],
        cost=(2 * clip_count * length * patch_count * width, 20_000_000),
        limit=24 * 2**20,
        far_outs=(0, 2),
    )(kept, order, freq, keep_time[:, None, :], patches, cotangent, norms)

    packs, mixes, totals, lows, out_lows = [], [], [], [], []

    attend_outs = [
        shape((clip_count, packed_width, length), BF16),
        shape((clip_count, local, length), BF16),
        shape((clip_count, heads, length), F32),
    ]
    low_outs = [shape((packed_width, width), BF16), shape((local, width), BF16)]
    low_specs = [whole_block(packed_width, width), whole_block(local, width)]
    attend_cost = (18_000_000_000, 25_000_000)

    def attend_own():
        def specs(clip):
            return [
                fixed_block(clip, packed_width, length),
                fixed_block(clip, local, length),
                fixed_block(clip, heads, length),
            ]

        results = call(
            functools.partial(attend_kernel, "own", 0, heads),
            (1,),
            [fixed_block(0, length, width)] + low_specs,
            specs(0) + low_specs,
            attend_outs + low_outs,
            cost=attend_cost,
            far=(1, 2),
            far_outs=(0, 1, 2),
        )(kept, order, gate(first), qkv_rows, w_out)
        yield results
        for clip in range(1, clip_count):
            _, *arrays, low, out_low = results
            arrays = call(
                functools.partial(attend_kernel, "rest", clip, heads),
                (1,),
                [fixed_block(clip, length, width), low_specs[0]] + [ANY] * 3,
                specs(clip),
                attend_outs,
                aliases={4 + index: index for index in range(3)},
                cost=attend_cost,
                far=(2, 3, 4),
                far_outs=(0, 1, 2),
            )(kept, order, gate(first), low, *arrays)
            results = [*arrays, low, out_low]
            yield results

    def attend(pieces):
        return call(
            functools.partial(attend_kernel, "gathered", None, heads),
            grid,
            [row(width)] + [ANY] * SOURCES,
            [
                clip_block(packed_width, length),
                clip_block(local, length),
                clip_block(heads, length),
            ]
            + low_specs,
            attend_outs + low_outs,
            scratch=(
                pltpu.VMEM((packed_width, width), F32),
                pltpu.VMEM((local, width), F32),
                pltpu.SemaphoreType.DMA((2, GROUP)),
            ),
            cost=attend_cost,
            far_outs=(0, 1, 2, 3, 4),
        )(kept, order, gate(first), *pieces)

    def keep(results):
        done, packed, mixed, total, low, out_low = results
        packs.append(packed)
        mixes.append(mixed)
        totals.append(total)
        lows.append(low)
        out_lows.append(out_low)
        return done

    own_rows = width // clips
    norm_moments = jnp.zeros((8, width), F32)
    norm_moments = lax.dynamic_update_slice(
        norm_moments, jnp.concatenate([m_norms, v_norms]), (0, clip_index * own_rows)
    )

    early[s1] = hop(early[s1], front_done)
    early[s3] = [move(tie(early_piece, front_done), s3)]
    norm_moments = norm_moments + swap(tie(norm_moments, front_done), 1)
    halves = attend_own()
    results = next(halves)
    early[s1] = hop(early[s1], results[0])
    early[s2] = hop(early[s2], results[0])
    late[s1] = [move(tie(late_piece, results[0]), s1, True)]
    for results in halves:
        pass
    done = keep(results)
    early[s1] = hop(early[s1], done)
    early[s2] = hop(early[s2], done)
    early[s3] = hop(early[s3], done)
    late[s2] = [move(tie(late_piece, done), s2, True)]
    done = keep(attend(early[s1]))
    early[s2] = hop(early[s2], done)
    early[s3] = hop(early[s3], done)
    late[s1] = hop(late[s1], done)
    late_up = move(tie(up_piece, done), s3, True)
    done = keep(attend(early[s2]))
    early[s3] = hop(early[s3], done)
    late[s1] = hop(late[s1], done)
    late[s2] = hop(late[s2], done)
    late_down = move(tie(down_piece, done), s3, True)
    done = keep(attend(early[s3]))
    late[s1] = hop(late[s1], done)
    late[s2] = hop(late[s2], done)
    norm_moments = norm_moments + swap(tie(norm_moments, done), 2)

    mlp_scratch = (pltpu.VMEM((width, hidden), BF16), pltpu.VMEM((hidden, width), BF16))
    stage_scratch = (
        pltpu.VMEM((2, width, hidden), F32),
        pltpu.SemaphoreType.DMA((2, GROUP)),
    )
    chunk = 256
    half_parts = shape((GROUP // 2, width // GROUP, 2 * hidden), F32)
    done, middle, second, branch, back, mlp_keep, mlp_send = call(
        functools.partial(mlp_own_kernel, chunk, shards),
        grid,
        [row(width), row(width), whole_block(4, width)]
        + [ANY, ANY]
        + [clip_block(local, length)] * shards
        + [whole_block(local, width)] * shards,
        [row(width)] * 4 + [ANY, ANY],
        [rows_f32, rows_low, rows_f32, rows_f32, half_parts, half_parts],
        scratch=mlp_scratch
        + (
            pltpu.VMEM((2, width, hidden), F32),
            pltpu.VMEM((width, 2 * hidden), F32),
            pltpu.SemaphoreType.DMA((GROUP,)),
        ),
        cost=(12_000_000_000, 30_000_000),
        limit=38 * 2**20,
        far=(0, *range(3, 5 + 2 * shards)),
        far_outs=(0, 4, 5),
    )(kept, order, gate(inputs), grad, norms, w_up, w_down, *mixes, *out_lows)

    late[s2] = hop(late[s2], done)
    late_parts = [late_up, late_down, *[ex(tie(part, done), 2) for part in (late_up, late_down)]]
    mlp_got = ex(mlp_send, 1)

    def mlp(branch, back, pieces):
        return call(
            functools.partial(mlp_kernel, chunk),
            grid,
            [row(width)] * 4 + [ANY] * SOURCES,
            [row(width), row(width)],
            [rows_f32, rows_f32],
            scratch=mlp_scratch + stage_scratch,
            aliases={4: 0, 5: 1},
            far=(4, 5, 6, 7),
            limit=MLP_LIMIT,
            cost=(9_000_000_000, 25_000_000),
        )(kept, order, gate(second), grad, branch, back, *pieces)

    done, branch, back = mlp(branch, back, late[s1])
    mask = 4
    while mask < clips:
        norm_moments = norm_moments + swap(tie(norm_moments, done), mask)
        mask *= 2
    late_parts = [tie(part, done) for part in late_parts]
    pair = jnp.concatenate(late_parts).reshape(2, late_piece.shape[0], width)
    late[s3] = [pair, ex(pair, 4)]
    mlp_sum = mlp_keep + mlp_got
    slow.append(exchange(tie(mlp_sum[2:], done), 4, clips, shards))
    mlp_got = slow[-1]
    done, branch, back = mlp(branch, back, late[s2])
    late[s3] = hop(late[s3], done)
    done, block_out, grad_middle, middle_low, norm_grad2 = call(
        functools.partial(mlp_last_kernel, chunk),
        grid,
        [row(width)] * 4 + [ANY] * SOURCES + [row(width), whole_block(4, width)],
        [row(width)] * 3 + [whole_block(2, width)],
        [rows_low, rows_f32, rows_low, shape((2, width), F32)],
        scratch=mlp_scratch + stage_scratch,
        far=(4, 5, 6, 7, 8),
        limit=MLP_LIMIT + 8 * 2**20,
        cost=(9_000_000_000, 25_000_000),
    )(kept, order, gate(second), grad, branch, back, *late[s3], middle, norms)
    mlp_sum = mlp_sum[:2] + tie(mlp_got, done)
    mlp_got = ex(mlp_sum[1], 2)

    half_parts = shape((GROUP // 2, width // GROUP, packed_width + local), F32)

    def attend_back(index):
        own = index == 0
        return call(
            functools.partial(attend_back_kernel, own, heads),
            grid,
            [
                clip_block(packed_width, length),
                clip_block(local, length),
                clip_block(heads, length),
                row(width),
                whole_block(local, width),
            ]
            + ([row(width)] if own else []),
            [clip_block(packed_width, length)] + ([ANY, ANY] if own else []),
            [shape((clip_count, packed_width, length), BF16)]
            + ([half_parts, half_parts] if own else []),
            scratch=(
                pltpu.VMEM((width, packed_width + local), F32),
                pltpu.SemaphoreType.DMA((GROUP,)),
            )
            if own
            else (),
            cost=(14_000_000_000, 14_000_000),
        )(
            kept,
            order,
            packs[index],
            mixes[index],
            totals[index],
            gate(middle_low),
            out_lows[index],
            *((first,) if own else ()),
        )

    def moments(gradient, layout, firsts, seconds):
        count = len(layout)
        specs = [whole_block(*array.shape) for array in (*firsts, *seconds)]
        results = call(
            functools.partial(moments_kernel, layout),
            (1,),
            [whole_block(*gradient.shape)] + specs,
            [whole_block(*gradient.shape)] + specs,
            [shape(array.shape, F32) for array in (gradient, *firsts, *seconds)],
            cost=(1_000_000, 5_000_000),
        )(kept, order, gradient, *firsts, *seconds)
        return results[1], results[2 : count + 2], results[count + 2 :]

    def assemble(pieces, weights, layout, done):
        total = sum(entry[0] for entry in layout)
        return call(
            functools.partial(assemble_kernel, layout),
            (1,),
            [ANY] * SOURCES + [whole_block(*weight.shape) for weight in weights],
            [whole_block(*weight.shape) for weight in weights for _ in range(2)],
            [shape(weight.shape, kind) for weight in weights for kind in (F32, BF16)],
            scratch=(pltpu.VMEM((width, total), F32), pltpu.SemaphoreType.DMA((GROUP,))),
            cost=(1_000_000, 15_000_000),
        )(kept, order, gate(tie(pieces[0], done)), *pieces[1:], *weights)

    rate_model = D ** (-0.5)
    grad_packs = [None] * shards
    done, grad_packs[0], att_keep, att_send = attend_back(0)
    att_got = ex(att_send, 1)
    mlp_sum = sum_rest(mlp_sum[0] + tie(mlp_got, done), clips, shards, clip_index)
    mlp_dir, (mom1_up, mom1_down), (mom2_up, mom2_down) = moments(
        mlp_sum,
        ((hidden, "plain"), (hidden, "plain")),
        (m_up, m_down.T),
        (v_up, v_down.T),
    )
    mlp_part = gather_rest(mlp_dir, clips, shards, clip_index)
    mlp_other = ex(mlp_part, 2)
    done, grad_packs[1] = attend_back(1)
    att_sum = att_keep + att_got
    att_got = ex(tie(att_sum[2:], done), 4)
    mlp_pair = jnp.stack([tie(mlp_part, done), tie(mlp_other, done)])
    slow.append(exchange(mlp_pair, 4, clips, shards))
    mlp_other = slow[-1]
    done, grad_packs[2] = attend_back(2)
    att_sum = att_sum[:2] + att_got
    att_got = ex(tie(att_sum[1], done), 2)
    done, grad_packs[3] = attend_back(3)
    att_sum = sum_rest(att_sum[0] + tie(att_got, done), clips, shards, clip_index)
    att_dir, (mom1_qkv, mom1_out), (mom2_qkv, mom2_out) = moments(
        att_sum,
        ((local, "stack"), (local, "turned")),
        (jnp.transpose(m_qkv, (1, 0, 2)), m_out),
        (jnp.transpose(v_qkv, (1, 0, 2)), v_out),
    )
    att_part = gather_rest(att_dir, clips, shards, clip_index)
    att_other = ex(att_part, 2)
    done, inputs_low, norm_grad1 = call(
        functools.partial(final_kernel, shards),
        grid,
        [row(width), row(width), whole_block(4, width)]
        + [clip_block(packed_width, length)] * shards
        + [whole_block(packed_width, width)] * shards,
        [row(width), whole_block(2, width)],
        [rows_low, shape((2, width), F32)],
        cost=(10_000_000, 20_000_000),
    )(kept, order, gate(tie(inputs, att_part)), grad_middle, norms, *grad_packs, *lows)

    att_pair = jnp.stack([tie(att_part, done), tie(att_other, done)])
    att_other = ex(tie(att_pair, done), 4)
    norm_sum = jnp.concatenate([norm_grad1, norm_grad2])
    norm_got = swap(norm_sum, 1)
    mlp_pieces = hop([mlp_pair, mlp_other], done)

    flat_rows = patch_count * (width // 128) * clip_count
    done, patch_flat = call(
        unselect_kernel,
        (1,),
        [whole_block(clip_count, 1, patch_count), whole_block(clip_count, length, width)],
        [whole_block(flat_rows, 128)],
        [shape((flat_rows, 128), F32)],
        cost=(5_000_000_000, 20_000_000),
    )(kept, order, placed, gate(inputs_low))
    patch_grad = (
        patch_flat.reshape(patch_count, width // 128, clip_count, 128)
        .transpose(0, 2, 1, 3)
        .reshape(patch_count, clip_count, width)
        .transpose(1, 0, 2)
    )
    att_pieces = hop([att_pair, att_other], done)
    norm_sum = norm_sum + tie(norm_got, done)
    norm_got = swap(norm_sum, 2)
    done, full_up, low_up, full_down, low_down = assemble(
        mlp_pieces,
        (w_up, w_down),
        ((hidden, False, rate_model), (hidden, True, FF ** (-0.5))),
        norm_sum,
    )
    norm_sum = norm_sum + tie(norm_got, done)
    mask = 4
    while mask < clips:
        norm_got = swap(norm_sum, mask)
        if mask == 4:
            done, qkv_full, qkv_low, full_out, low_out = assemble(
                att_pieces,
                (qkv_rows, w_out),
                (
                    (packed_width, True, rate_model),
                    (local, True, max(16 * D // BLOCK, 1) ** (-0.5)),
                ),
                norm_sum,
            )
            norm_got = tie(norm_got, done)
        norm_sum = norm_sum + norm_got
        mask *= 2

    def unrow(array):
        return jnp.transpose(array.reshape(3, local, width), (2, 0, 1))

    def norm_piece(array):
        return own_part(array, 1, clip_index, clips)

    norm_dir, mom1_norms, mom2_norms = adam_direction(norm_sum, norm_moments[:4], norm_moments[4:])
    norm_sum = tie(norm_sum, *tokens)
    full_norms = norms - 0.3 * (norm_dir + 0.01 * norms)

    return (
        block_out,
        patch_grad,
        norm_piece(norm_sum),
        unrow(qkv_full),
        full_out,
        full_up,
        full_down,
        full_norms,
        jnp.transpose(mom1_qkv, (1, 0, 2)),
        mom1_out,
        mom1_up,
        mom1_down.T,
        norm_piece(mom1_norms),
        jnp.transpose(mom2_qkv, (1, 0, 2)),
        mom2_out,
        mom2_up,
        mom2_down.T,
        norm_piece(mom2_norms),
        unrow(qkv_low),
        low_out,
        low_up,
        low_down,
    )


def solution(mesh):
    return jax.shard_map(
        on_device,
        mesh=mesh,
        in_specs=(
            P("clip", None, None),
            P("clip", None),
            P("clip", None),
            P("clip", None, None),
            P(None, None, "tp"),
            P("tp", None),
            P(None, "tp"),
            P("tp", None),
            P(),
            P("clip", None, "tp"),
            P("clip", None, "tp"),
            P("tp", "clip"),
            P("tp", "clip"),
            P("clip", "tp"),
            P("clip", "tp"),
            P("tp", "clip"),
            P("tp", "clip"),
            P(None, "clip"),
            P(None, "clip"),
        ),
        out_specs=(
            P("clip", None, None),
            P("clip", None, None),
            P(None, "clip"),
            P(None, None, "tp"),
            P("tp", None),
            P(None, "tp"),
            P("tp", None),
            P(),
            P("clip", None, "tp"),
            P("tp", "clip"),
            P("clip", "tp"),
            P("tp", "clip"),
            P(None, "clip"),
            P("clip", None, "tp"),
            P("tp", "clip"),
            P("clip", "tp"),
            P("tp", "clip"),
            P(None, "clip"),
            P(None, None, "tp"),
            P("tp", None),
            P(None, "tp"),
            P("tp", None),
        ),
        check_vma=False,
    )
```

```python
import functools

import jax
import jax.numpy as jnp
from jax import lax
from jax.experimental import pallas as pl
from jax.experimental.pallas import tpu as pltpu
from jax.sharding import PartitionSpec as P

D = 768
HD = 64
FF = 3072
BLOCK = 704
STEP = 3
EPSILON = 1e-06
SCALE = HD ** (-0.5)
GROUP = 8
SOURCES = GROUP // 2
F32 = jnp.float32
BF16 = jnp.bfloat16
VMEM_LIMIT = 18 * 2**20
MLP_LIMIT = 16 * 2**20
COST_PART = 3


def dot(left, right, left_dim, right_dim):
    return lax.dot_general(
        left, right, (((left_dim,), (right_dim,)), ((), ())), preferred_element_type=F32
    )


def positions(keep_freq, keep_time):
    bins, frames = keep_freq.shape[1], keep_time.shape[1]
    count = bins * frames
    patch = lax.broadcasted_iota(jnp.int32, (1, count), 1)
    patch_bin = jnp.zeros((1, count), jnp.int32)
    for index in range(1, bins):
        patch_bin += (patch >= index * frames).astype(jnp.int32)
    patch_frame = patch - patch_bin * frames

    def spread(index, size):
        return jnp.where(
            lax.broadcasted_iota(jnp.int32, (size, count), 0) == index, 1.0, 0.0
        ).astype(BF16)

    def before(size):
        row = lax.broadcasted_iota(jnp.int32, (size, size), 0)
        column = lax.broadcasted_iota(jnp.int32, (size, size), 1)
        return jnp.where(row < column, 1.0, 0.0).astype(BF16)

    freq, time = keep_freq.astype(F32).astype(BF16), keep_time.astype(F32).astype(BF16)
    rank_freq = dot(freq, before(bins), 1, 0).astype(BF16)
    rank_time = dot(time, before(frames), 1, 0).astype(BF16)
    by_bin, by_frame = spread(patch_bin, bins), spread(patch_frame, frames)
    time_count = jnp.sum(keep_time.astype(F32), axis=1, keepdims=True)
    placed = dot(rank_freq, by_bin, 1, 0) * time_count + dot(rank_time, by_frame, 1, 0)
    present = dot(freq, by_bin, 1, 0) * dot(time, by_frame, 1, 0)
    return jnp.where(present > 0.5, placed, -1.0).astype(jnp.int32)


def norm_parts(values):
    centre = values - jnp.mean(values, axis=-1, keepdims=True)
    spread = jnp.mean(centre * centre, axis=-1, keepdims=True)
    inverse = lax.rsqrt(spread + EPSILON)
    return centre * inverse, inverse


def norm_back(values, gain, grad):
    unit, inverse = norm_parts(values)
    grad_unit = grad * gain
    mean_grad = jnp.mean(grad_unit, axis=-1, keepdims=True)
    mean_both = jnp.mean(grad_unit * unit, axis=-1, keepdims=True)
    back = inverse * (grad_unit - mean_grad - unit * mean_both)
    gain_grad = jnp.sum(grad * unit, axis=0, keepdims=True)
    shift_grad = jnp.sum(grad, axis=0, keepdims=True)
    return back, gain_grad, shift_grad


def live_column(kept, length):
    return lax.broadcasted_iota(jnp.int32, (length, 1), 0) < kept


def tree_sum(parts, odd):
    if len(parts) != 4:
        total = parts[0]
        for part in parts[1:]:
            total = total + part
        return total
    own, after, across, before = parts
    near = jnp.where(odd, before, after)
    far = jnp.where(odd, after, before)
    return (own + near) + (across + far)


def plain_call(body, grid, in_specs, out_specs, out_shape, scratch=(), aliases=None, cost=None, limit=None, far=(), far_outs=()):
    at = 2 + len(in_specs)
    out_shape = [
        pltpu.HBM(array.shape, array.dtype) if index in far_outs else array
        for index, array in enumerate(out_shape)
    ]

    def with_token(*refs):
        refs[at][...] = jnp.zeros_like(refs[at])
        body(*refs[:at], *refs[at + 1 :])

    run = pl.pallas_call(
        with_token,
        grid_spec=pltpu.PrefetchScalarGridSpec(
            num_scalar_prefetch=2,
            grid=grid,
            in_specs=in_specs,
            out_specs=[whole_block(8, 128), *out_specs],
            scratch_shapes=list(scratch),
        ),
        out_shape=[jax.ShapeDtypeStruct((8, 128), F32), *out_shape],
        input_output_aliases={key: value + 1 for key, value in (aliases or {}).items()},
        compiler_params=pltpu.CompilerParams(
            dimension_semantics=("arbitrary",) * len(grid), vmem_limit_bytes=limit or VMEM_LIMIT
        ),
        cost_estimate=pl.CostEstimate(
            flops=cost[0] * COST_PART, bytes_accessed=cost[1] * COST_PART, transcendentals=0
        ),
    )

    def placed_run(*operands):
        return run(
            *[
                pltpu.with_memory_space_constraint(array, pltpu.HBM) if index - 2 in far else array
                for index, array in enumerate(operands)
            ]
        )

    return placed_run


def clip_block(*dims):
    return pl.BlockSpec((1, *dims), lambda c, *_: (c,) + (0,) * len(dims))


def whole_block(*dims):
    return pl.BlockSpec(dims, lambda *_: (0,) * len(dims))


ANY = pl.BlockSpec(memory_space=pl.ANY)


def front_kernel(kept, order, freq, time, patches, cot, norms, inputs, first, grad, placed):
    clip = pl.program_id(0)
    placed[0] = positions(freq[0], time[0])
    length, patch_count = first.shape[1], placed.shape[2]
    slots = lax.broadcasted_iota(jnp.int32, (length, patch_count), 0)
    select = jnp.where(placed[0] == slots, 1.0, 0.0).astype(BF16)
    picked = dot(select, patches[0], 1, 0)
    inputs[0] = picked
    unit, _ = norm_parts(picked)
    first[0] = (unit * norms[0:1] + norms[1:2]).astype(BF16)
    live = live_column(kept[clip], length)
    grad[0] = jnp.where(live, cot[0].astype(F32), 0.0).astype(BF16)


def pieces_kernel(kept, order, *refs):
    *sources, early, late, up, down, sems = refs
    copies = []
    for target, pair in ((early, sources[:2]), (late, sources[2:]), (up, sources[2:3]), (down, sources[3:])):
        start = 0
        for source in pair:
            rows = source.shape[0] // GROUP
            place = pl.multiple_of(order[2 * GROUP] * rows, 8)
            copies.append(
                pltpu.make_async_copy(
                    source.at[pl.ds(place, rows)],
                    target.at[pl.ds(start, rows)],
                    sems.at[len(copies)],
                )
            )
            start += rows
    for copy in copies:
        copy.start()
    for copy in copies:
        copy.wait()


def piece_copies(order, sources, start, rows, target, sems):
    copies = []
    for slot in range(GROUP):
        source = sources[slot // 2].at[slot % 2, pl.ds(start, rows)]
        place = pl.multiple_of(order[slot] * rows, 8)
        copies.append(
            pltpu.make_async_copy(source, target.at[pl.ds(place, rows)], sems.at[slot])
        )
    return copies


def augment(rows, extra_row, length):
    index = lax.broadcasted_iota(jnp.int32, (16, length), 0)
    extra = jnp.where(index == 0, extra_row, 0.0).astype(BF16)
    return jnp.concatenate([rows, extra], axis=0)


def key_bias(kept, length):
    slot = lax.broadcasted_iota(jnp.int32, (1, length), 1)
    return jnp.where(slot < kept, 0.0, -1000000000.0)


def attend_kernel(mode, fixed, heads, kept, order, first, *refs):
    clip = pl.program_id(0) if fixed is None else fixed
    if mode == "own":
        source, out_source, packed, mixed, total, low, out_low = refs
        low[...] = source[...].astype(BF16)
        out_low[...] = out_source[...].astype(BF16)
    elif mode == "gathered":
        sources, (packed, mixed, total, low, out_low) = refs[:SOURCES], refs[SOURCES:-3]
        staged, out_staged, sems = refs[-3:]

        @pl.when(clip == 0)
        def _():
            rows, out_rows = low.shape[0] // GROUP, out_low.shape[0] // GROUP
            copies = piece_copies(order, sources, 0, rows, staged, sems.at[0])
            copies += piece_copies(order, sources, rows, out_rows, out_staged, sems.at[1])
            for copy in copies:
                copy.start()
            for copy in copies:
                copy.wait()
            low[...] = staged[...].astype(BF16)
            out_low[...] = out_staged[...].astype(BF16)
    else:
        low, _, _, _, packed, mixed, total = refs

    length = first.shape[1]
    width = heads * HD
    rows = dot(low[...], first[0], 1, 1).astype(BF16)
    packed[0] = rows
    bias = key_bias(kept[clip], length)
    ones = jnp.ones((1, length), F32)
    for head in range(heads):
        at = head * HD
        query = augment((rows[at : at + HD] * SCALE).astype(BF16), ones, length)
        key = augment(rows[width + at : width + at + HD], bias, length)
        value = rows[2 * width + at : 2 * width + at + HD]
        scores = dot(key, query, 0, 0)
        largest = jnp.max(scores, axis=0, keepdims=True)
        exponent = jnp.exp(scores - largest)
        summed = jnp.sum(exponent, axis=0, keepdims=True)
        mix = dot(value, exponent.astype(BF16), 1, 0) / summed
        mixed[0, at : at + HD] = mix.astype(BF16)
        total[0, head : head + 1] = largest + jnp.log(summed)

HALF_ROOT = 0.7071067811865476
DENSITY = 0.3989422804014327


def load_mlp(order, sources, up_low, down_low, staged, sems):
    rows = up_low.shape[0] // GROUP
    lows = (up_low, down_low)
    copies = [
        piece_copies(order, sources, index * rows, rows, staged.at[index], sems.at[index])
        for index in range(2)
    ]
    for copy in copies[0] + copies[1]:
        copy.start()
    for index in range(2):
        for slot, copy in enumerate(copies[index]):
            copy.wait()
            place = pl.ds(pl.multiple_of(order[slot] * rows, 16), rows)
            lows[index][place] = staged[index, place].astype(BF16)


def mlp_rows(rows, upstream, up_low, down_low, chunk, grads=None):
    branch_sum = back_sum = None
    for start in range(0, up_low.shape[1], chunk):
        up = up_low[:, start : start + chunk]
        down = down_low[start : start + chunk]
        hidden = dot(rows, up, 1, 0)
        grad_active = dot(upstream, down, 1, 1)
        cumulative = 0.5 * (lax.erf(hidden * HALF_ROOT) + 1.0)
        active = (hidden * cumulative).astype(BF16)
        slope = cumulative + hidden * (DENSITY * jnp.exp(-0.5 * hidden * hidden))
        grad_hidden = (slope * grad_active).astype(BF16)
        branch_part = dot(active, down, 1, 0)
        back_part = dot(grad_hidden, up, 1, 1)
        branch_sum = branch_part if branch_sum is None else branch_sum + branch_part
        back_sum = back_part if back_sum is None else back_sum + back_part
        if grads is not None:
            width = up_low.shape[1]
            grads[:, start : start + chunk] += dot(rows, grad_hidden, 0, 0)
            grads[:, width + start : width + start + chunk] += dot(upstream, active, 0, 0)
    return branch_sum, back_sum


def part_copies(order, source, keep, send, sems):
    rows = keep.shape[1]
    copies = []
    for slot in range(GROUP):
        target = (keep if slot < GROUP // 2 else send).at[slot % (GROUP // 2)]
        place = pl.multiple_of(order[GROUP + slot] * rows, 8)
        copies.append(pltpu.make_async_copy(source.at[pl.ds(place, rows)], target, sems.at[slot]))
    return copies


def mlp_own_kernel(chunk, shards, kept, order, inputs, grad, norms, up_source, down_source, *refs):
    mixes, out_lows, refs = refs[:shards], refs[shards : 2 * shards], refs[2 * shards :]
    middle, second, branch, back, keep, send, up_low, down_low, staged, grads, sems = refs
    clip = pl.program_id(0)
    loads = [
        pltpu.make_async_copy(source, staged.at[index], sems.at[index])
        for index, source in enumerate((up_source, down_source))
    ]

    @pl.when(clip == 0)
    def _():
        for copy in loads:
            copy.start()
        grads[...] = jnp.zeros_like(grads)

    values = inputs[0]
    for mixed, out_low in zip(mixes, out_lows):
        values = values + dot(mixed[0], out_low[...], 0, 0)
    middle[0] = values
    unit, _ = norm_parts(values)
    second[0] = (unit * norms[2:3] + norms[3:4]).astype(BF16)

    @pl.when(clip == 0)
    def _():
        for copy, low, index in zip(loads, (up_low, down_low), range(2)):
            copy.wait()
            low[...] = staged[index].astype(BF16)

    branch_part, back_part = mlp_rows(second[0], grad[0], up_low, down_low, chunk, grads)
    branch[0] = values + branch_part
    back[0] = back_part

    @pl.when(clip == pl.num_programs(0) - 1)
    def _():
        copies = part_copies(order, grads, keep, send, sems)
        for copy in copies:
            copy.start()
        for copy in copies:
            copy.wait()


def mlp_kernel(chunk, kept, order, second, grad, branch_in, back_in, *refs):
    sources = refs[:SOURCES]
    branch, back, up_low, down_low, staged, sems = refs[SOURCES:]
    clip = pl.program_id(0)

    @pl.when(clip == 0)
    def _():
        load_mlp(order, sources, up_low, down_low, staged, sems)

    branch_part, back_part = mlp_rows(second[0], grad[0], up_low, down_low, chunk)
    branch[0] = branch_in[0] + branch_part
    back[0] = back_in[0] + back_part


def mlp_last_kernel(chunk, kept, order, second, grad, branch_in, back_in, *refs):
    sources = refs[:SOURCES]
    middle, norms, result, grad_middle, low, norm_grad = refs[SOURCES : SOURCES + 6]
    up_low, down_low, staged, sems = refs[SOURCES + 6 :]
    clip = pl.program_id(0)

    @pl.when(clip == 0)
    def _():
        load_mlp(order, sources, up_low, down_low, staged, sems)
        norm_grad[...] = jnp.zeros_like(norm_grad)

    branch_part, back_part = mlp_rows(second[0], grad[0], up_low, down_low, chunk)
    live = live_column(kept[clip], middle.shape[1])
    result[0] = jnp.where(live, branch_in[0] + branch_part, 0.0).astype(BF16)
    back, gain_grad, shift_grad = norm_back(middle[0], norms[2:3], back_in[0] + back_part)
    both = grad[0].astype(F32) + back
    grad_middle[0] = both
    low[0] = both.astype(BF16)
    norm_grad[0:1] += gain_grad
    norm_grad[1:2] += shift_grad


def attend_back_kernel(own, heads, kept, order, packed, mixed, total, grad, out_low, *refs):
    clip = pl.program_id(0)
    if own:
        first, grad_packed, keep, send, grads, sems = refs
    else:
        (grad_packed,) = refs
    length = grad.shape[1]
    width = heads * HD
    grad_mixed = dot(out_low[...], grad[0], 1, 1).astype(BF16)
    bias = key_bias(kept[clip], length)
    ones = jnp.ones((1, length), F32)
    for head in range(heads):
        at = head * HD
        query_low = (packed[0, at : at + HD] * SCALE).astype(BF16)
        key_low = packed[0, width + at : width + at + HD]
        value = packed[0, 2 * width + at : 2 * width + at + HD]
        query = augment(query_low, ones, length)
        key = augment(key_low, bias, length)
        upstream = grad_mixed[at : at + HD]
        offset = jnp.sum(
            upstream.astype(F32) * mixed[0, at : at + HD].astype(F32), axis=0, keepdims=True
        )
        probs = jnp.exp(dot(key, query, 0, 0) - total[0, head : head + 1])
        grad_probs = dot(value, upstream, 0, 0)
        scores_low = (probs * (grad_probs - offset)).astype(BF16)
        probs_low = probs.astype(BF16)
        grad_packed[0, at : at + HD] = (dot(key_low, scores_low, 1, 0) * SCALE).astype(BF16)
        grad_packed[0, width + at : width + at + HD] = dot(query_low, scores_low, 1, 1).astype(BF16)
        grad_packed[0, 2 * width + at : 2 * width + at + HD] = dot(
            upstream, probs_low, 1, 1
        ).astype(BF16)
    if own:

        @pl.when(clip == 0)
        def _():
            grads[...] = jnp.zeros_like(grads)

        grads[:, : 3 * width] += dot(first[0], grad_packed[0], 0, 1)
        grads[:, 3 * width :] += dot(grad[0], mixed[0], 0, 1)

        @pl.when(clip == pl.num_programs(0) - 1)
        def _():
            copies = part_copies(order, grads, keep, send, sems)
            for copy in copies:
                copy.start()
            for copy in copies:
                copy.wait()


def final_kernel(shards, kept, order, inputs, grad_middle, norms, *refs):
    packs, lows, (low, norm_grad) = refs[:shards], refs[shards : 2 * shards], refs[2 * shards :]
    clip = pl.program_id(0)
    grad_first = None
    for packed, weight in zip(packs, lows):
        part = dot(packed[0], weight[...], 0, 0)
        grad_first = part if grad_first is None else grad_first + part
    back, gain_grad, shift_grad = norm_back(inputs[0], norms[0:1], grad_first)
    low[0] = (grad_middle[0] + back).astype(BF16)

    @pl.when(clip == 0)
    def _():
        norm_grad[...] = jnp.zeros_like(norm_grad)

    norm_grad[0:1] += gain_grad
    norm_grad[1:2] += shift_grad


def unselect_kernel(kept, order, placed, low, patch_grad):
    clip_count, length, width = low.shape
    patch_count = placed.shape[2]
    lanes = 128
    tiles = width // lanes
    slots = lax.broadcasted_iota(jnp.int32, (length, patch_count), 0)
    for clip in range(clip_count):
        select = jnp.where(placed[clip] == slots, 1.0, 0.0).astype(BF16)
        back = dot(select, low[clip], 0, 0)
        for tile in range(tiles):
            rows = pl.ds(tile * clip_count + clip, patch_count, stride=tiles * clip_count)
            patch_grad[rows, :] = back[:, tile * lanes : (tile + 1) * lanes]


def adam_direction(gradient, first_mom, second_mom):
    first_new = 0.5 * first_mom + 0.5 * gradient
    second_new = 0.5 * second_mom + 0.5 * gradient * gradient
    fix = 1.0 - 0.5**STEP
    direction = first_new / fix / (jnp.sqrt(second_new / fix) + 1e-08)
    return direction, first_new, second_new


def moments_kernel(layout, riders, kept, order, gradient, *refs):
    count = len(layout)
    riding, refs = refs[:riders], refs[riders:]
    firsts, seconds = refs[:count], refs[count : 2 * count]
    direction, first_outs, second_outs = (
        refs[2 * count],
        refs[2 * count + 1 : 3 * count + 1],
        refs[3 * count + 1 :],
    )
    start = 0
    for index, (wide, form) in enumerate(layout):
        parts = 3 if form == "stack" else 1
        for part in range(parts):
            columns = slice(start, start + wide)
            grad = gradient[:, columns]
            if form == "turned":
                first, second = firsts[index][...].T, seconds[index][...].T
            elif form == "stack":
                first, second = firsts[index][part], seconds[index][part]
            else:
                first, second = firsts[index][...], seconds[index][...]
            step, first, second = adam_direction(grad, first, second)
            direction[: gradient.shape[0], columns] = step
            if form == "turned":
                first_outs[index][...], second_outs[index][...] = first.T, second.T
            elif form == "stack":
                first_outs[index][part], second_outs[index][part] = first, second
            else:
                first_outs[index][...], second_outs[index][...] = first, second
            start += wide
    if riders:
        row = gradient.shape[0]
        direction[row:] = jnp.zeros_like(direction[row:])
        for array in riding:
            direction[row : row + array.shape[0], : array.shape[1]] = array[...]
            row += array.shape[0]


def assemble_kernel(layout, riders, kept, order, *refs):
    count = len(layout)
    sources, refs = refs[:SOURCES], refs[SOURCES:]
    weights, outs = refs[:count], refs[count : 3 * count]
    if riders:
        ridden, staged, sems, riding, more_sems = refs[3 * count :]
    else:
        staged, sems = refs[3 * count :]
    rows = staged.shape[0] // GROUP
    copies = piece_copies(order, sources, 0, rows, staged, sems)
    if riders:
        for slot in range(GROUP):
            copies.append(
                pltpu.make_async_copy(
                    sources[slot // 2].at[slot % 2, pl.ds(rows, 8), pl.ds(0, 128)],
                    riding.at[order[slot]],
                    more_sems.at[slot],
                )
            )
    for copy in copies:
        copy.start()
    for copy in copies:
        copy.wait()
    start = 0
    for index, (wide, turned, rate) in enumerate(layout):
        step = staged[:, start : start + wide]
        if turned:
            step = step.T
        weight = weights[index][...]
        values = weight - rate * (step + 0.01 * weight)
        outs[2 * index][...] = values
        outs[2 * index + 1][...] = values.astype(BF16)
        start += wide
    if riders:
        for member in range(GROUP):
            ridden[:, member * rows : (member + 1) * rows] = riding[member][:, :rows]


def swap_bits(code):
    return code & 1 | (code >> 2 & 1) << 1 | (code >> 1 & 1) << 2


def members(clips):
    return clips // GROUP


def exchange(array, code, clips, shards):
    step = members(clips)
    pairs = []
    for clip in range(clips):
        member, rest = divmod(clip, step)
        other = member ^ (swap_bits(code) if member & 1 else code)
        for shard in range(shards):
            pairs.append((clip * shards + shard, (other * step + rest) * shards + shard))
    return lax.ppermute(array, ("clip", "tp"), pairs)


def swap_rest(array, mask, clips, shards):
    pairs = [
        (clip * shards + shard, (clip ^ mask) * shards + shard)
        for clip in range(clips)
        for shard in range(shards)
    ]
    return lax.ppermute(array, ("clip", "tp"), pairs)


def shift(array, step, clips, shards):
    pairs = [
        (clip * shards + (shard + step) % shards, clip * shards + shard)
        for clip in range(clips)
        for shard in range(shards)
    ]
    return lax.ppermute(array, ("clip", "tp"), pairs)


def tie(array, *others):
    return lax.optimization_barrier((array, *others))[0]


def piece_order(member):
    odd = member & 1

    def place(base, parity, code):
        return base ^ jnp.where(parity == 1, swap_bits(code), code)

    near = [place(member, odd, code) for code in (0, 2, 4, 6)]
    far = [place(member ^ 1, 1 - odd, code) for code in (0, 2, 4, 6)]
    return near + far


def grad_order(member):
    odd = member & 1

    def place(code):
        return member ^ jnp.where(odd == 1, swap_bits(code), code)

    return [place(code) for code in (0, 2, 4, 6)] + [place(code) for code in (1, 5, 3, 7)]


def sum_rest(part, clips, shards, clip_index):
    step = members(clips)
    rest = clip_index % step
    half = step // 2
    while half:
        low, high = jnp.split(part, 2)
        upper = (rest & half) > 0
        got = swap_rest(jnp.where(upper, low, high), half, clips, shards)
        part = jnp.where(upper, high, low) + got
        half //= 2
    return part


def gather_rest(part, clips, shards, clip_index):
    step = members(clips)
    rest = clip_index % step
    half = 1
    while half < step:
        got = swap_rest(part, half, clips, shards)
        upper = (rest & half) > 0
        part = jnp.concatenate([jnp.where(upper, got, part), jnp.where(upper, part, got)])
        half *= 2
    return part


def sum_all(array, clips, shards):
    mask = 1
    while mask < clips:
        array = array + swap_rest(array, mask, clips, shards)
        mask *= 2
    return array


def own_part(array, axis_dim, clip_index, parts):
    part_width = array.shape[axis_dim] // parts
    return lax.dynamic_slice_in_dim(array, clip_index * part_width, part_width, axis_dim)


def on_device(
    patches,
    keep_freq,
    keep_time,
    cotangent,
    w_qkv,
    w_out,
    w_up,
    w_down,
    norms,
    m_qkv,
    v_qkv,
    m_out,
    v_out,
    m_up,
    v_up,
    m_down,
    v_down,
    m_norms,
    v_norms,
):
    clip_count, length, width = cotangent.shape
    patch_count = patches.shape[1]
    clips, shards = lax.axis_size("clip"), lax.axis_size("tp")
    clip_index, shard_index = lax.axis_index("clip"), lax.axis_index("tp")
    local = w_qkv.shape[2]
    heads = local // HD
    hidden = w_up.shape[1]
    packed_width = 3 * local
    member = clip_index % GROUP

    group = members(clips)
    member = clip_index // group
    waiting, started, slow, tokens = [], [], [], []

    def call(*args, **kwargs):
        run = plain_call(*args, **kwargs)

        def keep_token(*operands):
            results = run(*operands)
            tokens.append(results[0])
            return results

        return keep_token


    def ex(array, code):
        started.append(exchange(array, code, clips, shards))
        return started[-1]

    def move(array, step, two_kernels=False):
        kind = slow if two_kernels else started
        kind.append(shift(array, step, clips, shards))
        return kind[-1]

    def swap(array, mask):
        started.append(swap_rest(array, mask, clips, shards))
        return started[-1]

    def gate(array):
        array = tie(array, *waiting, *tokens[-1:])
        waiting[:] = started
        started[:] = slow
        slow.clear()
        return array

    shape = jax.ShapeDtypeStruct

    qkv_rows = jnp.transpose(w_qkv, (1, 2, 0)).reshape(packed_width, width)

    order = jnp.stack([*piece_order(member), *grad_order(member), member]).astype(jnp.int32)
    kept = (jnp.sum(keep_freq, axis=-1) * jnp.sum(keep_time, axis=-1)).astype(jnp.int32)
    _, early_piece, late_piece, up_piece, down_piece = call(
        pieces_kernel,
        (1,),
        [ANY] * 4,
        [
            whole_block((packed_width + local) // GROUP, width),
            whole_block((width + hidden) // GROUP, width),
            whole_block(width // GROUP, hidden),
            whole_block(hidden // GROUP, width),
        ],
        [
            shape(((packed_width + local) // GROUP, width), F32),
            shape(((width + hidden) // GROUP, width), F32),
            shape((width // GROUP, hidden), F32),
            shape((hidden // GROUP, width), F32),
        ],
        scratch=(pltpu.SemaphoreType.DMA((6,)),),
        cost=(1_000_000, 4_000_000),
        limit=56 * 2**20,
    )(kept, order, qkv_rows, w_out, w_up, w_down)
    steps = (1, 3, 2) if shards == 4 else tuple(range(1, shards))
    early = {step: [move(early_piece, step)] for step in steps[:2]}
    late = {}

    def hop(pieces, done):
        if len(pieces) == 1:
            return [*pieces, ex(tie(pieces[0], done), 2)]
        if pieces[0].ndim == 2:
            pair = jnp.stack([tie(piece, done) for piece in pieces])
            return [pair, ex(pair, 4)]
        return [*pieces, *[ex(tie(piece, done), 1) for piece in pieces]]

    row = functools.partial(clip_block, length)
    rows_f32 = shape((clip_count, length, width), F32)
    rows_low = shape((clip_count, length, width), BF16)
    grid = (clip_count,)

    def fixed_block(clip, *dims):
        return pl.BlockSpec((1, *dims), lambda *_: (clip,) + (0,) * len(dims))

    s1, s2, s3 = steps
    freq = gate(keep_freq[:, None, :])
    front_done, inputs, first, grad, placed = call(
        front_kernel,
        grid,
        [
            clip_block(1, keep_freq.shape[1]),
            clip_block(1, keep_time.shape[1]),
            clip_block(patch_count, width),
            row(width),
            whole_block(4, width),
        ],
        [row(width)] * 3 + [clip_block(1, patch_count)],
        [rows_f32, rows_low, rows_low, shape((clip_count, 1, patch_count), jnp.int32)],
        cost=(2 * clip_count * length * patch_count * width, 20_000_000),
        limit=24 * 2**20,
        far_outs=(0, 2),
    )(kept, order, freq, keep_time[:, None, :], patches, cotangent, norms)

    packs, mixes, totals, lows, out_lows = [], [], [], [], []

    attend_outs = [
        shape((clip_count, packed_width, length), BF16),
        shape((clip_count, local, length), BF16),
        shape((clip_count, heads, length), F32),
    ]
    low_outs = [shape((packed_width, width), BF16), shape((local, width), BF16)]
    low_specs = [whole_block(packed_width, width), whole_block(local, width)]
    attend_cost = (18_000_000_000, 25_000_000)

    def attend_own():
        def specs(clip):
            return [
                fixed_block(clip, packed_width, length),
                fixed_block(clip, local, length),
                fixed_block(clip, heads, length),
            ]

        results = call(
            functools.partial(attend_kernel, "own", 0, heads),
            (1,),
            [fixed_block(0, length, width)] + low_specs,
            specs(0) + low_specs,
            attend_outs + low_outs,
            cost=attend_cost,
            far=(1, 2),
            far_outs=(0, 1, 2),
        )(kept, order, gate(first), qkv_rows, w_out)
        yield results
        for clip in range(1, clip_count):
            _, *arrays, low, out_low = results
            arrays = call(
                functools.partial(attend_kernel, "rest", clip, heads),
                (1,),
                [fixed_block(clip, length, width), low_specs[0]] + [ANY] * 3,
                specs(clip),
                attend_outs,
                aliases={4 + index: index for index in range(3)},
                cost=attend_cost,
                far=(2, 3, 4),
                far_outs=(0, 1, 2),
            )(kept, order, gate(first), low, *arrays)
            results = [*arrays, low, out_low]
            yield results

    def attend(pieces):
        return call(
            functools.partial(attend_kernel, "gathered", None, heads),
            grid,
            [row(width)] + [ANY] * SOURCES,
            [
                clip_block(packed_width, length),
                clip_block(local, length),
                clip_block(heads, length),
            ]
            + low_specs,
            attend_outs + low_outs,
            scratch=(
                pltpu.VMEM((packed_width, width), F32),
                pltpu.VMEM((local, width), F32),
                pltpu.SemaphoreType.DMA((2, GROUP)),
            ),
            cost=attend_cost,
            far_outs=(0, 1, 2, 3, 4),
        )(kept, order, gate(first), *pieces)

    def keep(results):
        done, packed, mixed, total, low, out_low = results
        packs.append(packed)
        mixes.append(mixed)
        totals.append(total)
        lows.append(low)
        out_lows.append(out_low)
        return done

    own_rows = width // clips

    early[s1] = hop(early[s1], front_done)
    early[s3] = [move(tie(early_piece, front_done), s3)]
    halves = attend_own()
    results = next(halves)
    early[s1] = hop(early[s1], results[0])
    early[s2] = hop(early[s2], results[0])
    late[s1] = [move(tie(late_piece, results[0]), s1, True)]
    for results in halves:
        pass
    done = keep(results)
    early[s1] = hop(early[s1], done)
    early[s2] = hop(early[s2], done)
    early[s3] = hop(early[s3], done)
    late[s2] = [move(tie(late_piece, done), s2, True)]
    done = keep(attend(early[s1]))
    early[s2] = hop(early[s2], done)
    early[s3] = hop(early[s3], done)
    late[s1] = hop(late[s1], done)
    late_up = move(tie(up_piece, done), s3, True)
    done = keep(attend(early[s2]))
    early[s3] = hop(early[s3], done)
    late[s1] = hop(late[s1], done)
    late[s2] = hop(late[s2], done)
    late_down = move(tie(down_piece, done), s3, True)
    done = keep(attend(early[s3]))
    late[s1] = hop(late[s1], done)
    late[s2] = hop(late[s2], done)

    mlp_scratch = (pltpu.VMEM((width, hidden), BF16), pltpu.VMEM((hidden, width), BF16))
    stage_scratch = (
        pltpu.VMEM((2, width, hidden), F32),
        pltpu.SemaphoreType.DMA((2, GROUP)),
    )
    chunk = 256
    half_parts = shape((GROUP // 2, width // GROUP, 2 * hidden), F32)
    done, middle, second, branch, back, mlp_keep, mlp_send = call(
        functools.partial(mlp_own_kernel, chunk, shards),
        grid,
        [row(width), row(width), whole_block(4, width)]
        + [ANY, ANY]
        + [clip_block(local, length)] * shards
        + [whole_block(local, width)] * shards,
        [row(width)] * 4 + [ANY, ANY],
        [rows_f32, rows_low, rows_f32, rows_f32, half_parts, half_parts],
        scratch=mlp_scratch
        + (
            pltpu.VMEM((2, width, hidden), F32),
            pltpu.VMEM((width, 2 * hidden), F32),
            pltpu.SemaphoreType.DMA((GROUP,)),
        ),
        cost=(12_000_000_000, 30_000_000),
        limit=38 * 2**20,
        far=(0, *range(3, 5 + 2 * shards)),
        far_outs=(0, 4, 5),
    )(kept, order, gate(inputs), grad, norms, w_up, w_down, *mixes, *out_lows)

    late[s2] = hop(late[s2], done)
    late_parts = [late_up, late_down, *[ex(tie(part, done), 2) for part in (late_up, late_down)]]
    mlp_got = ex(mlp_send, 1)

    def mlp(branch, back, pieces):
        return call(
            functools.partial(mlp_kernel, chunk),
            grid,
            [row(width)] * 4 + [ANY] * SOURCES,
            [row(width), row(width)],
            [rows_f32, rows_f32],
            scratch=mlp_scratch + stage_scratch,
            aliases={4: 0, 5: 1},
            far=(4, 5, 6, 7),
            limit=MLP_LIMIT,
            cost=(9_000_000_000, 25_000_000),
        )(kept, order, gate(second), grad, branch, back, *pieces)

    done, branch, back = mlp(branch, back, late[s1])
    late_parts = [tie(part, done) for part in late_parts]
    pair = jnp.concatenate(late_parts).reshape(2, late_piece.shape[0], width)
    late[s3] = [pair, ex(pair, 4)]
    mlp_sum = mlp_keep + mlp_got
    slow.append(exchange(tie(mlp_sum[2:], done), 4, clips, shards))
    mlp_got = slow[-1]
    done, branch, back = mlp(branch, back, late[s2])
    late[s3] = hop(late[s3], done)
    done, block_out, grad_middle, middle_low, norm_grad2 = call(
        functools.partial(mlp_last_kernel, chunk),
        grid,
        [row(width)] * 4 + [ANY] * SOURCES + [row(width), whole_block(4, width)],
        [row(width)] * 3 + [whole_block(2, width)],
        [rows_low, rows_f32, rows_low, shape((2, width), F32)],
        scratch=mlp_scratch + stage_scratch,
        far=(4, 5, 6, 7, 8),
        limit=MLP_LIMIT + 8 * 2**20,
        cost=(9_000_000_000, 25_000_000),
    )(kept, order, gate(second), grad, branch, back, *late[s3], middle, norms)
    mlp_sum = mlp_sum[:2] + tie(mlp_got, done)
    mlp_got = ex(mlp_sum[1], 2)

    half_parts = shape((GROUP // 2, width // GROUP, packed_width + local), F32)

    def attend_back(index):
        own = index == 0
        return call(
            functools.partial(attend_back_kernel, own, heads),
            grid,
            [
                clip_block(packed_width, length),
                clip_block(local, length),
                clip_block(heads, length),
                row(width),
                whole_block(local, width),
            ]
            + ([row(width)] if own else []),
            [clip_block(packed_width, length)] + ([ANY, ANY] if own else []),
            [shape((clip_count, packed_width, length), BF16)]
            + ([half_parts, half_parts] if own else []),
            scratch=(
                pltpu.VMEM((width, packed_width + local), F32),
                pltpu.SemaphoreType.DMA((GROUP,)),
            )
            if own
            else (),
            cost=(14_000_000_000, 14_000_000),
        )(
            kept,
            order,
            packs[index],
            mixes[index],
            totals[index],
            gate(middle_low),
            out_lows[index],
            *((first,) if own else ()),
        )

    def moments(gradient, layout, firsts, seconds, riders=()):
        count = len(layout)
        rows, wide = gradient.shape
        direction = shape((rows + sum(array.shape[0] for array in riders), wide), F32)
        specs = [whole_block(*array.shape) for array in (*firsts, *seconds)]
        results = call(
            functools.partial(moments_kernel, layout, len(riders)),
            (1,),
            [whole_block(*array.shape) for array in (gradient, *riders)] + specs,
            [whole_block(*direction.shape)] + specs,
            [direction, *[shape(array.shape, F32) for array in (*firsts, *seconds)]],
            cost=(1_000_000, 5_000_000),
        )(kept, order, gradient, *riders, *firsts, *seconds)
        return results[1], results[2 : count + 2], results[count + 2 :]

    def assemble(pieces, weights, layout, done, riders=False):
        total = sum(entry[0] for entry in layout)
        return call(
            functools.partial(assemble_kernel, layout, riders),
            (1,),
            [ANY] * SOURCES + [whole_block(*weight.shape) for weight in weights],
            [whole_block(*weight.shape) for weight in weights for _ in range(2)]
            + ([whole_block(8, width)] if riders else []),
            [shape(weight.shape, kind) for weight in weights for kind in (F32, BF16)]
            + ([shape((8, width), F32)] if riders else []),
            scratch=(pltpu.VMEM((width, total), F32), pltpu.SemaphoreType.DMA((GROUP,)))
            + (
                (pltpu.VMEM((GROUP, 8, 128), F32), pltpu.SemaphoreType.DMA((GROUP,)))
                if riders
                else ()
            ),
            cost=(1_000_000, 15_000_000),
        )(kept, order, gate(tie(pieces[0], done)), *pieces[1:], *weights)

    riders = group == 1
    rate_model = D ** (-0.5)
    grad_packs = [None] * shards
    done, grad_packs[0], att_keep, att_send = attend_back(0)
    att_got = ex(att_send, 1)
    mlp_sum = sum_rest(mlp_sum[0] + tie(mlp_got, done), clips, shards, clip_index)
    mlp_dir, (mom1_up, mom1_down), (mom2_up, mom2_down) = moments(
        mlp_sum,
        ((hidden, "plain"), (hidden, "plain")),
        (m_up, m_down.T),
        (v_up, v_down.T),
        (m_norms, v_norms) if riders else (),
    )
    mlp_part = gather_rest(mlp_dir, clips, shards, clip_index)
    mlp_other = ex(mlp_part, 2)
    done, grad_packs[1] = attend_back(1)
    att_sum = att_keep + att_got
    att_got = ex(tie(att_sum[2:], done), 4)
    mlp_pair = jnp.stack([tie(mlp_part, done), tie(mlp_other, done)])
    slow.append(exchange(mlp_pair, 4, clips, shards))
    mlp_other = slow[-1]
    done, grad_packs[2] = attend_back(2)
    att_sum = att_sum[:2] + att_got
    att_got = ex(tie(att_sum[1], done), 2)
    done, grad_packs[3] = attend_back(3)
    att_sum = sum_rest(att_sum[0] + tie(att_got, done), clips, shards, clip_index)
    att_dir, (mom1_qkv, mom1_out), (mom2_qkv, mom2_out) = moments(
        att_sum,
        ((local, "stack"), (local, "turned")),
        (jnp.transpose(m_qkv, (1, 0, 2)), m_out),
        (jnp.transpose(v_qkv, (1, 0, 2)), v_out),
    )
    att_part = gather_rest(att_dir, clips, shards, clip_index)
    att_other = ex(att_part, 2)
    done, inputs_low, norm_grad1 = call(
        functools.partial(final_kernel, shards),
        grid,
        [row(width), row(width), whole_block(4, width)]
        + [clip_block(packed_width, length)] * shards
        + [whole_block(packed_width, width)] * shards,
        [row(width), whole_block(2, width)],
        [rows_low, shape((2, width), F32)],
        cost=(10_000_000, 20_000_000),
    )(kept, order, gate(tie(inputs, att_part)), grad_middle, norms, *grad_packs, *lows)

    att_pair = jnp.stack([tie(att_part, done), tie(att_other, done)])
    att_other = ex(tie(att_pair, done), 4)
    norm_sum = jnp.concatenate([norm_grad1, norm_grad2])
    norm_got = swap(norm_sum, 1)
    mlp_pieces = hop([mlp_pair, mlp_other], done)

    flat_rows = patch_count * (width // 128) * clip_count
    done, patch_flat = call(
        unselect_kernel,
        (1,),
        [whole_block(clip_count, 1, patch_count), whole_block(clip_count, length, width)],
        [whole_block(flat_rows, 128)],
        [shape((flat_rows, 128), F32)],
        cost=(5_000_000_000, 20_000_000),
    )(kept, order, placed, gate(inputs_low))
    patch_grad = (
        patch_flat.reshape(patch_count, width // 128, clip_count, 128)
        .transpose(0, 2, 1, 3)
        .reshape(patch_count, clip_count, width)
        .transpose(1, 0, 2)
    )
    att_pieces = hop([att_pair, att_other], done)
    norm_sum = norm_sum + tie(norm_got, done)
    norm_got = swap(norm_sum, 2)
    done, full_up, low_up, full_down, low_down, *norm_moments = assemble(
        mlp_pieces,
        (w_up, w_down),
        ((hidden, False, rate_model), (hidden, True, FF ** (-0.5))),
        norm_sum,
        riders,
    )
    norm_sum = norm_sum + tie(norm_got, done)
    mask = 4
    while mask < clips:
        norm_got = swap(norm_sum, mask)
        if mask == 4:
            done, qkv_full, qkv_low, full_out, low_out = assemble(
                att_pieces,
                (qkv_rows, w_out),
                (
                    (packed_width, True, rate_model),
                    (local, True, max(16 * D // BLOCK, 1) ** (-0.5)),
                ),
                norm_sum,
            )
            norm_got = tie(norm_got, done)
        norm_sum = norm_sum + norm_got
        mask *= 2

    def unrow(array):
        return jnp.transpose(array.reshape(3, local, width), (2, 0, 1))

    def norm_piece(array):
        return own_part(array, 1, clip_index, clips)

    if riders:
        (norm_moments,) = norm_moments
    else:
        norm_moments = jnp.zeros((8, width), F32)
        norm_moments = lax.dynamic_update_slice(
            norm_moments, jnp.concatenate([m_norms, v_norms]), (0, clip_index * own_rows)
        )
        norm_moments = sum_all(norm_moments, clips, shards)
    norm_dir, mom1_norms, mom2_norms = adam_direction(norm_sum, norm_moments[:4], norm_moments[4:])
    norm_sum = tie(norm_sum, *tokens)
    full_norms = norms - 0.3 * (norm_dir + 0.01 * norms)

    return (
        block_out,
        patch_grad,
        norm_piece(norm_sum),
        unrow(qkv_full),
        full_out,
        full_up,
        full_down,
        full_norms,
        jnp.transpose(mom1_qkv, (1, 0, 2)),
        mom1_out,
        mom1_up,
        mom1_down.T,
        norm_piece(mom1_norms),
        jnp.transpose(mom2_qkv, (1, 0, 2)),
        mom2_out,
        mom2_up,
        mom2_down.T,
        norm_piece(mom2_norms),
        unrow(qkv_low),
        low_out,
        low_up,
        low_down,
    )


def solution(mesh):
    return jax.shard_map(
        on_device,
        mesh=mesh,
        in_specs=(
            P("clip", None, None),
            P("clip", None),
            P("clip", None),
            P("clip", None, None),
            P(None, None, "tp"),
            P("tp", None),
            P(None, "tp"),
            P("tp", None),
            P(),
            P("clip", None, "tp"),
            P("clip", None, "tp"),
            P("tp", "clip"),
            P("tp", "clip"),
            P("clip", "tp"),
            P("clip", "tp"),
            P("tp", "clip"),
            P("tp", "clip"),
            P(None, "clip"),
            P(None, "clip"),
        ),
        out_specs=(
            P("clip", None, None),
            P("clip", None, None),
            P(None, "clip"),
            P(None, None, "tp"),
            P("tp", None),
            P(None, "tp"),
            P("tp", None),
            P(),
            P("clip", None, "tp"),
            P("tp", "clip"),
            P("clip", "tp"),
            P("tp", "clip"),
            P(None, "clip"),
            P("clip", None, "tp"),
            P("tp", "clip"),
            P("clip", "tp"),
            P("tp", "clip"),
            P(None, "clip"),
            P(None, None, "tp"),
            P("tp", None),
            P(None, "tp"),
            P("tp", None),
        ),
        check_vma=False,
    )
```

```python
import functools

import jax
import jax.numpy as jnp
from jax import lax
from jax.experimental import pallas as pl
from jax.experimental.pallas import tpu as pltpu
from jax.sharding import PartitionSpec as P

D = 768
HD = 64
FF = 3072
BLOCK = 704
STEP = 3
EPSILON = 1e-06
SCALE = HD ** (-0.5)
GROUP = 8
SOURCES = GROUP // 2
F32 = jnp.float32
BF16 = jnp.bfloat16
VMEM_LIMIT = 18 * 2**20
MLP_LIMIT = 16 * 2**20
COST_PART = 3


def dot(left, right, left_dim, right_dim):
    return lax.dot_general(
        left, right, (((left_dim,), (right_dim,)), ((), ())), preferred_element_type=F32
    )


def positions(keep_freq, keep_time):
    bins, frames = keep_freq.shape[1], keep_time.shape[1]
    count = bins * frames
    patch = lax.broadcasted_iota(jnp.int32, (1, count), 1)
    patch_bin = jnp.zeros((1, count), jnp.int32)
    for index in range(1, bins):
        patch_bin += (patch >= index * frames).astype(jnp.int32)
    patch_frame = patch - patch_bin * frames

    def spread(index, size):
        return jnp.where(
            lax.broadcasted_iota(jnp.int32, (size, count), 0) == index, 1.0, 0.0
        ).astype(BF16)

    def before(size):
        row = lax.broadcasted_iota(jnp.int32, (size, size), 0)
        column = lax.broadcasted_iota(jnp.int32, (size, size), 1)
        return jnp.where(row < column, 1.0, 0.0).astype(BF16)

    freq, time = keep_freq.astype(F32).astype(BF16), keep_time.astype(F32).astype(BF16)
    rank_freq = dot(freq, before(bins), 1, 0).astype(BF16)
    rank_time = dot(time, before(frames), 1, 0).astype(BF16)
    by_bin, by_frame = spread(patch_bin, bins), spread(patch_frame, frames)
    time_count = jnp.sum(keep_time.astype(F32), axis=1, keepdims=True)
    placed = dot(rank_freq, by_bin, 1, 0) * time_count + dot(rank_time, by_frame, 1, 0)
    present = dot(freq, by_bin, 1, 0) * dot(time, by_frame, 1, 0)
    return jnp.where(present > 0.5, placed, -1.0).astype(jnp.int32)


def norm_parts(values):
    centre = values - jnp.mean(values, axis=-1, keepdims=True)
    spread = jnp.mean(centre * centre, axis=-1, keepdims=True)
    inverse = lax.rsqrt(spread + EPSILON)
    return centre * inverse, inverse


def norm_back(values, gain, grad):
    unit, inverse = norm_parts(values)
    grad_unit = grad * gain
    mean_grad = jnp.mean(grad_unit, axis=-1, keepdims=True)
    mean_both = jnp.mean(grad_unit * unit, axis=-1, keepdims=True)
    back = inverse * (grad_unit - mean_grad - unit * mean_both)
    gain_grad = jnp.sum(grad * unit, axis=0, keepdims=True)
    shift_grad = jnp.sum(grad, axis=0, keepdims=True)
    return back, gain_grad, shift_grad


def live_column(kept, length):
    return lax.broadcasted_iota(jnp.int32, (length, 1), 0) < kept


def tree_sum(parts, odd):
    if len(parts) != 4:
        total = parts[0]
        for part in parts[1:]:
            total = total + part
        return total
    own, after, across, before = parts
    near = jnp.where(odd, before, after)
    far = jnp.where(odd, after, before)
    return (own + near) + (across + far)


def plain_call(body, grid, in_specs, out_specs, out_shape, scratch=(), aliases=None, cost=None, limit=None, far=(), far_outs=()):
    at = 2 + len(in_specs)
    out_shape = [
        pltpu.HBM(array.shape, array.dtype) if index in far_outs else array
        for index, array in enumerate(out_shape)
    ]

    def with_token(*refs):
        refs[at][...] = jnp.zeros_like(refs[at])
        body(*refs[:at], *refs[at + 1 :])

    run = pl.pallas_call(
        with_token,
        grid_spec=pltpu.PrefetchScalarGridSpec(
            num_scalar_prefetch=2,
            grid=grid,
            in_specs=in_specs,
            out_specs=[whole_block(8, 128), *out_specs],
            scratch_shapes=list(scratch),
        ),
        out_shape=[jax.ShapeDtypeStruct((8, 128), F32), *out_shape],
        input_output_aliases={key: value + 1 for key, value in (aliases or {}).items()},
        compiler_params=pltpu.CompilerParams(
            dimension_semantics=("arbitrary",) * len(grid), vmem_limit_bytes=limit or VMEM_LIMIT
        ),
        cost_estimate=pl.CostEstimate(
            flops=cost[0] * COST_PART, bytes_accessed=cost[1] * COST_PART, transcendentals=0
        ),
    )

    def placed_run(*operands):
        return run(
            *[
                pltpu.with_memory_space_constraint(array, pltpu.HBM) if index - 2 in far else array
                for index, array in enumerate(operands)
            ]
        )

    return placed_run


def clip_block(*dims):
    return pl.BlockSpec((1, *dims), lambda c, *_: (c,) + (0,) * len(dims))


def whole_block(*dims):
    return pl.BlockSpec(dims, lambda *_: (0,) * len(dims))


ANY = pl.BlockSpec(memory_space=pl.ANY)


def front_kernel(kept, order, freq, time, patches, cot, norms, inputs, first, grad, placed):
    clip = pl.program_id(0)
    placed[0] = positions(freq[0], time[0])
    length, patch_count = first.shape[1], placed.shape[2]
    slots = lax.broadcasted_iota(jnp.int32, (length, patch_count), 0)
    select = jnp.where(placed[0] == slots, 1.0, 0.0).astype(BF16)
    picked = dot(select, patches[0], 1, 0)
    inputs[0] = picked
    unit, _ = norm_parts(picked)
    first[0] = (unit * norms[0:1] + norms[1:2]).astype(BF16)
    live = live_column(kept[clip], length)
    grad[0] = jnp.where(live, cot[0].astype(F32), 0.0).astype(BF16)


def pieces_kernel(kept, order, *refs):
    *sources, early, late, up, down, sems = refs
    copies = []
    for target, pair in ((early, sources[:2]), (late, sources[2:]), (up, sources[2:3]), (down, sources[3:])):
        start = 0
        for source in pair:
            rows = source.shape[0] // GROUP
            place = pl.multiple_of(order[2 * GROUP] * rows, 8)
            copies.append(
                pltpu.make_async_copy(
                    source.at[pl.ds(place, rows)],
                    target.at[pl.ds(start, rows)],
                    sems.at[len(copies)],
                )
            )
            start += rows
    for copy in copies:
        copy.start()
    for copy in copies:
        copy.wait()


def piece_copies(order, sources, start, rows, target, sems):
    copies = []
    for slot in range(GROUP):
        source = sources[slot // 2].at[slot % 2, pl.ds(start, rows)]
        place = pl.multiple_of(order[slot] * rows, 8)
        copies.append(
            pltpu.make_async_copy(source, target.at[pl.ds(place, rows)], sems.at[slot])
        )
    return copies


def augment(rows, extra_row, length):
    index = lax.broadcasted_iota(jnp.int32, (16, length), 0)
    extra = jnp.where(index == 0, extra_row, 0.0).astype(BF16)
    return jnp.concatenate([rows, extra], axis=0)


def key_bias(kept, length):
    slot = lax.broadcasted_iota(jnp.int32, (1, length), 1)
    return jnp.where(slot < kept, 0.0, -1000000000.0)


def attend_kernel(mode, fixed, heads, kept, order, first, *refs):
    clip = pl.program_id(0) if fixed is None else fixed
    if mode == "own":
        source, out_source, packed, mixed, total, low, out_low = refs
        low[...] = source[...].astype(BF16)
        out_low[...] = out_source[...].astype(BF16)
    elif mode == "gathered":
        sources, (packed, mixed, total, low, out_low) = refs[:SOURCES], refs[SOURCES:-3]
        staged, out_staged, sems = refs[-3:]

        @pl.when(clip == 0)
        def _():
            rows, out_rows = low.shape[0] // GROUP, out_low.shape[0] // GROUP
            copies = piece_copies(order, sources, 0, rows, staged, sems.at[0])
            copies += piece_copies(order, sources, rows, out_rows, out_staged, sems.at[1])
            for copy in copies:
                copy.start()
            for copy in copies:
                copy.wait()
            low[...] = staged[...].astype(BF16)
            out_low[...] = out_staged[...].astype(BF16)
    else:
        low, _, _, _, packed, mixed, total = refs

    length = first.shape[1]
    width = heads * HD
    rows = dot(low[...], first[0], 1, 1).astype(BF16)
    packed[0] = rows
    bias = key_bias(kept[clip], length)
    ones = jnp.ones((1, length), F32)
    for head in range(heads):
        at = head * HD
        query = augment((rows[at : at + HD] * SCALE).astype(BF16), ones, length)
        key = augment(rows[width + at : width + at + HD], bias, length)
        value = rows[2 * width + at : 2 * width + at + HD]
        scores = dot(key, query, 0, 0)
        largest = jnp.max(scores, axis=0, keepdims=True)
        exponent = jnp.exp(scores - largest)
        summed = jnp.sum(exponent, axis=0, keepdims=True)
        mix = dot(value, exponent.astype(BF16), 1, 0) / summed
        mixed[0, at : at + HD] = mix.astype(BF16)
        total[0, head : head + 1] = largest + jnp.log(summed)

HALF_ROOT = 0.7071067811865476
DENSITY = 0.3989422804014327


def load_mlp(order, sources, up_low, down_low, staged, sems):
    rows = up_low.shape[0] // GROUP
    lows = (up_low, down_low)
    copies = [
        piece_copies(order, sources, index * rows, rows, staged.at[index], sems.at[index])
        for index in range(2)
    ]
    for copy in copies[0] + copies[1]:
        copy.start()
    for index in range(2):
        for slot, copy in enumerate(copies[index]):
            copy.wait()
            place = pl.ds(pl.multiple_of(order[slot] * rows, 16), rows)
            lows[index][place] = staged[index, place].astype(BF16)


def mlp_rows(rows, upstream, up_low, down_low, chunk, grads=None):
    branch_sum = back_sum = None
    for start in range(0, up_low.shape[1], chunk):
        up = up_low[:, start : start + chunk]
        down = down_low[start : start + chunk]
        hidden = dot(rows, up, 1, 0)
        grad_active = dot(upstream, down, 1, 1)
        cumulative = 0.5 * (lax.erf(hidden * HALF_ROOT) + 1.0)
        active = (hidden * cumulative).astype(BF16)
        slope = cumulative + hidden * (DENSITY * jnp.exp(-0.5 * hidden * hidden))
        grad_hidden = (slope * grad_active).astype(BF16)
        branch_part = dot(active, down, 1, 0)
        back_part = dot(grad_hidden, up, 1, 1)
        branch_sum = branch_part if branch_sum is None else branch_sum + branch_part
        back_sum = back_part if back_sum is None else back_sum + back_part
        if grads is not None:
            width = up_low.shape[1]
            grads[:, start : start + chunk] += dot(rows, grad_hidden, 0, 0)
            grads[:, width + start : width + start + chunk] += dot(upstream, active, 0, 0)
    return branch_sum, back_sum


def part_copies(order, source, keep, send, sems):
    rows = keep.shape[1]
    copies = []
    for slot in range(GROUP):
        target = (keep if slot < GROUP // 2 else send).at[slot % (GROUP // 2)]
        place = pl.multiple_of(order[GROUP + slot] * rows, 8)
        copies.append(pltpu.make_async_copy(source.at[pl.ds(place, rows)], target, sems.at[slot]))
    return copies


def mlp_own_kernel(chunk, shards, kept, order, inputs, grad, norms, up_source, down_source, *refs):
    mixes, out_lows, refs = refs[:shards], refs[shards : 2 * shards], refs[2 * shards :]
    middle, second, branch, back, keep, send, up_low, down_low, staged, grads, sems = refs
    clip = pl.program_id(0)
    loads = [
        pltpu.make_async_copy(source, staged.at[index], sems.at[index])
        for index, source in enumerate((up_source, down_source))
    ]

    @pl.when(clip == 0)
    def _():
        for copy in loads:
            copy.start()
        grads[...] = jnp.zeros_like(grads)

    values = inputs[0]
    for mixed, out_low in zip(mixes, out_lows):
        values = values + dot(mixed[0], out_low[...], 0, 0)
    middle[0] = values
    unit, _ = norm_parts(values)
    second[0] = (unit * norms[2:3] + norms[3:4]).astype(BF16)

    @pl.when(clip == 0)
    def _():
        for copy, low, index in zip(loads, (up_low, down_low), range(2)):
            copy.wait()
            low[...] = staged[index].astype(BF16)

    branch_part, back_part = mlp_rows(second[0], grad[0], up_low, down_low, chunk, grads)
    branch[0] = values + branch_part
    back[0] = back_part

    @pl.when(clip == pl.num_programs(0) - 1)
    def _():
        copies = part_copies(order, grads, keep, send, sems)
        for copy in copies:
            copy.start()
        for copy in copies:
            copy.wait()


def mlp_kernel(chunk, kept, order, second, grad, branch_in, back_in, *refs):
    sources = refs[:SOURCES]
    branch, back, up_low, down_low, staged, sems = refs[SOURCES:]
    clip = pl.program_id(0)

    @pl.when(clip == 0)
    def _():
        load_mlp(order, sources, up_low, down_low, staged, sems)

    branch_part, back_part = mlp_rows(second[0], grad[0], up_low, down_low, chunk)
    branch[0] = branch_in[0] + branch_part
    back[0] = back_in[0] + back_part


def mlp_last_kernel(chunk, kept, order, second, grad, branch_in, back_in, *refs):
    sources = refs[:SOURCES]
    middle, norms, result, grad_middle, low, norm_grad = refs[SOURCES : SOURCES + 6]
    up_low, down_low, staged, sems = refs[SOURCES + 6 :]
    clip = pl.program_id(0)

    @pl.when(clip == 0)
    def _():
        load_mlp(order, sources, up_low, down_low, staged, sems)
        norm_grad[...] = jnp.zeros_like(norm_grad)

    branch_part, back_part = mlp_rows(second[0], grad[0], up_low, down_low, chunk)
    live = live_column(kept[clip], middle.shape[1])
    result[0] = jnp.where(live, branch_in[0] + branch_part, 0.0).astype(BF16)
    back, gain_grad, shift_grad = norm_back(middle[0], norms[2:3], back_in[0] + back_part)
    both = grad[0].astype(F32) + back
    grad_middle[0] = both
    low[0] = both.astype(BF16)
    norm_grad[0:1] += gain_grad
    norm_grad[1:2] += shift_grad


def attend_back_kernel(own, heads, kept, order, packed, mixed, total, grad, out_low, *refs):
    clip = pl.program_id(0)
    if own:
        first, grad_packed, keep, send, grads, sems = refs
    else:
        (grad_packed,) = refs
    length = grad.shape[1]
    width = heads * HD
    grad_mixed = dot(out_low[...], grad[0], 1, 1).astype(BF16)
    bias = key_bias(kept[clip], length)
    ones = jnp.ones((1, length), F32)
    for head in range(heads):
        at = head * HD
        query_low = (packed[0, at : at + HD] * SCALE).astype(BF16)
        key_low = packed[0, width + at : width + at + HD]
        value = packed[0, 2 * width + at : 2 * width + at + HD]
        query = augment(query_low, ones, length)
        key = augment(key_low, bias, length)
        upstream = grad_mixed[at : at + HD]
        offset = jnp.sum(
            upstream.astype(F32) * mixed[0, at : at + HD].astype(F32), axis=0, keepdims=True
        )
        probs = jnp.exp(dot(key, query, 0, 0) - total[0, head : head + 1])
        grad_probs = dot(value, upstream, 0, 0)
        scores_low = (probs * (grad_probs - offset)).astype(BF16)
        probs_low = probs.astype(BF16)
        grad_packed[0, at : at + HD] = (dot(key_low, scores_low, 1, 0) * SCALE).astype(BF16)
        grad_packed[0, width + at : width + at + HD] = dot(query_low, scores_low, 1, 1).astype(BF16)
        grad_packed[0, 2 * width + at : 2 * width + at + HD] = dot(
            upstream, probs_low, 1, 1
        ).astype(BF16)
    if own:

        @pl.when(clip == 0)
        def _():
            grads[...] = jnp.zeros_like(grads)

        grads[:, : 3 * width] += dot(first[0], grad_packed[0], 0, 1)
        grads[:, 3 * width :] += dot(grad[0], mixed[0], 0, 1)

        @pl.when(clip == pl.num_programs(0) - 1)
        def _():
            copies = part_copies(order, grads, keep, send, sems)
            for copy in copies:
                copy.start()
            for copy in copies:
                copy.wait()


def final_kernel(shards, kept, order, inputs, grad_middle, norms, *refs):
    packs, lows, (low, norm_grad) = refs[:shards], refs[shards : 2 * shards], refs[2 * shards :]
    clip = pl.program_id(0)
    grad_first = None
    for packed, weight in zip(packs, lows):
        part = dot(packed[0], weight[...], 0, 0)
        grad_first = part if grad_first is None else grad_first + part
    back, gain_grad, shift_grad = norm_back(inputs[0], norms[0:1], grad_first)
    low[0] = (grad_middle[0] + back).astype(BF16)

    @pl.when(clip == 0)
    def _():
        norm_grad[...] = jnp.zeros_like(norm_grad)

    norm_grad[0:1] += gain_grad
    norm_grad[1:2] += shift_grad


def unselect_kernel(kept, order, placed, low, patch_grad):
    clip_count, length, width = low.shape
    patch_count = placed.shape[2]
    lanes = 128
    tiles = width // lanes
    slots = lax.broadcasted_iota(jnp.int32, (length, patch_count), 0)
    for clip in range(clip_count):
        select = jnp.where(placed[clip] == slots, 1.0, 0.0).astype(BF16)
        back = dot(select, low[clip], 0, 0)
        for tile in range(tiles):
            rows = pl.ds(tile * clip_count + clip, patch_count, stride=tiles * clip_count)
            patch_grad[rows, :] = back[:, tile * lanes : (tile + 1) * lanes]


def adam_direction(gradient, first_mom, second_mom):
    first_new = 0.5 * first_mom + 0.5 * gradient
    second_new = 0.5 * second_mom + 0.5 * gradient * gradient
    fix = 1.0 - 0.5**STEP
    direction = first_new / fix / (jnp.sqrt(second_new / fix) + 1e-08)
    return direction, first_new, second_new


def moments_kernel(layout, riders, kept, order, gradient, *refs):
    count = len(layout)
    riding, refs = refs[:riders], refs[riders:]
    firsts, seconds = refs[:count], refs[count : 2 * count]
    direction, first_outs, second_outs = (
        refs[2 * count],
        refs[2 * count + 1 : 3 * count + 1],
        refs[3 * count + 1 :],
    )
    start = 0
    for index, (wide, form) in enumerate(layout):
        parts = 3 if form == "stack" else 1
        for part in range(parts):
            columns = slice(start, start + wide)
            grad = gradient[:, columns]
            if form == "turned":
                first, second = firsts[index][...].T, seconds[index][...].T
            elif form == "stack":
                first, second = firsts[index][part], seconds[index][part]
            else:
                first, second = firsts[index][...], seconds[index][...]
            step, first, second = adam_direction(grad, first, second)
            direction[: gradient.shape[0], columns] = step
            if form == "turned":
                first_outs[index][...], second_outs[index][...] = first.T, second.T
            elif form == "stack":
                first_outs[index][part], second_outs[index][part] = first, second
            else:
                first_outs[index][...], second_outs[index][...] = first, second
            start += wide
    if riders:
        row = gradient.shape[0]
        direction[row:] = jnp.zeros_like(direction[row:])
        for array in riding:
            direction[row : row + array.shape[0], : array.shape[1]] = array[...]
            row += array.shape[0]


def assemble_kernel(layout, riders, kept, order, *refs):
    count = len(layout)
    sources, refs = refs[:SOURCES], refs[SOURCES:]
    weights, outs = refs[:count], refs[count : 3 * count]
    if riders:
        ridden, staged, sems, riding, more_sems = refs[3 * count :]
    else:
        staged, sems = refs[3 * count :]
    rows = staged.shape[0] // GROUP
    copies = piece_copies(order, sources, 0, rows, staged, sems)
    if riders:
        for slot in range(GROUP):
            copies.append(
                pltpu.make_async_copy(
                    sources[slot // 2].at[slot % 2, pl.ds(rows, 8), pl.ds(0, 128)],
                    riding.at[order[slot]],
                    more_sems.at[slot],
                )
            )
    for copy in copies:
        copy.start()
    for copy in copies:
        copy.wait()
    start = 0
    for index, (wide, turned, rate) in enumerate(layout):
        step = staged[:, start : start + wide]
        if turned:
            step = step.T
        weight = weights[index][...]
        values = weight - rate * (step + 0.01 * weight)
        outs[2 * index][...] = values
        outs[2 * index + 1][...] = values.astype(BF16)
        start += wide
    if riders:
        for member in range(GROUP):
            ridden[:, member * rows : (member + 1) * rows] = riding[member][:, :rows]


def swap_bits(code):
    return code & 1 | (code >> 2 & 1) << 1 | (code >> 1 & 1) << 2


def members(clips):
    return clips // GROUP


def exchange(array, code, clips, shards):
    step = members(clips)
    pairs = []
    for clip in range(clips):
        member, rest = divmod(clip, step)
        other = member ^ (swap_bits(code) if member & 1 else code)
        for shard in range(shards):
            pairs.append((clip * shards + shard, (other * step + rest) * shards + shard))
    return lax.ppermute(array, ("clip", "tp"), pairs)


def swap_rest(array, mask, clips, shards):
    pairs = [
        (clip * shards + shard, (clip ^ mask) * shards + shard)
        for clip in range(clips)
        for shard in range(shards)
    ]
    return lax.ppermute(array, ("clip", "tp"), pairs)


def shift(array, step, clips, shards):
    pairs = [
        (clip * shards + (shard + step) % shards, clip * shards + shard)
        for clip in range(clips)
        for shard in range(shards)
    ]
    return lax.ppermute(array, ("clip", "tp"), pairs)


def tie(array, *others):
    return lax.optimization_barrier((array, *others))[0]


def piece_order(member):
    odd = member & 1

    def place(base, parity, code):
        return base ^ jnp.where(parity == 1, swap_bits(code), code)

    near = [place(member, odd, code) for code in (0, 2, 4, 6)]
    far = [place(member ^ 1, 1 - odd, code) for code in (0, 2, 4, 6)]
    return near + far


def grad_order(member):
    odd = member & 1

    def place(code):
        return member ^ jnp.where(odd == 1, swap_bits(code), code)

    return [place(code) for code in (0, 2, 4, 6)] + [place(code) for code in (1, 5, 3, 7)]


def sum_rest(part, clips, shards, clip_index):
    step = members(clips)
    rest = clip_index % step
    half = step // 2
    while half:
        low, high = jnp.split(part, 2)
        upper = (rest & half) > 0
        got = swap_rest(jnp.where(upper, low, high), half, clips, shards)
        part = jnp.where(upper, high, low) + got
        half //= 2
    return part


def gather_rest(part, clips, shards, clip_index):
    step = members(clips)
    rest = clip_index % step
    half = 1
    while half < step:
        got = swap_rest(part, half, clips, shards)
        upper = (rest & half) > 0
        part = jnp.concatenate([jnp.where(upper, got, part), jnp.where(upper, part, got)])
        half *= 2
    return part


def sum_all(array, clips, shards):
    mask = 1
    while mask < clips:
        array = array + swap_rest(array, mask, clips, shards)
        mask *= 2
    return array


def own_part(array, axis_dim, clip_index, parts):
    part_width = array.shape[axis_dim] // parts
    return lax.dynamic_slice_in_dim(array, clip_index * part_width, part_width, axis_dim)


def on_device(
    patches,
    keep_freq,
    keep_time,
    cotangent,
    w_qkv,
    w_out,
    w_up,
    w_down,
    norms,
    m_qkv,
    v_qkv,
    m_out,
    v_out,
    m_up,
    v_up,
    m_down,
    v_down,
    m_norms,
    v_norms,
):
    clip_count, length, width = cotangent.shape
    patch_count = patches.shape[1]
    clips, shards = lax.axis_size("clip"), lax.axis_size("tp")
    clip_index, shard_index = lax.axis_index("clip"), lax.axis_index("tp")
    local = w_qkv.shape[2]
    heads = local // HD
    hidden = w_up.shape[1]
    packed_width = 3 * local
    member = clip_index % GROUP

    group = members(clips)
    member = clip_index // group
    waiting, started, slow, tokens = [], [], [], []

    def call(*args, **kwargs):
        run = plain_call(*args, **kwargs)

        def keep_token(*operands):
            results = run(*operands)
            tokens.append(results[0])
            return results

        return keep_token


    def ex(array, code):
        started.append(exchange(array, code, clips, shards))
        return started[-1]

    def move(array, step, two_kernels=False):
        kind = slow if two_kernels else started
        kind.append(shift(array, step, clips, shards))
        return kind[-1]

    def swap(array, mask):
        started.append(swap_rest(array, mask, clips, shards))
        return started[-1]

    def gate(array):
        array = tie(array, *waiting, *tokens[-1:])
        waiting[:] = started
        started[:] = slow
        slow.clear()
        return array

    shape = jax.ShapeDtypeStruct

    qkv_rows = jnp.transpose(w_qkv, (1, 2, 0)).reshape(packed_width, width)

    order = jnp.stack([*piece_order(member), *grad_order(member), member]).astype(jnp.int32)
    kept = (jnp.sum(keep_freq, axis=-1) * jnp.sum(keep_time, axis=-1)).astype(jnp.int32)
    _, early_piece, late_piece, up_piece, down_piece = call(
        pieces_kernel,
        (1,),
        [ANY] * 4,
        [
            whole_block((packed_width + local) // GROUP, width),
            whole_block((width + hidden) // GROUP, width),
            whole_block(width // GROUP, hidden),
            whole_block(hidden // GROUP, width),
        ],
        [
            shape(((packed_width + local) // GROUP, width), F32),
            shape(((width + hidden) // GROUP, width), F32),
            shape((width // GROUP, hidden), F32),
            shape((hidden // GROUP, width), F32),
        ],
        scratch=(pltpu.SemaphoreType.DMA((6,)),),
        cost=(1_000_000, 4_000_000),
        limit=56 * 2**20,
    )(kept, order, qkv_rows, w_out, w_up, w_down)
    steps = (1, 3, 2) if shards == 4 else tuple(range(1, shards))
    early = {step: [move(early_piece, step)] for step in steps[:2]}
    late = {}

    def hop(pieces, done):
        if len(pieces) == 1:
            return [*pieces, ex(tie(pieces[0], done), 2)]
        if pieces[0].ndim == 2:
            pair = jnp.stack([tie(piece, done) for piece in pieces])
            return [pair, ex(pair, 4)]
        return [*pieces, *[ex(tie(piece, done), 1) for piece in pieces]]

    row = functools.partial(clip_block, length)
    rows_f32 = shape((clip_count, length, width), F32)
    rows_low = shape((clip_count, length, width), BF16)
    grid = (clip_count,)

    def fixed_block(clip, *dims):
        return pl.BlockSpec((1, *dims), lambda *_: (clip,) + (0,) * len(dims))

    s1, s2, s3 = steps
    freq = gate(keep_freq[:, None, :])
    front_done, inputs, first, grad, placed = call(
        front_kernel,
        grid,
        [
            clip_block(1, keep_freq.shape[1]),
            clip_block(1, keep_time.shape[1]),
            clip_block(patch_count, width),
            row(width),
            whole_block(4, width),
        ],
        [row(width)] * 3 + [clip_block(1, patch_count)],
        [rows_f32, rows_low, rows_low, shape((clip_count, 1, patch_count), jnp.int32)],
        cost=(2 * clip_count * length * patch_count * width, 20_000_000),
        limit=24 * 2**20,
        far_outs=(0, 2),
    )(kept, order, freq, keep_time[:, None, :], patches, cotangent, norms)

    packs, mixes, totals, lows, out_lows = [], [], [], [], []

    attend_outs = [
        shape((clip_count, packed_width, length), BF16),
        shape((clip_count, local, length), BF16),
        shape((clip_count, heads, length), F32),
    ]
    low_outs = [shape((packed_width, width), BF16), shape((local, width), BF16)]
    low_specs = [whole_block(packed_width, width), whole_block(local, width)]
    attend_cost = (18_000_000_000, 25_000_000)

    def attend_own():
        def specs(clip):
            return [
                fixed_block(clip, packed_width, length),
                fixed_block(clip, local, length),
                fixed_block(clip, heads, length),
            ]

        results = call(
            functools.partial(attend_kernel, "own", 0, heads),
            (1,),
            [fixed_block(0, length, width)] + low_specs,
            specs(0) + low_specs,
            attend_outs + low_outs,
            cost=attend_cost,
            far=(1, 2),
            far_outs=(0, 1, 2),
        )(kept, order, gate(first), qkv_rows, w_out)
        yield results
        for clip in range(1, clip_count):
            _, *arrays, low, out_low = results
            arrays = call(
                functools.partial(attend_kernel, "rest", clip, heads),
                (1,),
                [fixed_block(clip, length, width), low_specs[0]] + [ANY] * 3,
                specs(clip),
                attend_outs,
                aliases={4 + index: index for index in range(3)},
                cost=attend_cost,
                far=(2, 3, 4),
                far_outs=(0, 1, 2),
            )(kept, order, gate(first), low, *arrays)
            results = [*arrays, low, out_low]
            yield results

    def attend(pieces):
        return call(
            functools.partial(attend_kernel, "gathered", None, heads),
            grid,
            [row(width)] + [ANY] * SOURCES,
            [
                clip_block(packed_width, length),
                clip_block(local, length),
                clip_block(heads, length),
            ]
            + low_specs,
            attend_outs + low_outs,
            scratch=(
                pltpu.VMEM((packed_width, width), F32),
                pltpu.VMEM((local, width), F32),
                pltpu.SemaphoreType.DMA((2, GROUP)),
            ),
            cost=attend_cost,
            far_outs=(0, 1, 2, 3, 4),
        )(kept, order, gate(first), *pieces)

    def keep(results):
        done, packed, mixed, total, low, out_low = results
        packs.append(packed)
        mixes.append(mixed)
        totals.append(total)
        lows.append(low)
        out_lows.append(out_low)
        return done

    own_rows = width // clips

    early[s1] = hop(early[s1], front_done)
    early[s3] = [move(tie(early_piece, front_done), s3)]
    halves = attend_own()
    results = next(halves)
    early[s1] = hop(early[s1], results[0])
    early[s2] = hop(early[s2], results[0])
    early[s3] = hop(early[s3], results[0])
    late[s1] = [move(tie(late_piece, results[0]), s1, True)]
    for results in halves:
        pass
    done = keep(results)
    early[s1] = hop(early[s1], done)
    early[s2] = hop(early[s2], done)
    late[s2] = [move(tie(late_piece, done), s2, True)]
    done = keep(attend(early[s1]))
    early[s2] = hop(early[s2], done)
    early[s3] = hop(early[s3], done)
    late[s1] = hop(late[s1], done)
    late_up = move(tie(up_piece, done), s3, True)
    done = keep(attend(early[s2]))
    early[s3] = hop(early[s3], done)
    late[s1] = hop(late[s1], done)
    late[s2] = hop(late[s2], done)
    late_down = move(tie(down_piece, done), s3, True)
    done = keep(attend(early[s3]))
    late[s1] = hop(late[s1], done)
    late[s2] = hop(late[s2], done)

    mlp_scratch = (pltpu.VMEM((width, hidden), BF16), pltpu.VMEM((hidden, width), BF16))
    stage_scratch = (
        pltpu.VMEM((2, width, hidden), F32),
        pltpu.SemaphoreType.DMA((2, GROUP)),
    )
    chunk = 256
    half_parts = shape((GROUP // 2, width // GROUP, 2 * hidden), F32)
    done, middle, second, branch, back, mlp_keep, mlp_send = call(
        functools.partial(mlp_own_kernel, chunk, shards),
        grid,
        [row(width), row(width), whole_block(4, width)]
        + [ANY, ANY]
        + [clip_block(local, length)] * shards
        + [whole_block(local, width)] * shards,
        [row(width)] * 4 + [ANY, ANY],
        [rows_f32, rows_low, rows_f32, rows_f32, half_parts, half_parts],
        scratch=mlp_scratch
        + (
            pltpu.VMEM((2, width, hidden), F32),
            pltpu.VMEM((width, 2 * hidden), F32),
            pltpu.SemaphoreType.DMA((GROUP,)),
        ),
        cost=(12_000_000_000, 30_000_000),
        limit=38 * 2**20,
        far=(0, *range(3, 5 + 2 * shards)),
        far_outs=(0, 4, 5),
    )(kept, order, gate(inputs), grad, norms, w_up, w_down, *mixes, *out_lows)

    late[s2] = hop(late[s2], done)
    late_parts = [late_up, late_down, *[ex(tie(part, done), 2) for part in (late_up, late_down)]]
    mlp_got = ex(mlp_send, 1)

    def mlp(branch, back, pieces):
        return call(
            functools.partial(mlp_kernel, chunk),
            grid,
            [row(width)] * 4 + [ANY] * SOURCES,
            [row(width), row(width)],
            [rows_f32, rows_f32],
            scratch=mlp_scratch + stage_scratch,
            aliases={4: 0, 5: 1},
            far=(4, 5, 6, 7),
            limit=MLP_LIMIT,
            cost=(9_000_000_000, 25_000_000),
        )(kept, order, gate(second), grad, branch, back, *pieces)

    done, branch, back = mlp(branch, back, late[s1])
    late_parts = [tie(part, done) for part in late_parts]
    pair = jnp.concatenate(late_parts).reshape(2, late_piece.shape[0], width)
    late[s3] = [pair, ex(pair, 4)]
    mlp_sum = mlp_keep + mlp_got
    slow.append(exchange(tie(mlp_sum[2:], done), 4, clips, shards))
    mlp_got = slow[-1]
    done, branch, back = mlp(branch, back, late[s2])
    late[s3] = hop(late[s3], done)
    done, block_out, grad_middle, middle_low, norm_grad2 = call(
        functools.partial(mlp_last_kernel, chunk),
        grid,
        [row(width)] * 4 + [ANY] * SOURCES + [row(width), whole_block(4, width)],
        [row(width)] * 3 + [whole_block(2, width)],
        [rows_low, rows_f32, rows_low, shape((2, width), F32)],
        scratch=mlp_scratch + stage_scratch,
        far=(4, 5, 6, 7, 8),
        limit=MLP_LIMIT + 8 * 2**20,
        cost=(9_000_000_000, 25_000_000),
    )(kept, order, gate(second), grad, branch, back, *late[s3], middle, norms)
    mlp_sum = mlp_sum[:2] + tie(mlp_got, done)
    mlp_got = ex(mlp_sum[1], 2)

    half_parts = shape((GROUP // 2, width // GROUP, packed_width + local), F32)

    def attend_back(index):
        own = index == 0
        return call(
            functools.partial(attend_back_kernel, own, heads),
            grid,
            [
                clip_block(packed_width, length),
                clip_block(local, length),
                clip_block(heads, length),
                row(width),
                whole_block(local, width),
            ]
            + ([row(width)] if own else []),
            [clip_block(packed_width, length)] + ([ANY, ANY] if own else []),
            [shape((clip_count, packed_width, length), BF16)]
            + ([half_parts, half_parts] if own else []),
            scratch=(
                pltpu.VMEM((width, packed_width + local), F32),
                pltpu.SemaphoreType.DMA((GROUP,)),
            )
            if own
            else (),
            cost=(14_000_000_000, 14_000_000),
        )(
            kept,
            order,
            packs[index],
            mixes[index],
            totals[index],
            gate(middle_low),
            out_lows[index],
            *((first,) if own else ()),
        )

    def moments(gradient, layout, firsts, seconds, riders=()):
        count = len(layout)
        rows, wide = gradient.shape
        direction = shape((rows + sum(array.shape[0] for array in riders), wide), F32)
        specs = [whole_block(*array.shape) for array in (*firsts, *seconds)]
        results = call(
            functools.partial(moments_kernel, layout, len(riders)),
            (1,),
            [whole_block(*array.shape) for array in (gradient, *riders)] + specs,
            [whole_block(*direction.shape)] + specs,
            [direction, *[shape(array.shape, F32) for array in (*firsts, *seconds)]],
            cost=(1_000_000, 5_000_000),
        )(kept, order, gradient, *riders, *firsts, *seconds)
        return results[1], results[2 : count + 2], results[count + 2 :]

    def assemble(pieces, weights, layout, done, riders=False):
        total = sum(entry[0] for entry in layout)
        return call(
            functools.partial(assemble_kernel, layout, riders),
            (1,),
            [ANY] * SOURCES + [whole_block(*weight.shape) for weight in weights],
            [whole_block(*weight.shape) for weight in weights for _ in range(2)]
            + ([whole_block(8, width)] if riders else []),
            [shape(weight.shape, kind) for weight in weights for kind in (F32, BF16)]
            + ([shape((8, width), F32)] if riders else []),
            scratch=(pltpu.VMEM((width, total), F32), pltpu.SemaphoreType.DMA((GROUP,)))
            + (
                (pltpu.VMEM((GROUP, 8, 128), F32), pltpu.SemaphoreType.DMA((GROUP,)))
                if riders
                else ()
            ),
            cost=(1_000_000, 15_000_000),
        )(kept, order, gate(tie(pieces[0], done)), *pieces[1:], *weights)

    riders = group == 1
    rate_model = D ** (-0.5)
    grad_packs = [None] * shards
    done, grad_packs[0], att_keep, att_send = attend_back(0)
    att_got = ex(att_send, 1)
    mlp_sum = sum_rest(mlp_sum[0] + tie(mlp_got, done), clips, shards, clip_index)
    mlp_dir, (mom1_up, mom1_down), (mom2_up, mom2_down) = moments(
        mlp_sum,
        ((hidden, "plain"), (hidden, "plain")),
        (m_up, m_down.T),
        (v_up, v_down.T),
        (m_norms, v_norms) if riders else (),
    )
    mlp_part = gather_rest(mlp_dir, clips, shards, clip_index)
    mlp_other = ex(mlp_part, 2)
    done, grad_packs[1] = attend_back(1)
    att_sum = att_keep + att_got
    att_got = ex(tie(att_sum[2:], done), 4)
    mlp_pair = jnp.stack([tie(mlp_part, done), tie(mlp_other, done)])
    slow.append(exchange(mlp_pair, 4, clips, shards))
    mlp_other = slow[-1]
    done, grad_packs[2] = attend_back(2)
    att_sum = att_sum[:2] + att_got
    att_got = ex(tie(att_sum[1], done), 2)
    done, grad_packs[3] = attend_back(3)
    att_sum = sum_rest(att_sum[0] + tie(att_got, done), clips, shards, clip_index)
    att_dir, (mom1_qkv, mom1_out), (mom2_qkv, mom2_out) = moments(
        att_sum,
        ((local, "stack"), (local, "turned")),
        (jnp.transpose(m_qkv, (1, 0, 2)), m_out),
        (jnp.transpose(v_qkv, (1, 0, 2)), v_out),
    )
    att_part = gather_rest(att_dir, clips, shards, clip_index)
    att_other = ex(att_part, 2)
    done, inputs_low, norm_grad1 = call(
        functools.partial(final_kernel, shards),
        grid,
        [row(width), row(width), whole_block(4, width)]
        + [clip_block(packed_width, length)] * shards
        + [whole_block(packed_width, width)] * shards,
        [row(width), whole_block(2, width)],
        [rows_low, shape((2, width), F32)],
        cost=(10_000_000, 20_000_000),
    )(kept, order, gate(tie(inputs, att_part)), grad_middle, norms, *grad_packs, *lows)

    att_pair = jnp.stack([tie(att_part, done), tie(att_other, done)])
    att_other = ex(tie(att_pair, done), 4)
    norm_sum = jnp.concatenate([norm_grad1, norm_grad2])
    norm_got = swap(norm_sum, 1)
    mlp_pieces = hop([mlp_pair, mlp_other], done)

    flat_rows = patch_count * (width // 128) * clip_count
    done, patch_flat = call(
        unselect_kernel,
        (1,),
        [whole_block(clip_count, 1, patch_count), whole_block(clip_count, length, width)],
        [whole_block(flat_rows, 128)],
        [shape((flat_rows, 128), F32)],
        cost=(5_000_000_000, 20_000_000),
    )(kept, order, placed, gate(inputs_low))
    patch_grad = (
        patch_flat.reshape(patch_count, width // 128, clip_count, 128)
        .transpose(0, 2, 1, 3)
        .reshape(patch_count, clip_count, width)
        .transpose(1, 0, 2)
    )
    att_pieces = hop([att_pair, att_other], done)
    norm_sum = norm_sum + tie(norm_got, done)
    norm_got = swap(norm_sum, 2)
    done, full_up, low_up, full_down, low_down, *norm_moments = assemble(
        mlp_pieces,
        (w_up, w_down),
        ((hidden, False, rate_model), (hidden, True, FF ** (-0.5))),
        norm_sum,
        riders,
    )
    norm_sum = norm_sum + tie(norm_got, done)
    mask = 4
    while mask < clips:
        norm_got = swap(norm_sum, mask)
        if mask == 4:
            done, qkv_full, qkv_low, full_out, low_out = assemble(
                att_pieces,
                (qkv_rows, w_out),
                (
                    (packed_width, True, rate_model),
                    (local, True, max(16 * D // BLOCK, 1) ** (-0.5)),
                ),
                norm_sum,
            )
            norm_got = tie(norm_got, done)
        norm_sum = norm_sum + norm_got
        mask *= 2

    def unrow(array):
        return jnp.transpose(array.reshape(3, local, width), (2, 0, 1))

    def norm_piece(array):
        return own_part(array, 1, clip_index, clips)

    if riders:
        (norm_moments,) = norm_moments
    else:
        norm_moments = jnp.zeros((8, width), F32)
        norm_moments = lax.dynamic_update_slice(
            norm_moments, jnp.concatenate([m_norms, v_norms]), (0, clip_index * own_rows)
        )
        norm_moments = sum_all(norm_moments, clips, shards)
    norm_dir, mom1_norms, mom2_norms = adam_direction(norm_sum, norm_moments[:4], norm_moments[4:])
    norm_sum = tie(norm_sum, *tokens)
    full_norms = norms - 0.3 * (norm_dir + 0.01 * norms)

    return (
        block_out,
        patch_grad,
        norm_piece(norm_sum),
        unrow(qkv_full),
        full_out,
        full_up,
        full_down,
        full_norms,
        jnp.transpose(mom1_qkv, (1, 0, 2)),
        mom1_out,
        mom1_up,
        mom1_down.T,
        norm_piece(mom1_norms),
        jnp.transpose(mom2_qkv, (1, 0, 2)),
        mom2_out,
        mom2_up,
        mom2_down.T,
        norm_piece(mom2_norms),
        unrow(qkv_low),
        low_out,
        low_up,
        low_down,
    )


def solution(mesh):
    return jax.shard_map(
        on_device,
        mesh=mesh,
        in_specs=(
            P("clip", None, None),
            P("clip", None),
            P("clip", None),
            P("clip", None, None),
            P(None, None, "tp"),
            P("tp", None),
            P(None, "tp"),
            P("tp", None),
            P(),
            P("clip", None, "tp"),
            P("clip", None, "tp"),
            P("tp", "clip"),
            P("tp", "clip"),
            P("clip", "tp"),
            P("clip", "tp"),
            P("tp", "clip"),
            P("tp", "clip"),
            P(None, "clip"),
            P(None, "clip"),
        ),
        out_specs=(
            P("clip", None, None),
            P("clip", None, None),
            P(None, "clip"),
            P(None, None, "tp"),
            P("tp", None),
            P(None, "tp"),
            P("tp", None),
            P(),
            P("clip", None, "tp"),
            P("tp", "clip"),
            P("clip", "tp"),
            P("tp", "clip"),
            P(None, "clip"),
            P("clip", None, "tp"),
            P("tp", "clip"),
            P("clip", "tp"),
            P("tp", "clip"),
            P(None, "clip"),
            P(None, None, "tp"),
            P("tp", None),
            P(None, "tp"),
            P("tp", None),
        ),
        check_vma=False,
    )
```

```python
import functools

import jax
import jax.numpy as jnp
from jax import lax
from jax.experimental import pallas as pl
from jax.experimental.pallas import tpu as pltpu
from jax.sharding import PartitionSpec as P

D = 768
HD = 64
FF = 3072
BLOCK = 704
STEP = 3
EPSILON = 1e-06
SCALE = HD ** (-0.5)
GROUP = 8
SOURCES = GROUP // 2
F32 = jnp.float32
BF16 = jnp.bfloat16
VMEM_LIMIT = 18 * 2**20
MLP_LIMIT = 20 * 2**20
COST_PART = 3


def dot(left, right, left_dim, right_dim):
    return lax.dot_general(
        left, right, (((left_dim,), (right_dim,)), ((), ())), preferred_element_type=F32
    )


def positions(keep_freq, keep_time):
    bins, frames = keep_freq.shape[1], keep_time.shape[1]
    count = bins * frames
    patch = lax.broadcasted_iota(jnp.int32, (1, count), 1)
    patch_bin = jnp.zeros((1, count), jnp.int32)
    for index in range(1, bins):
        patch_bin += (patch >= index * frames).astype(jnp.int32)
    patch_frame = patch - patch_bin * frames

    def spread(index, size):
        return jnp.where(
            lax.broadcasted_iota(jnp.int32, (size, count), 0) == index, 1.0, 0.0
        ).astype(BF16)

    def before(size):
        row = lax.broadcasted_iota(jnp.int32, (size, size), 0)
        column = lax.broadcasted_iota(jnp.int32, (size, size), 1)
        return jnp.where(row < column, 1.0, 0.0).astype(BF16)

    freq, time = keep_freq.astype(F32).astype(BF16), keep_time.astype(F32).astype(BF16)
    rank_freq = dot(freq, before(bins), 1, 0).astype(BF16)
    rank_time = dot(time, before(frames), 1, 0).astype(BF16)
    by_bin, by_frame = spread(patch_bin, bins), spread(patch_frame, frames)
    time_count = jnp.sum(keep_time.astype(F32), axis=1, keepdims=True)
    placed = dot(rank_freq, by_bin, 1, 0) * time_count + dot(rank_time, by_frame, 1, 0)
    present = dot(freq, by_bin, 1, 0) * dot(time, by_frame, 1, 0)
    return jnp.where(present > 0.5, placed, -1.0).astype(jnp.int32)


def norm_parts(values):
    centre = values - jnp.mean(values, axis=-1, keepdims=True)
    spread = jnp.mean(centre * centre, axis=-1, keepdims=True)
    inverse = lax.rsqrt(spread + EPSILON)
    return centre * inverse, inverse


def norm_back(values, gain, grad):
    unit, inverse = norm_parts(values)
    grad_unit = grad * gain
    mean_grad = jnp.mean(grad_unit, axis=-1, keepdims=True)
    mean_both = jnp.mean(grad_unit * unit, axis=-1, keepdims=True)
    back = inverse * (grad_unit - mean_grad - unit * mean_both)
    gain_grad = jnp.sum(grad * unit, axis=0, keepdims=True)
    shift_grad = jnp.sum(grad, axis=0, keepdims=True)
    return back, gain_grad, shift_grad


def live_column(kept, length):
    return lax.broadcasted_iota(jnp.int32, (length, 1), 0) < kept


def tree_sum(parts, odd):
    if len(parts) != 4:
        total = parts[0]
        for part in parts[1:]:
            total = total + part
        return total
    own, after, across, before = parts
    near = jnp.where(odd, before, after)
    far = jnp.where(odd, after, before)
    return (own + near) + (across + far)


def plain_call(body, grid, in_specs, out_specs, out_shape, scratch=(), aliases=None, cost=None, limit=None, far=(), far_outs=()):
    at = 2 + len(in_specs)
    out_shape = [
        pltpu.HBM(array.shape, array.dtype) if index in far_outs else array
        for index, array in enumerate(out_shape)
    ]

    def with_token(*refs):
        refs[at][...] = jnp.zeros_like(refs[at])
        body(*refs[:at], *refs[at + 1 :])

    run = pl.pallas_call(
        with_token,
        grid_spec=pltpu.PrefetchScalarGridSpec(
            num_scalar_prefetch=2,
            grid=grid,
            in_specs=in_specs,
            out_specs=[whole_block(8, 128), *out_specs],
            scratch_shapes=list(scratch),
        ),
        out_shape=[jax.ShapeDtypeStruct((8, 128), F32), *out_shape],
        input_output_aliases={key: value + 1 for key, value in (aliases or {}).items()},
        compiler_params=pltpu.CompilerParams(
            dimension_semantics=("arbitrary",) * len(grid), vmem_limit_bytes=limit or VMEM_LIMIT
        ),
        cost_estimate=pl.CostEstimate(
            flops=cost[0] * COST_PART, bytes_accessed=cost[1] * COST_PART, transcendentals=0
        ),
    )

    def placed_run(*operands):
        return run(
            *[
                pltpu.with_memory_space_constraint(array, pltpu.HBM) if index - 2 in far else array
                for index, array in enumerate(operands)
            ]
        )

    return placed_run


def clip_block(*dims):
    return pl.BlockSpec((1, *dims), lambda c, *_: (c,) + (0,) * len(dims))


def whole_block(*dims):
    return pl.BlockSpec(dims, lambda *_: (0,) * len(dims))


ANY = pl.BlockSpec(memory_space=pl.ANY)


def front_kernel(kept, order, freq, time, patches, cot, norms, inputs, first, grad, placed):
    clip = pl.program_id(0)
    placed[0] = positions(freq[0], time[0])
    length, patch_count = first.shape[1], placed.shape[2]
    slots = lax.broadcasted_iota(jnp.int32, (length, patch_count), 0)
    select = jnp.where(placed[0] == slots, 1.0, 0.0).astype(BF16)
    picked = dot(select, patches[0], 1, 0)
    inputs[0] = picked
    unit, _ = norm_parts(picked)
    first[0] = (unit * norms[0:1] + norms[1:2]).astype(BF16)
    live = live_column(kept[clip], length)
    grad[0] = jnp.where(live, cot[0].astype(F32), 0.0).astype(BF16)


def pieces_kernel(kept, order, *refs):
    *sources, early, late, up, down, sems = refs
    copies = []
    for target, pair in ((early, sources[:2]), (late, sources[2:]), (up, sources[2:3]), (down, sources[3:])):
        start = 0
        for source in pair:
            rows = source.shape[0] // GROUP
            place = pl.multiple_of(order[2 * GROUP] * rows, 8)
            copies.append(
                pltpu.make_async_copy(
                    source.at[pl.ds(place, rows)],
                    target.at[pl.ds(start, rows)],
                    sems.at[len(copies)],
                )
            )
            start += rows
    for copy in copies:
        copy.start()
    for copy in copies:
        copy.wait()


def piece_copies(order, sources, start, rows, target, sems):
    copies = []
    for slot in range(GROUP):
        source = sources[slot // 2].at[slot % 2, pl.ds(start, rows)]
        place = pl.multiple_of(order[slot] * rows, 8)
        copies.append(
            pltpu.make_async_copy(source, target.at[pl.ds(place, rows)], sems.at[slot])
        )
    return copies


def augment(rows, extra_row, length):
    index = lax.broadcasted_iota(jnp.int32, (16, length), 0)
    extra = jnp.where(index == 0, extra_row, 0.0).astype(BF16)
    return jnp.concatenate([rows, extra], axis=0)


def key_bias(kept, length):
    slot = lax.broadcasted_iota(jnp.int32, (1, length), 1)
    return jnp.where(slot < kept, 0.0, -1000000000.0)


def attend_kernel(mode, fixed, heads, kept, order, first, *refs):
    clip = pl.program_id(0) if fixed is None else fixed
    if mode == "own":
        source, out_source, packed, mixed, total, low, out_low = refs
        low[...] = source[...].astype(BF16)
        out_low[...] = out_source[...].astype(BF16)
    elif mode == "gathered":
        sources, (packed, mixed, total, low, out_low) = refs[:SOURCES], refs[SOURCES:-3]
        staged, out_staged, sems = refs[-3:]

        @pl.when(clip == 0)
        def _():
            rows, out_rows = low.shape[0] // GROUP, out_low.shape[0] // GROUP
            copies = piece_copies(order, sources, 0, rows, staged, sems.at[0])
            copies += piece_copies(order, sources, rows, out_rows, out_staged, sems.at[1])
            for copy in copies:
                copy.start()
            for copy in copies:
                copy.wait()
            low[...] = staged[...].astype(BF16)
            out_low[...] = out_staged[...].astype(BF16)
    else:
        low, _, _, _, packed, mixed, total = refs

    length = first.shape[1]
    width = heads * HD
    rows = dot(low[...], first[0], 1, 1).astype(BF16)
    packed[0] = rows
    bias = key_bias(kept[clip], length)
    ones = jnp.ones((1, length), F32)
    for head in range(heads):
        at = head * HD
        query = augment((rows[at : at + HD] * SCALE).astype(BF16), ones, length)
        key = augment(rows[width + at : width + at + HD], bias, length)
        value = rows[2 * width + at : 2 * width + at + HD]
        scores = dot(key, query, 0, 0)
        largest = jnp.max(scores, axis=0, keepdims=True)
        exponent = jnp.exp(scores - largest)
        summed = jnp.sum(exponent, axis=0, keepdims=True)
        mix = dot(value, exponent.astype(BF16), 1, 0) / summed
        mixed[0, at : at + HD] = mix.astype(BF16)
        total[0, head : head + 1] = largest + jnp.log(summed)

HALF_ROOT = 0.7071067811865476
DENSITY = 0.3989422804014327


def load_mlp(order, sources, up_low, down_low, staged, sems):
    rows = up_low.shape[0] // GROUP
    lows = (up_low, down_low)
    copies = [
        piece_copies(order, sources, index * rows, rows, staged.at[index], sems.at[index])
        for index in range(2)
    ]
    for copy in copies[0] + copies[1]:
        copy.start()
    for index in range(2):
        for slot, copy in enumerate(copies[index]):
            copy.wait()
            place = pl.ds(pl.multiple_of(order[slot] * rows, 16), rows)
            lows[index][place] = staged[index, place].astype(BF16)


def mlp_rows(rows, upstream, up_low, down_low, chunk, grads=None):
    branch_sum = back_sum = None
    for start in range(0, up_low.shape[1], chunk):
        up = up_low[:, start : start + chunk]
        down = down_low[start : start + chunk]
        hidden = dot(rows, up, 1, 0)
        grad_active = dot(upstream, down, 1, 1)
        cumulative = 0.5 * (lax.erf(hidden * HALF_ROOT) + 1.0)
        active = (hidden * cumulative).astype(BF16)
        slope = cumulative + hidden * (DENSITY * jnp.exp(-0.5 * hidden * hidden))
        grad_hidden = (slope * grad_active).astype(BF16)
        branch_part = dot(active, down, 1, 0)
        back_part = dot(grad_hidden, up, 1, 1)
        branch_sum = branch_part if branch_sum is None else branch_sum + branch_part
        back_sum = back_part if back_sum is None else back_sum + back_part
        if grads is not None:
            width = up_low.shape[1]
            grads[:, start : start + chunk] += dot(rows, grad_hidden, 0, 0)
            grads[:, width + start : width + start + chunk] += dot(upstream, active, 0, 0)
    return branch_sum, back_sum


def part_copies(order, source, keep, send, sems):
    rows = keep.shape[1]
    copies = []
    for slot in range(GROUP):
        target = (keep if slot < GROUP // 2 else send).at[slot % (GROUP // 2)]
        place = pl.multiple_of(order[GROUP + slot] * rows, 8)
        copies.append(pltpu.make_async_copy(source.at[pl.ds(place, rows)], target, sems.at[slot]))
    return copies


def mlp_own_kernel(chunk, shards, kept, order, inputs, grad, norms, up_source, down_source, *refs):
    mixes, out_lows, refs = refs[:shards], refs[shards : 2 * shards], refs[2 * shards :]
    middle, second, branch, back, keep, send, up_low, down_low, staged, grads, sems = refs
    clip = pl.program_id(0)
    loads = [
        pltpu.make_async_copy(source, staged.at[index], sems.at[index])
        for index, source in enumerate((up_source, down_source))
    ]

    @pl.when(clip == 0)
    def _():
        for copy in loads:
            copy.start()
        grads[...] = jnp.zeros_like(grads)

    values = inputs[0]
    for mixed, out_low in zip(mixes, out_lows):
        values = values + dot(mixed[0], out_low[...], 0, 0)
    middle[0] = values
    unit, _ = norm_parts(values)
    second[0] = (unit * norms[2:3] + norms[3:4]).astype(BF16)

    @pl.when(clip == 0)
    def _():
        for copy, low, index in zip(loads, (up_low, down_low), range(2)):
            copy.wait()
            low[...] = staged[index].astype(BF16)

    branch_part, back_part = mlp_rows(second[0], grad[0], up_low, down_low, chunk, grads)
    branch[0] = values + branch_part
    back[0] = back_part

    @pl.when(clip == pl.num_programs(0) - 1)
    def _():
        copies = part_copies(order, grads, keep, send, sems)
        for copy in copies:
            copy.start()
        for copy in copies:
            copy.wait()


def mlp_kernel(chunk, kept, order, second, grad, branch_in, back_in, *refs):
    sources = refs[:SOURCES]
    branch, back, up_low, down_low, staged, sems = refs[SOURCES:]
    clip = pl.program_id(0)

    @pl.when(clip == 0)
    def _():
        load_mlp(order, sources, up_low, down_low, staged, sems)

    branch_part, back_part = mlp_rows(second[0], grad[0], up_low, down_low, chunk)
    branch[0] = branch_in[0] + branch_part
    back[0] = back_in[0] + back_part


def mlp_last_kernel(chunk, kept, order, second, grad, branch_in, back_in, *refs):
    sources = refs[:SOURCES]
    middle, norms, result, grad_middle, low, norm_grad = refs[SOURCES : SOURCES + 6]
    up_low, down_low, staged, sems = refs[SOURCES + 6 :]
    clip = pl.program_id(0)

    @pl.when(clip == 0)
    def _():
        load_mlp(order, sources, up_low, down_low, staged, sems)
        norm_grad[...] = jnp.zeros_like(norm_grad)

    branch_part, back_part = mlp_rows(second[0], grad[0], up_low, down_low, chunk)
    live = live_column(kept[clip], middle.shape[1])
    result[0] = jnp.where(live, branch_in[0] + branch_part, 0.0).astype(BF16)
    back, gain_grad, shift_grad = norm_back(middle[0], norms[2:3], back_in[0] + back_part)
    both = grad[0].astype(F32) + back
    grad_middle[0] = both
    low[0] = both.astype(BF16)
    norm_grad[0:1] += gain_grad
    norm_grad[1:2] += shift_grad


def attend_back_kernel(own, heads, kept, order, packed, mixed, total, grad, out_low, *refs):
    clip = pl.program_id(0)
    if own:
        first, grad_packed, keep, send, grads, sems = refs
    else:
        (grad_packed,) = refs
    length = grad.shape[1]
    width = heads * HD
    grad_mixed = dot(out_low[...], grad[0], 1, 1).astype(BF16)
    bias = key_bias(kept[clip], length)
    ones = jnp.ones((1, length), F32)
    for head in range(heads):
        at = head * HD
        query_low = (packed[0, at : at + HD] * SCALE).astype(BF16)
        key_low = packed[0, width + at : width + at + HD]
        value = packed[0, 2 * width + at : 2 * width + at + HD]
        query = augment(query_low, ones, length)
        key = augment(key_low, bias, length)
        upstream = grad_mixed[at : at + HD]
        offset = jnp.sum(
            upstream.astype(F32) * mixed[0, at : at + HD].astype(F32), axis=0, keepdims=True
        )
        probs = jnp.exp(dot(key, query, 0, 0) - total[0, head : head + 1])
        grad_probs = dot(value, upstream, 0, 0)
        scores_low = (probs * (grad_probs - offset)).astype(BF16)
        probs_low = probs.astype(BF16)
        grad_packed[0, at : at + HD] = (dot(key_low, scores_low, 1, 0) * SCALE).astype(BF16)
        grad_packed[0, width + at : width + at + HD] = dot(query_low, scores_low, 1, 1).astype(BF16)
        grad_packed[0, 2 * width + at : 2 * width + at + HD] = dot(
            upstream, probs_low, 1, 1
        ).astype(BF16)
    if own:

        @pl.when(clip == 0)
        def _():
            grads[...] = jnp.zeros_like(grads)

        grads[:, : 3 * width] += dot(first[0], grad_packed[0], 0, 1)
        grads[:, 3 * width :] += dot(grad[0], mixed[0], 0, 1)

        @pl.when(clip == pl.num_programs(0) - 1)
        def _():
            copies = part_copies(order, grads, keep, send, sems)
            for copy in copies:
                copy.start()
            for copy in copies:
                copy.wait()


def final_kernel(shards, kept, order, inputs, grad_middle, norms, *refs):
    packs, lows, (low, norm_grad) = refs[:shards], refs[shards : 2 * shards], refs[2 * shards :]
    clip = pl.program_id(0)
    grad_first = None
    for packed, weight in zip(packs, lows):
        part = dot(packed[0], weight[...], 0, 0)
        grad_first = part if grad_first is None else grad_first + part
    back, gain_grad, shift_grad = norm_back(inputs[0], norms[0:1], grad_first)
    low[0] = (grad_middle[0] + back).astype(BF16)

    @pl.when(clip == 0)
    def _():
        norm_grad[...] = jnp.zeros_like(norm_grad)

    norm_grad[0:1] += gain_grad
    norm_grad[1:2] += shift_grad


def unselect_kernel(kept, order, placed, low, patch_grad):
    clip_count, length, width = low.shape
    patch_count = placed.shape[2]
    lanes = 128
    tiles = width // lanes
    slots = lax.broadcasted_iota(jnp.int32, (length, patch_count), 0)
    for clip in range(clip_count):
        select = jnp.where(placed[clip] == slots, 1.0, 0.0).astype(BF16)
        back = dot(select, low[clip], 0, 0)
        for tile in range(tiles):
            rows = pl.ds(tile * clip_count + clip, patch_count, stride=tiles * clip_count)
            patch_grad[rows, :] = back[:, tile * lanes : (tile + 1) * lanes]


def adam_direction(gradient, first_mom, second_mom):
    first_new = 0.5 * first_mom + 0.5 * gradient
    second_new = 0.5 * second_mom + 0.5 * gradient * gradient
    fix = 1.0 - 0.5**STEP
    direction = first_new / fix / (jnp.sqrt(second_new / fix) + 1e-08)
    return direction, first_new, second_new


def moments_kernel(layout, riders, kept, order, gradient, *refs):
    count = len(layout)
    riding, refs = refs[:riders], refs[riders:]
    firsts, seconds = refs[:count], refs[count : 2 * count]
    direction, first_outs, second_outs = (
        refs[2 * count],
        refs[2 * count + 1 : 3 * count + 1],
        refs[3 * count + 1 :],
    )
    start = 0
    for index, (wide, form) in enumerate(layout):
        parts = 3 if form == "stack" else 1
        for part in range(parts):
            columns = slice(start, start + wide)
            grad = gradient[:, columns]
            if form == "turned":
                first, second = firsts[index][...].T, seconds[index][...].T
            elif form == "stack":
                first, second = firsts[index][part], seconds[index][part]
            else:
                first, second = firsts[index][...], seconds[index][...]
            step, first, second = adam_direction(grad, first, second)
            direction[: gradient.shape[0], columns] = step
            if form == "turned":
                first_outs[index][...], second_outs[index][...] = first.T, second.T
            elif form == "stack":
                first_outs[index][part], second_outs[index][part] = first, second
            else:
                first_outs[index][...], second_outs[index][...] = first, second
            start += wide
    if riders:
        row = gradient.shape[0]
        direction[row:] = jnp.zeros_like(direction[row:])
        for array in riding:
            direction[row : row + array.shape[0], : array.shape[1]] = array[...]
            row += array.shape[0]


def assemble_kernel(layout, riders, kept, order, *refs):
    count = len(layout)
    sources, refs = refs[:SOURCES], refs[SOURCES:]
    weights, outs = refs[:count], refs[count : 3 * count]
    if riders:
        ridden, staged, sems, riding, more_sems = refs[3 * count :]
    else:
        staged, sems = refs[3 * count :]
    rows = staged.shape[0] // GROUP
    copies = piece_copies(order, sources, 0, rows, staged, sems)
    if riders:
        for slot in range(GROUP):
            copies.append(
                pltpu.make_async_copy(
                    sources[slot // 2].at[slot % 2, pl.ds(rows, 8), pl.ds(0, 128)],
                    riding.at[order[slot]],
                    more_sems.at[slot],
                )
            )
    for copy in copies:
        copy.start()
    for copy in copies:
        copy.wait()
    start = 0
    for index, (wide, turned, rate) in enumerate(layout):
        step = staged[:, start : start + wide]
        if turned:
            step = step.T
        weight = weights[index][...]
        values = weight - rate * (step + 0.01 * weight)
        outs[2 * index][...] = values
        outs[2 * index + 1][...] = values.astype(BF16)
        start += wide
    if riders:
        for member in range(GROUP):
            ridden[:, member * rows : (member + 1) * rows] = riding[member][:, :rows]


def swap_bits(code):
    return code & 1 | (code >> 2 & 1) << 1 | (code >> 1 & 1) << 2


def members(clips):
    return clips // GROUP


def exchange(array, code, clips, shards):
    step = members(clips)
    pairs = []
    for clip in range(clips):
        member, rest = divmod(clip, step)
        other = member ^ (swap_bits(code) if member & 1 else code)
        for shard in range(shards):
            pairs.append((clip * shards + shard, (other * step + rest) * shards + shard))
    return lax.ppermute(array, ("clip", "tp"), pairs)


def swap_rest(array, mask, clips, shards):
    pairs = [
        (clip * shards + shard, (clip ^ mask) * shards + shard)
        for clip in range(clips)
        for shard in range(shards)
    ]
    return lax.ppermute(array, ("clip", "tp"), pairs)


def shift(array, step, clips, shards):
    pairs = [
        (clip * shards + (shard + step) % shards, clip * shards + shard)
        for clip in range(clips)
        for shard in range(shards)
    ]
    return lax.ppermute(array, ("clip", "tp"), pairs)


def tie(array, *others):
    return lax.optimization_barrier((array, *others))[0]


def piece_order(member):
    odd = member & 1

    def place(base, parity, code):
        return base ^ jnp.where(parity == 1, swap_bits(code), code)

    near = [place(member, odd, code) for code in (0, 2, 4, 6)]
    far = [place(member ^ 1, 1 - odd, code) for code in (0, 2, 4, 6)]
    return near + far


def grad_order(member):
    odd = member & 1

    def place(code):
        return member ^ jnp.where(odd == 1, swap_bits(code), code)

    return [place(code) for code in (0, 2, 4, 6)] + [place(code) for code in (1, 5, 3, 7)]


def sum_rest(part, clips, shards, clip_index):
    step = members(clips)
    rest = clip_index % step
    half = step // 2
    while half:
        low, high = jnp.split(part, 2)
        upper = (rest & half) > 0
        got = swap_rest(jnp.where(upper, low, high), half, clips, shards)
        part = jnp.where(upper, high, low) + got
        half //= 2
    return part


def gather_rest(part, clips, shards, clip_index):
    step = members(clips)
    rest = clip_index % step
    half = 1
    while half < step:
        got = swap_rest(part, half, clips, shards)
        upper = (rest & half) > 0
        part = jnp.concatenate([jnp.where(upper, got, part), jnp.where(upper, part, got)])
        half *= 2
    return part


def sum_all(array, clips, shards):
    mask = 1
    while mask < clips:
        array = array + swap_rest(array, mask, clips, shards)
        mask *= 2
    return array


def own_part(array, axis_dim, clip_index, parts):
    part_width = array.shape[axis_dim] // parts
    return lax.dynamic_slice_in_dim(array, clip_index * part_width, part_width, axis_dim)


def on_device(
    patches,
    keep_freq,
    keep_time,
    cotangent,
    w_qkv,
    w_out,
    w_up,
    w_down,
    norms,
    m_qkv,
    v_qkv,
    m_out,
    v_out,
    m_up,
    v_up,
    m_down,
    v_down,
    m_norms,
    v_norms,
):
    clip_count, length, width = cotangent.shape
    patch_count = patches.shape[1]
    clips, shards = lax.axis_size("clip"), lax.axis_size("tp")
    clip_index, shard_index = lax.axis_index("clip"), lax.axis_index("tp")
    local = w_qkv.shape[2]
    heads = local // HD
    hidden = w_up.shape[1]
    packed_width = 3 * local
    member = clip_index % GROUP

    group = members(clips)
    member = clip_index // group
    waiting, started, slow, tokens = [], [], [], []

    def call(*args, **kwargs):
        run = plain_call(*args, **kwargs)

        def keep_token(*operands):
            results = run(*operands)
            tokens.append(results[0])
            return results

        return keep_token


    def ex(array, code):
        started.append(exchange(array, code, clips, shards))
        return started[-1]

    def move(array, step, two_kernels=False):
        kind = slow if two_kernels else started
        kind.append(shift(array, step, clips, shards))
        return kind[-1]

    def swap(array, mask):
        started.append(swap_rest(array, mask, clips, shards))
        return started[-1]

    def gate(array):
        array = tie(array, *waiting, *tokens[-1:])
        waiting[:] = started
        started[:] = slow
        slow.clear()
        return array

    shape = jax.ShapeDtypeStruct

    qkv_rows = jnp.transpose(w_qkv, (1, 2, 0)).reshape(packed_width, width)

    order = jnp.stack([*piece_order(member), *grad_order(member), member]).astype(jnp.int32)
    kept = (jnp.sum(keep_freq, axis=-1) * jnp.sum(keep_time, axis=-1)).astype(jnp.int32)
    _, early_piece, late_piece, up_piece, down_piece = call(
        pieces_kernel,
        (1,),
        [ANY] * 4,
        [
            whole_block((packed_width + local) // GROUP, width),
            whole_block((width + hidden) // GROUP, width),
            whole_block(width // GROUP, hidden),
            whole_block(hidden // GROUP, width),
        ],
        [
            shape(((packed_width + local) // GROUP, width), F32),
            shape(((width + hidden) // GROUP, width), F32),
            shape((width // GROUP, hidden), F32),
            shape((hidden // GROUP, width), F32),
        ],
        scratch=(pltpu.SemaphoreType.DMA((6,)),),
        cost=(1_000_000, 4_000_000),
        limit=56 * 2**20,
    )(kept, order, qkv_rows, w_out, w_up, w_down)
    steps = (1, 3, 2) if shards == 4 else tuple(range(1, shards))
    early = {step: [move(early_piece, step)] for step in steps[:2]}
    late = {}

    def hop(pieces, done):
        if len(pieces) == 1:
            return [*pieces, ex(tie(pieces[0], done), 2)]
        if pieces[0].ndim == 2:
            pair = jnp.stack([tie(piece, done) for piece in pieces])
            return [pair, ex(pair, 4)]
        return [*pieces, *[ex(tie(piece, done), 1) for piece in pieces]]

    row = functools.partial(clip_block, length)
    rows_f32 = shape((clip_count, length, width), F32)
    rows_low = shape((clip_count, length, width), BF16)
    grid = (clip_count,)

    def fixed_block(clip, *dims):
        return pl.BlockSpec((1, *dims), lambda *_: (clip,) + (0,) * len(dims))

    s1, s2, s3 = steps
    freq = gate(keep_freq[:, None, :])
    front_done, inputs, first, grad, placed = call(
        front_kernel,
        grid,
        [
            clip_block(1, keep_freq.shape[1]),
            clip_block(1, keep_time.shape[1]),
            clip_block(patch_count, width),
            row(width),
            whole_block(4, width),
        ],
        [row(width)] * 3 + [clip_block(1, patch_count)],
        [rows_f32, rows_low, rows_low, shape((clip_count, 1, patch_count), jnp.int32)],
        cost=(2 * clip_count * length * patch_count * width, 20_000_000),
        limit=24 * 2**20,
        far_outs=(0, 2),
    )(kept, order, freq, keep_time[:, None, :], patches, cotangent, norms)

    packs, mixes, totals, lows, out_lows = [], [], [], [], []

    attend_outs = [
        shape((clip_count, packed_width, length), BF16),
        shape((clip_count, local, length), BF16),
        shape((clip_count, heads, length), F32),
    ]
    low_outs = [shape((packed_width, width), BF16), shape((local, width), BF16)]
    low_specs = [whole_block(packed_width, width), whole_block(local, width)]
    attend_cost = (18_000_000_000, 25_000_000)

    def attend_own():
        def specs(clip):
            return [
                fixed_block(clip, packed_width, length),
                fixed_block(clip, local, length),
                fixed_block(clip, heads, length),
            ]

        results = call(
            functools.partial(attend_kernel, "own", 0, heads),
            (1,),
            [fixed_block(0, length, width)] + low_specs,
            specs(0) + low_specs,
            attend_outs + low_outs,
            cost=attend_cost,
            far=(1, 2),
            far_outs=(0, 1, 2),
        )(kept, order, gate(first), qkv_rows, w_out)
        yield results
        for clip in range(1, clip_count):
            _, *arrays, low, out_low = results
            arrays = call(
                functools.partial(attend_kernel, "rest", clip, heads),
                (1,),
                [fixed_block(clip, length, width), low_specs[0]] + [ANY] * 3,
                specs(clip),
                attend_outs,
                aliases={4 + index: index for index in range(3)},
                cost=attend_cost,
                far=(2, 3, 4),
                far_outs=(0, 1, 2),
            )(kept, order, gate(first), low, *arrays)
            results = [*arrays, low, out_low]
            yield results

    def attend(pieces):
        return call(
            functools.partial(attend_kernel, "gathered", None, heads),
            grid,
            [row(width)] + [ANY] * SOURCES,
            [
                clip_block(packed_width, length),
                clip_block(local, length),
                clip_block(heads, length),
            ]
            + low_specs,
            attend_outs + low_outs,
            scratch=(
                pltpu.VMEM((packed_width, width), F32),
                pltpu.VMEM((local, width), F32),
                pltpu.SemaphoreType.DMA((2, GROUP)),
            ),
            cost=attend_cost,
            far_outs=(0, 1, 2, 3, 4),
        )(kept, order, gate(first), *pieces)

    def keep(results):
        done, packed, mixed, total, low, out_low = results
        packs.append(packed)
        mixes.append(mixed)
        totals.append(total)
        lows.append(low)
        out_lows.append(out_low)
        return done

    own_rows = width // clips

    early[s1] = hop(early[s1], front_done)
    early[s3] = [move(tie(early_piece, front_done), s3)]
    halves = attend_own()
    results = next(halves)
    early[s1] = hop(early[s1], results[0])
    early[s2] = hop(early[s2], results[0])
    early[s3] = hop(early[s3], results[0])
    late[s1] = [move(tie(late_piece, results[0]), s1, True)]
    for results in halves:
        pass
    done = keep(results)
    early[s1] = hop(early[s1], done)
    early[s2] = hop(early[s2], done)
    late[s2] = [move(tie(late_piece, done), s2, True)]
    done = keep(attend(early[s1]))
    early[s2] = hop(early[s2], done)
    early[s3] = hop(early[s3], done)
    late[s1] = hop(late[s1], done)
    late_up = move(tie(up_piece, done), s3, True)
    done = keep(attend(early[s2]))
    early[s3] = hop(early[s3], done)
    late[s1] = hop(late[s1], done)
    late[s2] = hop(late[s2], done)
    late_down = move(tie(down_piece, done), s3, True)
    done = keep(attend(early[s3]))
    late[s1] = hop(late[s1], done)
    late[s2] = hop(late[s2], done)

    mlp_scratch = (pltpu.VMEM((width, hidden), BF16), pltpu.VMEM((hidden, width), BF16))
    stage_scratch = (
        pltpu.VMEM((2, width, hidden), F32),
        pltpu.SemaphoreType.DMA((2, GROUP)),
    )
    chunk = 384
    half_parts = shape((GROUP // 2, width // GROUP, 2 * hidden), F32)
    done, middle, second, branch, back, mlp_keep, mlp_send = call(
        functools.partial(mlp_own_kernel, chunk, shards),
        grid,
        [row(width), row(width), whole_block(4, width)]
        + [ANY, ANY]
        + [clip_block(local, length)] * shards
        + [whole_block(local, width)] * shards,
        [row(width)] * 4 + [ANY, ANY],
        [rows_f32, rows_low, rows_f32, rows_f32, half_parts, half_parts],
        scratch=mlp_scratch
        + (
            pltpu.VMEM((2, width, hidden), F32),
            pltpu.VMEM((width, 2 * hidden), F32),
            pltpu.SemaphoreType.DMA((GROUP,)),
        ),
        cost=(12_000_000_000, 30_000_000),
        limit=42 * 2**20,
        far=(0, *range(3, 5 + 2 * shards)),
        far_outs=(0, 4, 5),
    )(kept, order, gate(inputs), grad, norms, w_up, w_down, *mixes, *out_lows)

    late[s2] = hop(late[s2], done)
    late_parts = [late_up, late_down, *[ex(tie(part, done), 2) for part in (late_up, late_down)]]
    mlp_got = ex(mlp_send, 1)

    def mlp(branch, back, pieces):
        return call(
            functools.partial(mlp_kernel, chunk),
            grid,
            [row(width)] * 4 + [ANY] * SOURCES,
            [row(width), row(width)],
            [rows_f32, rows_f32],
            scratch=mlp_scratch + stage_scratch,
            aliases={4: 0, 5: 1},
            far=(4, 5, 6, 7),
            limit=MLP_LIMIT,
            cost=(9_000_000_000, 25_000_000),
        )(kept, order, gate(second), grad, branch, back, *pieces)

    done, branch, back = mlp(branch, back, late[s1])
    late_parts = [tie(part, done) for part in late_parts]
    pair = jnp.concatenate(late_parts).reshape(2, late_piece.shape[0], width)
    late[s3] = [pair, ex(pair, 4)]
    mlp_sum = mlp_keep + mlp_got
    slow.append(exchange(tie(mlp_sum[2:], done), 4, clips, shards))
    mlp_got = slow[-1]
    done, branch, back = mlp(branch, back, late[s2])
    late[s3] = hop(late[s3], done)
    done, block_out, grad_middle, middle_low, norm_grad2 = call(
        functools.partial(mlp_last_kernel, chunk),
        grid,
        [row(width)] * 4 + [ANY] * SOURCES + [row(width), whole_block(4, width)],
        [row(width)] * 3 + [whole_block(2, width)],
        [rows_low, rows_f32, rows_low, shape((2, width), F32)],
        scratch=mlp_scratch + stage_scratch,
        far=(4, 5, 6, 7, 8),
        limit=MLP_LIMIT + 8 * 2**20,
        cost=(9_000_000_000, 25_000_000),
    )(kept, order, gate(second), grad, branch, back, *late[s3], middle, norms)
    mlp_sum = mlp_sum[:2] + tie(mlp_got, done)
    mlp_got = ex(mlp_sum[1], 2)

    half_parts = shape((GROUP // 2, width // GROUP, packed_width + local), F32)

    def attend_back(index):
        own = index == 0
        return call(
            functools.partial(attend_back_kernel, own, heads),
            grid,
            [
                clip_block(packed_width, length),
                clip_block(local, length),
                clip_block(heads, length),
                row(width),
                whole_block(local, width),
            ]
            + ([row(width)] if own else []),
            [clip_block(packed_width, length)] + ([ANY, ANY] if own else []),
            [shape((clip_count, packed_width, length), BF16)]
            + ([half_parts, half_parts] if own else []),
            scratch=(
                pltpu.VMEM((width, packed_width + local), F32),
                pltpu.SemaphoreType.DMA((GROUP,)),
            )
            if own
            else (),
            cost=(14_000_000_000, 14_000_000),
        )(
            kept,
            order,
            packs[index],
            mixes[index],
            totals[index],
            gate(middle_low),
            out_lows[index],
            *((first,) if own else ()),
        )

    def moments(gradient, layout, firsts, seconds, riders=()):
        count = len(layout)
        rows, wide = gradient.shape
        direction = shape((rows + sum(array.shape[0] for array in riders), wide), F32)
        specs = [whole_block(*array.shape) for array in (*firsts, *seconds)]
        results = call(
            functools.partial(moments_kernel, layout, len(riders)),
            (1,),
            [whole_block(*array.shape) for array in (gradient, *riders)] + specs,
            [whole_block(*direction.shape)] + specs,
            [direction, *[shape(array.shape, F32) for array in (*firsts, *seconds)]],
            cost=(1_000_000, 5_000_000),
        )(kept, order, gradient, *riders, *firsts, *seconds)
        return results[1], results[2 : count + 2], results[count + 2 :]

    def assemble(pieces, weights, layout, done, riders=False):
        total = sum(entry[0] for entry in layout)
        return call(
            functools.partial(assemble_kernel, layout, riders),
            (1,),
            [ANY] * SOURCES + [whole_block(*weight.shape) for weight in weights],
            [whole_block(*weight.shape) for weight in weights for _ in range(2)]
            + ([whole_block(8, width)] if riders else []),
            [shape(weight.shape, kind) for weight in weights for kind in (F32, BF16)]
            + ([shape((8, width), F32)] if riders else []),
            scratch=(pltpu.VMEM((width, total), F32), pltpu.SemaphoreType.DMA((GROUP,)))
            + (
                (pltpu.VMEM((GROUP, 8, 128), F32), pltpu.SemaphoreType.DMA((GROUP,)))
                if riders
                else ()
            ),
            cost=(1_000_000, 15_000_000),
        )(kept, order, gate(tie(pieces[0], done)), *pieces[1:], *weights)

    riders = group == 1
    rate_model = D ** (-0.5)
    grad_packs = [None] * shards
    done, grad_packs[0], att_keep, att_send = attend_back(0)
    att_got = ex(att_send, 1)
    mlp_sum = sum_rest(mlp_sum[0] + tie(mlp_got, done), clips, shards, clip_index)
    mlp_dir, (mom1_up, mom1_down), (mom2_up, mom2_down) = moments(
        mlp_sum,
        ((hidden, "plain"), (hidden, "plain")),
        (m_up, m_down.T),
        (v_up, v_down.T),
        (m_norms, v_norms) if riders else (),
    )
    mlp_part = gather_rest(mlp_dir, clips, shards, clip_index)
    mlp_other = ex(mlp_part, 2)
    done, grad_packs[1] = attend_back(1)
    att_sum = att_keep + att_got
    att_got = ex(tie(att_sum[2:], done), 4)
    mlp_pair = jnp.stack([tie(mlp_part, done), tie(mlp_other, done)])
    slow.append(exchange(mlp_pair, 4, clips, shards))
    mlp_other = slow[-1]
    done, grad_packs[2] = attend_back(2)
    att_sum = att_sum[:2] + att_got
    att_got = ex(tie(att_sum[1], done), 2)
    done, grad_packs[3] = attend_back(3)
    att_sum = sum_rest(att_sum[0] + tie(att_got, done), clips, shards, clip_index)
    att_dir, (mom1_qkv, mom1_out), (mom2_qkv, mom2_out) = moments(
        att_sum,
        ((local, "stack"), (local, "turned")),
        (jnp.transpose(m_qkv, (1, 0, 2)), m_out),
        (jnp.transpose(v_qkv, (1, 0, 2)), v_out),
    )
    att_part = gather_rest(att_dir, clips, shards, clip_index)
    att_other = ex(att_part, 2)
    done, inputs_low, norm_grad1 = call(
        functools.partial(final_kernel, shards),
        grid,
        [row(width), row(width), whole_block(4, width)]
        + [clip_block(packed_width, length)] * shards
        + [whole_block(packed_width, width)] * shards,
        [row(width), whole_block(2, width)],
        [rows_low, shape((2, width), F32)],
        cost=(10_000_000, 20_000_000),
    )(kept, order, gate(tie(inputs, att_part)), grad_middle, norms, *grad_packs, *lows)

    att_pair = jnp.stack([tie(att_part, done), tie(att_other, done)])
    att_other = ex(tie(att_pair, done), 4)
    norm_sum = jnp.concatenate([norm_grad1, norm_grad2])
    norm_got = swap(norm_sum, 1)
    mlp_pieces = hop([mlp_pair, mlp_other], done)

    flat_rows = patch_count * (width // 128) * clip_count
    done, patch_flat = call(
        unselect_kernel,
        (1,),
        [whole_block(clip_count, 1, patch_count), whole_block(clip_count, length, width)],
        [whole_block(flat_rows, 128)],
        [shape((flat_rows, 128), F32)],
        cost=(5_000_000_000, 20_000_000),
    )(kept, order, placed, gate(inputs_low))
    patch_grad = (
        patch_flat.reshape(patch_count, width // 128, clip_count, 128)
        .transpose(0, 2, 1, 3)
        .reshape(patch_count, clip_count, width)
        .transpose(1, 0, 2)
    )
    att_pieces = hop([att_pair, att_other], done)
    norm_sum = norm_sum + tie(norm_got, done)
    norm_got = swap(norm_sum, 2)
    done, full_up, low_up, full_down, low_down, *norm_moments = assemble(
        mlp_pieces,
        (w_up, w_down),
        ((hidden, False, rate_model), (hidden, True, FF ** (-0.5))),
        norm_sum,
        riders,
    )
    norm_sum = norm_sum + tie(norm_got, done)
    mask = 4
    while mask < clips:
        norm_got = swap(norm_sum, mask)
        if mask == 4:
            done, qkv_full, qkv_low, full_out, low_out = assemble(
                att_pieces,
                (qkv_rows, w_out),
                (
                    (packed_width, True, rate_model),
                    (local, True, max(16 * D // BLOCK, 1) ** (-0.5)),
                ),
                norm_sum,
            )
            norm_got = tie(norm_got, done)
        norm_sum = norm_sum + norm_got
        mask *= 2

    def unrow(array):
        return jnp.transpose(array.reshape(3, local, width), (2, 0, 1))

    def norm_piece(array):
        return own_part(array, 1, clip_index, clips)

    if riders:
        (norm_moments,) = norm_moments
    else:
        norm_moments = jnp.zeros((8, width), F32)
        norm_moments = lax.dynamic_update_slice(
            norm_moments, jnp.concatenate([m_norms, v_norms]), (0, clip_index * own_rows)
        )
        norm_moments = sum_all(norm_moments, clips, shards)
    norm_dir, mom1_norms, mom2_norms = adam_direction(norm_sum, norm_moments[:4], norm_moments[4:])
    norm_sum = tie(norm_sum, *tokens)
    full_norms = norms - 0.3 * (norm_dir + 0.01 * norms)

    return (
        block_out,
        patch_grad,
        norm_piece(norm_sum),
        unrow(qkv_full),
        full_out,
        full_up,
        full_down,
        full_norms,
        jnp.transpose(mom1_qkv, (1, 0, 2)),
        mom1_out,
        mom1_up,
        mom1_down.T,
        norm_piece(mom1_norms),
        jnp.transpose(mom2_qkv, (1, 0, 2)),
        mom2_out,
        mom2_up,
        mom2_down.T,
        norm_piece(mom2_norms),
        unrow(qkv_low),
        low_out,
        low_up,
        low_down,
    )


def solution(mesh):
    return jax.shard_map(
        on_device,
        mesh=mesh,
        in_specs=(
            P("clip", None, None),
            P("clip", None),
            P("clip", None),
            P("clip", None, None),
            P(None, None, "tp"),
            P("tp", None),
            P(None, "tp"),
            P("tp", None),
            P(),
            P("clip", None, "tp"),
            P("clip", None, "tp"),
            P("tp", "clip"),
            P("tp", "clip"),
            P("clip", "tp"),
            P("clip", "tp"),
            P("tp", "clip"),
            P("tp", "clip"),
            P(None, "clip"),
            P(None, "clip"),
        ),
        out_specs=(
            P("clip", None, None),
            P("clip", None, None),
            P(None, "clip"),
            P(None, None, "tp"),
            P("tp", None),
            P(None, "tp"),
            P("tp", None),
            P(),
            P("clip", None, "tp"),
            P("tp", "clip"),
            P("clip", "tp"),
            P("tp", "clip"),
            P(None, "clip"),
            P("clip", None, "tp"),
            P("tp", "clip"),
            P("clip", "tp"),
            P("tp", "clip"),
            P(None, "clip"),
            P(None, None, "tp"),
            P("tp", None),
            P(None, "tp"),
            P("tp", None),
        ),
        check_vma=False,
    )
```
